32 devices in a mesh: slab: 8 (over z, y), ray: 4 (over x, core).
Axes of the slice: x: 2, y: 2, z: 4, core: 2. Of those that a mesh axis runs over, the one named last changes fastest.
Arguments:
- ray_code: bfloat16 [2048, 128], P(('ray', 'slab')), may hold values from -4 to 4
- direction: int32 [2048], P('ray'), may hold values from 0 to 1
- target: float32 [3, 2048], P(None, 'ray'), may hold values from 0 to 1
- brick_code: bfloat16 [8, 1024, 128], P('slab'), may hold values from -4 to 4
- sample_code: bfloat16 [8, 64, 128], P('slab'), may hold values from -4 to 4
- w_hidden: bfloat16 [8, 128, 128], P('slab'), may hold values from -0.5 to 0.5
- b_hidden: float32 [8, 128], P('slab'), may hold values from -3 to 3
- w_out: bfloat16 [8, 4, 128], P('slab'), may hold values from -0.5 to 0.5
- b_out: float32 [8, 4], P('slab'), may hold values from -4 to 4
- brick_ids: int32 [8, 2, 2048], P('slab', None, 'ray'), may hold values from 0 to 1023
- occupancy: int32 [8, 2048], P('slab', 'ray'), may hold values from 0 to 2, as said below
Outputs:
- color: float32 [3, 2048], P(None, ('ray', 'slab'))
- grad_ray: float32 [2048, 128], P(('ray', 'slab'))
- grad_brick: float32 [8, 1024, 128], P('slab', 'ray')
- grad_sample: float32 [8, 64, 128], P('slab')
- grad_w_hidden: float32 [8, 128, 128], P('slab')
- grad_b_hidden: float32 [8, 128], P('slab')
- grad_w_out: float32 [8, 4, 128], P('slab')
- grad_b_out: float32 [8, 4], P('slab')
The draws below stay inside these ranges and needn't reach their ends.
Inputs may be any that keep to these rules, and one draw needn't show every extreme that they name: Slots k >= occupancy[s, r] are padding and carry no density; every slab has a ray segment with 2 occupied slots. `brick_ids`: padded slots still name some brick of the slab's table.
All inputs are finite; a program needn't handle non-finite values.
Results may differ from the reference program's by a relative error of at most 0.008.
Values may be sent and summed in bfloat16 or wider, within the bound.
No kernel may reach another device: no remote copies, remote signals or barrier semaphores. Data moves between devices by JAX's collectives and lax.ppermute only.
A program may use at most 64 MiB of HBM per device.

```python
import math
import jax
import jax.numpy as jnp
import numpy as np
from jax import lax

D = 128
SAMPLES = 64
BMAX = 2
BRICKS = 1024
SLABS = 8
RAYS = 2048


def draw_occupancy(key, part):
    level_key, spread_key = jax.random.split(jax.random.fold_in(key, 17))
    slab_level = jax.random.randint(level_key, (SLABS, 1), 0, 4)
    spread = jax.random.randint(spread_key, (SLABS, RAYS), 0, 4)
    counted = jnp.clip(spread + slab_level - 2, 0, BMAX)
    first_ray = jnp.arange(RAYS)[None, :] == 0
    return jnp.where(first_ray, BMAX, counted).astype(jnp.int32)


def set_ends(values, own_key, least, top_value):
    shape = values.shape
    place = [jax.random.randint(jax.random.fold_in(own_key, axis), (), 0, shape[axis]) for axis in range(len(shape))]
    values = values.at[tuple(place)].set(least)
    longest = shape.index(max(shape))
    place[longest] = (place[longest] + 1) % shape[longest]
    return values.at[tuple(place)].set(top_value)


def shard_levels(key, dims, cuts, least, largest):
    factor_of, own = 1.0, jax.random.fold_in(key, 6)
    for dim, blocks in cuts:
        heights = jnp.exp(jax.random.uniform(jax.random.fold_in(own, dim), (blocks,), jnp.float32, least / len(cuts), largest / len(cuts)))
        factor_of = factor_of * jnp.repeat(heights, dims[dim] // blocks).reshape([-1 if axis == dim else 1 for axis in range(len(dims))])
    return factor_of


def rank_bounds(count, lean):
    weights = [(1 << 20) // math.isqrt(standing ** lean) + 1 for standing in range(1, count + 1)]
    deviation = 1 + sum(weights) // (1 << 30)
    return np.cumsum(np.array([max(1, weight // deviation) for weight in weights]))


def ranked(own_key, extent, count, lean):
    table = rank_bounds(count, lean)
    ticket = jax.random.randint(jax.random.fold_in(own_key, 1), extent, 0, int(table[count - 1]))
    rank = jnp.searchsorted(jnp.asarray(table, jnp.int32), ticket, side="right")
    return jax.random.permutation(jax.random.fold_in(own_key, 2), count)[rank].astype(jnp.int32)


def gaussian(key, shape, scale, bound, cuts=(), kind=jnp.bfloat16):
    entries = jax.random.normal(key, shape, jnp.float32) * scale
    if len(cuts) > 0:
        entries = shard_levels(key, shape, cuts, -0.22, 0.18) * entries
    return jnp.clip(entries, min=-bound, max=bound).astype(kind)


def setup_inputs(seed: int = 0) -> dict:
    arg_keys = jax.random.split(jax.random.key(seed), 12)
    return {
        "ray_code": gaussian(arg_keys[0], (RAYS, D), 0.6, 4.0, ((0, 32),)),
        "direction": set_ends(jax.random.randint(arg_keys[1], (RAYS,), 0, 2), jax.random.fold_in(arg_keys[1], 1), 0, 1).astype(jnp.int32),
        "target": jnp.clip(1.0 * jax.random.uniform(arg_keys[2], (3, RAYS), jnp.float32) ** shard_levels(arg_keys[2], (3, RAYS), ((1, 4),), -0.2, 0.2), 0.0, 1.0),
        "brick_code": gaussian(arg_keys[3], (SLABS, BRICKS, D), 0.6, 4.0, ((0, 8),)),
        "sample_code": gaussian(arg_keys[4], (SLABS, SAMPLES, D), 0.6, 4.0, ((0, 8),)),
        "w_hidden": gaussian(arg_keys[5], (SLABS, D, D), D ** -0.5, 0.5, ((0, 8),)),
        "b_hidden": gaussian(arg_keys[6], (SLABS, D), 0.5, 3.0, ((0, 8),), jnp.float32),
        "w_out": gaussian(arg_keys[7], (SLABS, 4, D), D ** -0.5, 0.5, ((0, 8),)),
        "b_out": gaussian(arg_keys[8], (SLABS, 4), 1.0, 4.0, ((0, 8),), jnp.float32),
        "brick_ids": set_ends(ranked(arg_keys[9], (SLABS, BMAX, RAYS), BRICKS, 2), jax.random.fold_in(arg_keys[9], 3), 0, BRICKS - 1).astype(jnp.int32),
        "occupancy": draw_occupancy(jax.random.fold_in(arg_keys[11], 71), 0),
    }


step_length = 0.002


def shade_forward(brick_rows, sample_rows, ray_rows, slot_ids, occupied_count, hidden_w, hidden_b, out_w, out_b):
    chosen = jnp.take(brick_rows, slot_ids.T, axis=0)
    summed = (chosen.astype(jnp.float32)[:, :, None, :] + sample_rows.astype(jnp.float32)[None, None, :, :]
              + ray_rows.astype(jnp.float32)[:, None, None, :])
    inputs = summed.astype(jnp.bfloat16).reshape(-1, summed.shape[-1])
    preact = jnp.dot(inputs, hidden_w, preferred_element_type=jnp.float32) + hidden_b[None, :]
    hidden = jnp.maximum(preact, 0.0).astype(jnp.bfloat16)
    raw_out = jnp.dot(out_w, hidden.T, preferred_element_type=jnp.float32) + out_b[:, None]
    raw_out = raw_out.reshape(4, ray_rows.shape[0], -1)
    position = jnp.arange(raw_out.shape[2], dtype=jnp.int32) // sample_rows.shape[0]
    occupied = (position[None, :] < occupied_count[:, None]).astype(jnp.float32)
    return inputs, preact, hidden, raw_out, occupied


def render(raw_out, occupied):
    optical = step_length * jax.nn.softplus(raw_out[0]) * occupied
    entered = jnp.cumsum(optical, axis=-1) - optical
    weight = jnp.exp(-entered) * (-jnp.expm1(-optical))
    shading = jax.nn.sigmoid(raw_out[1:])
    colors = jnp.sum(weight[None] * shading, axis=-1)
    through = jnp.exp(-jnp.sum(optical, axis=-1))
    return optical, entered, weight, shading, colors, through


def shade_backward(inputs, preact, hidden, raw_out, occupied, hidden_w, out_w, color_cot, trans_cot):
    optical, entered, weight, shading, colors, through = render(raw_out, occupied)
    q_term = jnp.sum(shading * color_cot[:, :, None], axis=0)
    q_weight = q_term * weight
    after_sum = jnp.sum(q_weight, axis=-1, keepdims=True) - jnp.cumsum(q_weight, axis=-1)
    grad_optical = q_term * jnp.exp(-(entered + optical)) - after_sum - (trans_cot * through)[:, None]
    grad_density = step_length * grad_optical * occupied * jax.nn.sigmoid(raw_out[0])
    grad_shade = weight[None] * color_cot[:, :, None] * shading * (1.0 - shading)
    grad_raw = jnp.concatenate([grad_density[None], grad_shade], axis=0).reshape(4, -1)
    raw_rounded = grad_raw.astype(jnp.bfloat16)
    grad_hidden = jnp.dot(raw_rounded.T, out_w, preferred_element_type=jnp.float32)
    grad_pre = jnp.where(preact > 0.0, grad_hidden, 0.0).astype(jnp.bfloat16)
    grad_w_out = jnp.dot(raw_rounded, hidden, preferred_element_type=jnp.float32)
    grad_b_out = jnp.sum(grad_raw, axis=1)
    grad_w_hidden = jnp.dot(inputs.T, grad_pre, preferred_element_type=jnp.float32)
    grad_b_hidden = jnp.sum(grad_pre.astype(jnp.float32), axis=0)
    grad_inputs = jnp.dot(grad_pre, hidden_w.T, preferred_element_type=jnp.float32)
    return grad_w_out, grad_b_out, grad_w_hidden, grad_b_hidden, grad_inputs


def combine_pair(first, second, order_flag):
    first_color, first_trans = first
    second_color, second_trans = second
    first_ahead = first_color + first_trans[None] * second_color
    second_ahead = second_color + second_trans[None] * first_color
    return jnp.where(order_flag[None], first_ahead, second_ahead), first_trans * second_trans


def composite(seg_color, seg_trans, direction):
    forward = direction == 0
    backward = direction == 1
    start = (jnp.zeros(seg_color.shape[1:], jnp.float32), jnp.ones(seg_trans.shape[1:], jnp.float32))

    def lower_step(totals, pieces):
        return combine_pair(totals, pieces, forward), totals

    def upper_step(totals, pieces):
        return combine_pair(totals, pieces, backward), totals

    ended, (low_color, low_trans) = lax.scan(lower_step, start, (seg_color, seg_trans))
    ended, (high_color, high_trans) = lax.scan(upper_step, start, (seg_color, seg_trans), reverse=True)
    return low_color, low_trans, high_color, high_trans


def reference(ray_code, direction, target, brick_code, sample_code, w_hidden, b_hidden, w_out, b_out, brick_ids, occupancy):
    total_rays = ray_code.shape[0]
    feature_width = ray_code.shape[1]
    block_rays = math.gcd(total_rays, 128)
    count_blocks = total_rays // block_rays
    ray_blocks = ray_code.reshape(count_blocks, block_rays, feature_width)
    slots = brick_ids.shape[1]

    def split_slab(slot_all, occ_all):
        id_blocks = slot_all.reshape(slots, count_blocks, block_rays).transpose(1, 0, 2)
        return id_blocks, occ_all.reshape(count_blocks, block_rays)

    def slab_forward(pieces):
        brick_rows, sample_rows, hidden_w, hidden_b, out_w, out_b, slot_all, occ_all = pieces
        id_blocks, occ_blocks = split_slab(slot_all, occ_all)

        def one_block(operands):
            ray_rows, slot_ids, occupied_count = operands
            inputs, preact, hidden, raw_out, occupied = shade_forward(
                brick_rows, sample_rows, ray_rows, slot_ids, occupied_count, hidden_w, hidden_b, out_w, out_b)
            rendered = render(raw_out, occupied)
            return rendered[4], rendered[5]

        colors_b, through_b = lax.map(one_block, (ray_blocks, id_blocks, occ_blocks))
        return colors_b.transpose(1, 0, 2).reshape(3, total_rays), through_b.reshape(total_rays)

    seg_color, seg_trans = lax.map(slab_forward, (brick_code, sample_code, w_hidden, b_hidden, w_out, b_out, brick_ids, occupancy))
    low_color, low_trans, high_color, high_trans = composite(seg_color, seg_trans, direction)
    forward = (direction == 0)[None, :]
    before_color = jnp.where(forward[:, None, :], low_color, high_color)
    before_trans = jnp.where(forward, low_trans, high_trans)
    after_color = jnp.where(forward[:, None, :], high_color, low_color)
    color = before_color[0] + before_trans[0][None, :] * (seg_color[0] + seg_trans[0][None, :] * after_color[0])
    residual_g = color - target
    cot_color = before_trans[:, None, :] * residual_g[None]
    cot_trans = before_trans * jnp.sum(after_color * residual_g[None], axis=1)

    def slab_backward(pieces):
        brick_rows, sample_rows, hidden_w, hidden_b, out_w, out_b, slot_all, occ_all, color_cot, trans_cot = pieces
        id_blocks, occ_blocks = split_slab(slot_all, occ_all)
        color_blocks = color_cot.reshape(3, count_blocks, block_rays).transpose(1, 0, 2)
        trans_blocks = trans_cot.reshape(count_blocks, block_rays)

        def one_block(totals, operands):
            ray_rows, slot_ids, occupied_count, block_color_cot, block_trans_cot = operands
            inputs, preact, hidden, raw_out, occupied = shade_forward(
                brick_rows, sample_rows, ray_rows, slot_ids, occupied_count, hidden_w, hidden_b, out_w, out_b)
            grad_w_out, grad_b_out, grad_w_hidden, grad_b_hidden, grad_inputs = shade_backward(
                inputs, preact, hidden, raw_out, occupied, hidden_w, out_w, block_color_cot, block_trans_cot)
            per_position = grad_inputs.reshape(block_rays, slots, sample_rows.shape[0], feature_width)
            per_slot = jnp.sum(per_position, axis=2)
            brick_sum = jax.ops.segment_sum(per_slot.reshape(-1, feature_width), slot_ids.T.reshape(-1),
                                            num_segments=brick_rows.shape[0])
            totals = (totals[0] + grad_w_out, totals[1] + grad_b_out, totals[2] + grad_w_hidden,
                      totals[3] + grad_b_hidden, totals[4] + jnp.sum(per_position, axis=(0, 1)), totals[5] + brick_sum)
            return totals, jnp.sum(per_slot, axis=1)

        start = (jnp.zeros((4, feature_width), jnp.float32), jnp.zeros((4,), jnp.float32),
                 jnp.zeros((feature_width, feature_width), jnp.float32), jnp.zeros((feature_width,), jnp.float32),
                 jnp.zeros((sample_rows.shape[0], feature_width), jnp.float32),
                 jnp.zeros((brick_rows.shape[0], feature_width), jnp.float32))
        totals, ray_grads = lax.scan(one_block, start, (ray_blocks, id_blocks, occ_blocks, color_blocks, trans_blocks))
        return totals + (ray_grads.reshape(total_rays, feature_width),)

    results = lax.map(slab_backward, (brick_code, sample_code, w_hidden, b_hidden, w_out, b_out, brick_ids, occupancy, cot_color, cot_trans))
    grad_w_out, grad_b_out, grad_w_hidden, grad_b_hidden, grad_sample, grad_brick, ray_all = results
    grad_ray = jnp.sum(ray_all, axis=0)
    return color, grad_ray, grad_brick, grad_sample, grad_w_hidden, grad_b_hidden, grad_w_out, grad_b_out
```

```python
import functools

import jax
import jax.numpy as jnp
from jax import lax
from jax.experimental import pallas as pl
from jax.experimental.pallas import tpu as pltpu
from jax.sharding import PartitionSpec as P

step_length = 0.002
f32 = jnp.float32
bf16 = jnp.bfloat16
vmem_bytes = 48 * 1024 * 1024
exact = lax.Precision.HIGHEST


def bits_of(count):
    bits = count.bit_length() - 1
    assert count == 1 << bits
    return bits


def reversed_bits(value, bits):
    return sum(((value >> i) & 1) << (bits - 1 - i) for i in range(bits))


def nt_dot(a, b, precision=None):
    return lax.dot_general(
        a, b, (((1,), (1,)), ((), ())), precision=precision, preferred_element_type=f32
    )


def nn_dot(a, b, precision=None):
    return jnp.dot(a, b, precision=precision, preferred_element_type=f32)


def swap(array, axis, size, distance):
    return lax.ppermute(array, axis, [(i, i ^ distance) for i in range(size)])


def call(kernel, out_shape, name, scratch=(), smem=0, count=0):
    specs = [pl.BlockSpec(memory_space=pltpu.SMEM)] * smem
    specs += [pl.BlockSpec(memory_space=pltpu.VMEM)] * (count - smem)
    return pl.pallas_call(
        kernel,
        out_shape=out_shape,
        in_specs=specs,
        out_specs=jax.tree.map(lambda _: pl.BlockSpec(memory_space=pltpu.VMEM), out_shape),
        scratch_shapes=list(scratch),
        compiler_params=pltpu.CompilerParams(vmem_limit_bytes=vmem_bytes),
        name=name,
    )


def prepare_kernel(ids_ref, brick_ref, w_ref, chosen_ref, project_ref):
    slots, rays = ids_ref.shape
    bricks = brick_ref.shape[0]
    brick_t = brick_ref[...].astype(f32).T.astype(bf16)
    w_t = w_ref[...].astype(f32).T.astype(bf16)
    row = lax.broadcasted_iota(jnp.int32, (bricks, rays), 0)
    for k in range(slots):
        one_hot = jnp.where(row == ids_ref[k : k + 1, :], 1.0, 0.0).astype(bf16)
        chosen = nn_dot(brick_t, one_hot).astype(bf16)
        chosen_ref[:, k * rays : (k + 1) * rays] = chosen
        project_ref[:, k * rays : (k + 1) * rays] = nn_dot(w_t, chosen)


def forward_kernel(
    me_ref,
    project_ref,
    ray_ref,
    w_ref,
    b_ref,
    sample_ref,
    w_out_ref,
    b_out_ref,
    occ_ref,
    seg_ref,
    coef_ref,
    u_ref,
    s_ref,
    ray_sorted_ref,
    ut_ref,
    wide_ref,
    raw_ref,
    *,
    owners,
):
    width, total = project_ref.shape
    rays = ray_ref.shape[0]
    slots = total // rays
    samples = sample_ref.shape[0]
    own = rays // owners
    bits = bits_of(owners)
    me = me_ref[0, 0]
    for t in range(owners):
        place = pl.multiple_of((me ^ t) * own, own)
        at = reversed_bits(t, bits) * own
        ray_sorted_ref[pl.ds(place, own), :] = ray_ref[at : at + own, :]
    w_t = w_ref[...].astype(f32).T.astype(bf16)
    ray_t = nt_dot(w_t, ray_sorted_ref[...])
    for k in range(slots):
        part = (project_ref[:, k * rays : (k + 1) * rays] + ray_t).astype(bf16)
        ut_ref[:, k * rays : (k + 1) * rays] = part
        u_ref[k * rays : (k + 1) * rays, :] = part.astype(f32).T.astype(bf16)
    s = nn_dot(sample_ref[...], w_ref[...]) + b_ref[...]
    s_low = s.astype(bf16)
    s_ref[...] = s_low.astype(f32)
    s_t = jnp.concatenate([s, s], 0).T
    for j in range(samples):
        wide_ref[j] = jnp.broadcast_to(s_t[:, j : j + 1], (width, 128)).astype(bf16)
    outs = w_out_ref.shape[0]
    w_rows = jnp.concatenate(
        [jnp.broadcast_to(w_out_ref[c : c + 1, :].astype(f32), (8, width)) for c in range(outs)], 0
    )
    row8 = lax.broadcasted_iota(jnp.int32, (outs * 8, width), 0) % 8
    left = [jnp.where(row8 == i, w_rows, 0.0).astype(bf16) for i in range(8)]
    left = [jnp.concatenate([left[2 * i], left[2 * i + 1]], 1) for i in range(4)]

    def shade_block(block, carry):
        for n in range(total // 256):
            lanes = slice(n * 256, n * 256 + 256)
            ut = ut_ref[:, lanes]
            acc = None
            for i in range(4):
                parts = []
                for h in range(2):
                    column = wide_ref[block * 8 + 2 * i + h]
                    column = jnp.concatenate([column, column], 1)
                    parts.append(jnp.maximum(ut + column, 0))
                term = nn_dot(left[i], jnp.concatenate(parts, 0))
                acc = term if acc is None else acc + term
            for c in range(outs):
                raw_ref[c, pl.ds(pl.multiple_of(block * 8, 8), 8), lanes] = (
                    acc[c * 8 : c * 8 + 8, :] + b_out_ref[0, c]
                )
        return carry

    lax.fori_loop(0, samples // 8, shade_block, 0)
    r_i = lax.broadcasted_iota(jnp.int32, (samples, samples), 0)
    c_i = lax.broadcasted_iota(jnp.int32, (samples, samples), 1)
    earlier = jnp.where(c_i < r_i, 1.0, 0.0).astype(f32)
    later = jnp.where(c_i > r_i, 1.0, 0.0).astype(f32)
    chunk = 128
    for n in range(rays // chunk):
        occ = occ_ref[:, n * chunk : (n + 1) * chunk]
        before = jnp.zeros((1, chunk), f32)
        kept = []
        for k in range(slots):
            lanes = slice(k * rays + n * chunk, k * rays + (n + 1) * chunk)
            x = raw_ref[0, :, lanes]
            occupied = (k < occ).astype(f32)
            tail = jnp.exp(-jnp.abs(x))
            optical = step_length * (jnp.maximum(x, 0.0) + jnp.log1p(tail)) * occupied
            entered = nn_dot(earlier, optical, exact) + before
            before = before + jnp.sum(optical, 0, keepdims=True)
            half = jnp.tanh(0.5 * optical)
            weight = jnp.exp(-entered) * (2.0 * half / (1.0 + half))
            shading = [jax.nn.sigmoid(raw_ref[c, :, lanes]) for c in range(1, outs)]
            passed = jnp.exp(-(entered + optical))
            density = step_length * occupied * jax.nn.sigmoid(x)
            kept.append((lanes, weight, shading, passed, density))
        through = jnp.exp(-before)
        after = [jnp.zeros((1, chunk), f32)] * (outs - 1)
        for lanes, weight, shading, passed, density in reversed(kept):
            for c in range(outs - 1):
                light = weight * shading[c]
                behind = nn_dot(later, light, exact) + after[c]
                after[c] = after[c] + jnp.sum(light, 0, keepdims=True)
                coef_ref[c, :, lanes] = density * (shading[c] * passed - behind)
                coef_ref[outs + c, :, lanes] = light * (1.0 - shading[c])
            coef_ref[outs - 1, :, lanes] = density * through
        place = slice(n * chunk, (n + 1) * chunk)
        for c in range(outs - 1):
            seg_ref[c : c + 1, place] = after[c]
        seg_ref[outs - 1 : outs, place] = through


def merge(first, second, forward):
    fc, ft = first
    sc, st = second
    return jnp.where(forward, fc + ft * sc, sc + st * fc), ft * st


def backward_kernel(
    me_ref,
    seg_ref,
    got_ref,
    direction_ref,
    target_ref,
    coef_ref,
    u_ref,
    s_ref,
    ids_ref,
    chosen_ref,
    ray_ref,
    sample_ref,
    w_ref,
    w_out_ref,
    color_ref,
    ray_out_ref,
    brick_out_ref,
    small_ref,
    g_ref,
    gg_ref,
    slot_ref,
    by_sample_ref,
    *,
    owners,
    shares,
):
    me = me_ref[0, 0]
    share = me_ref[0, 1]
    channels = target_ref.shape[0]
    outs = channels + 1
    rays = target_ref.shape[1]
    total, width = u_ref.shape
    slots = total // rays
    samples = s_ref.shape[0]
    bricks = brick_out_ref.shape[0]
    bits = bits_of(owners)
    forward = direction_ref[...] == 0

    def pair(values):
        return values[:channels, :], values[channels : channels + 1, :]

    low = high = None
    for b in reversed(range(bits)):
        piece = pair(got_ref[b])
        is_low = ((me >> b) & 1) == 1
        piece = (jnp.where(is_low, piece[0], 0.0), jnp.where(is_low, piece[1], 1.0))
        low = piece if low is None else merge(low, piece, forward)
    for b in range(bits):
        piece = pair(got_ref[b])
        is_high = ((me >> b) & 1) == 0
        piece = (jnp.where(is_high, piece[0], 0.0), jnp.where(is_high, piece[1], 1.0))
        high = piece if high is None else merge(high, piece, forward)
    seg_color, seg_trans = pair(seg_ref[...])
    before_color = jnp.where(forward, low[0], high[0])
    before_trans = jnp.where(forward, low[1], high[1])
    after_color = jnp.where(forward, high[0], low[0])
    color = before_color + before_trans * (seg_color + seg_trans * after_color)
    residual = color - target_ref[...]
    color_cot = before_trans * residual
    trans_cot = before_trans * jnp.sum(after_color * residual, 0, keepdims=True)
    own = rays // owners
    r_i = lax.broadcasted_iota(jnp.int32, (rays, own), 0)
    c_i = lax.broadcasted_iota(jnp.int32, (rays, own), 1)
    pick = jnp.where(r_i == c_i + me * own, 1.0, 0.0).astype(f32)
    color_ref[...] = nn_dot(color, pick, exact)

    bias_sums = [jnp.zeros((1, 128), f32)] * outs
    for n in range(total // 128):
        lanes = slice(n * 128, n * 128 + 128)
        at = (n * 128) % rays
        cots = [color_cot[c : c + 1, at : at + 128] for c in range(channels)]
        grads = [
            sum(cots[c] * coef_ref[c, :, lanes] for c in range(channels))
            - trans_cot[:, at : at + 128] * coef_ref[channels, :, lanes]
        ]
        for c in range(channels):
            grads.append(cots[c] * coef_ref[outs + c, :, lanes])
        for c in range(outs):
            g = grads[c]
            bias_sums[c] = bias_sums[c] + jnp.sum(g, 0, keepdims=True)
            gg_ref[c, lanes, :] = jnp.concatenate([g] * (128 // samples), 0).T
        for j in range(0, samples, 8):
            g_ref[j // 8, :, lanes] = jnp.concatenate([g[j : j + 8] for g in grads], 0).astype(bf16)
    w_rows = [w_out_ref[c : c + 1, :].astype(f32) for c in range(outs)]
    negative = (-s_ref[...]).astype(bf16)
    one = jnp.ones((samples, width), bf16)
    zero = jnp.zeros((samples, width), bf16)
    lane = lax.broadcasted_iota(jnp.int32, (8, 8 * samples), 1) // samples
    row = lax.broadcasted_iota(jnp.int32, (8, 8 * samples), 0)
    block_mask = lane == row
    repeat = 8 * samples // 128

    def slot_block(block, sums):
        at = pl.multiple_of(block * 16, 16)
        u16 = u_ref[pl.ds(at, 16), :]
        sums = list(sums)
        for h in range(2):
            base = pl.multiple_of(block * 16 + h * 8, 8)
            left = [
                jnp.where(
                    block_mask, jnp.concatenate([gg_ref[c, pl.ds(base, 8), :]] * repeat, 1), 0.0
                )
                for c in range(outs)
            ]
            left = jnp.concatenate(left, 0).astype(bf16)
            tiles = [
                jnp.where(
                    jnp.broadcast_to(u16[h * 8 + i : h * 8 + i + 1, :], (samples, width))
                    > negative,
                    one,
                    zero,
                )
                for i in range(8)
            ]
            h1 = nn_dot(left, jnp.concatenate(tiles, 0))
            u8 = u16[h * 8 : h * 8 + 8, :].astype(f32)
            grad = None
            for c in range(outs):
                piece = h1[c * 8 : c * 8 + 8, :]
                sums[c] = sums[c] + u8 * piece
                term = w_rows[c] * piece
                grad = term if grad is None else grad + term
            slot_ref[pl.ds(base, 8), :] = grad
        return tuple(sums)

    sums = lax.fori_loop(0, total // 16, slot_block, tuple([jnp.zeros((8, width), f32)] * outs))
    row8 = lax.broadcasted_iota(jnp.int32, (8, width), 0)

    def sample_block(block, sums):
        at = pl.multiple_of(block * 8, 8)
        left = g_ref[block]
        s8 = s_ref[pl.ds(at, 8), :]
        acc = [jnp.zeros((8, width), f32)] * outs
        for i in range(8):
            edge = (-s8[i : i + 1, :]).astype(bf16)
            h2 = None
            for n in range(total // 256):
                u = u_ref[n * 256 : n * 256 + 256, :]
                live = jnp.where(
                    u > jnp.broadcast_to(edge, u.shape),
                    jnp.ones(u.shape, bf16),
                    jnp.zeros(u.shape, bf16),
                )
                term = nn_dot(left[:, n * 256 : n * 256 + 256], live)
                h2 = term if h2 is None else h2 + term
            for c in range(outs):
                acc[c] = acc[c] + jnp.where(row8 == i, h2[c * 8 : c * 8 + 8, :], 0.0)
        by_sample_ref[pl.ds(at, 8), :] = sum(w_rows[c] * acc[c] for c in range(outs))
        return tuple(sums[c] + s8 * acc[c] for c in range(outs))

    sums = lax.fori_loop(0, samples // 8, sample_block, sums)

    w = w_ref[...].astype(f32)
    slot = slot_ref[...]
    by_sample = by_sample_ref[...]
    moved = nt_dot(slot, w, exact)
    grad_ray = moved[:rays, :]
    for k in range(1, slots):
        grad_ray = grad_ray + moved[k * rays : (k + 1) * rays, :]
    slot_ref[:rays, :] = grad_ray
    for t in range(owners):
        place = pl.multiple_of((me ^ t) * own, own)
        at = reversed_bits(t, bits) * own
        ray_out_ref[at : at + own, :] = slot_ref[pl.ds(place, own), :].astype(ray_out_ref.dtype)
    share_bits = bits_of(shares)
    part = bricks // shares
    high_part = moved.astype(bf16)
    low_part = (moved - high_part.astype(f32)).astype(bf16)
    row = lax.broadcasted_iota(jnp.int32, (part, rays), 0)
    for t in range(shares):
        first = (share ^ t) * part
        at = reversed_bits(t, share_bits) * part
        acc = jnp.zeros((part, width), f32)
        for k in range(slots):
            one_hot = jnp.where(row + first == ids_ref[k : k + 1, :], 1.0, 0.0).astype(bf16)
            rows = slice(k * rays, (k + 1) * rays)
            acc = acc + nn_dot(one_hot, high_part[rows]) + nn_dot(one_hot, low_part[rows])
        brick_out_ref[at : at + part, :] = acc
    slot_ray = slot[:rays, :]
    for k in range(1, slots):
        slot_ray = slot_ray + slot[k * rays : (k + 1) * rays, :]
    small_ref[:samples, :] = nt_dot(by_sample, w, exact)
    ray_t = ray_ref[...].astype(f32).T
    sample_t = jnp.concatenate([sample_ref[...].astype(f32)] * (128 // samples), 0).T[:, :samples]
    small_ref[samples : samples + width, :] = (
        nn_dot(chosen_ref[...].astype(f32), slot, exact)
        + nn_dot(ray_t, slot_ray, exact)
        + nn_dot(sample_t, by_sample, exact)
    )
    at = samples + width
    small_ref[at : at + 1, :] = jnp.sum(by_sample, 0, keepdims=True)
    for c in range(outs):
        small_ref[at + 1 + c : at + 2 + c, :] = jnp.sum(sums[c], 0, keepdims=True)
    lane128 = lax.broadcasted_iota(jnp.int32, (1, 128), 1)
    bias = jnp.zeros((1, 128), f32)
    for c in range(outs):
        bias = bias + jnp.where(lane128 == c, jnp.sum(bias_sums[c], 1, keepdims=True), 0.0)
    small_ref[at + 1 + outs : at + 2 + outs, :] = bias
    rest = small_ref.shape[0] - (at + 2 + outs)
    small_ref[at + 2 + outs :, :] = jnp.zeros((rest, width), f32)


def gather_rays(rays, owners):
    for b in reversed(range(bits_of(owners))):
        rays = jnp.concatenate([rays, swap(rays, "slab", owners, 1 << b)], 0)
    return rays


def body(
    ray_code,
    direction,
    target,
    brick_code,
    sample_code,
    w_hidden,
    b_hidden,
    w_out,
    b_out,
    brick_ids,
    occupancy,
):
    owners = lax.axis_size("slab")
    shares = lax.axis_size("ray")
    me = lax.axis_index("slab")
    share = lax.axis_index("ray")
    ids = brick_ids[0]
    slots, rays = ids.shape
    total = slots * rays
    bricks, width = brick_code.shape[1:]
    samples = sample_code.shape[1]
    outs = w_out.shape[1]
    channels = outs - 1
    w = w_hidden[0]
    direction = direction[None]
    where_am_i = jnp.stack([me, share]).astype(jnp.int32)[None]

    chosen, project = call(
        prepare_kernel,
        (
            jax.ShapeDtypeStruct((width, total), bf16),
            jax.ShapeDtypeStruct((width, total), f32),
        ),
        "prepare",
        count=3,
    )(ids, brick_code[0], w)
    ray_all = gather_rays(ray_code, owners)
    seg, coef, u, s, ray_sorted = call(
        functools.partial(forward_kernel, owners=owners),
        (
            jax.ShapeDtypeStruct((outs, rays), f32),
            jax.ShapeDtypeStruct((outs + channels, samples, total), f32),
            jax.ShapeDtypeStruct((total, width), bf16),
            jax.ShapeDtypeStruct((samples, width), f32),
            jax.ShapeDtypeStruct((rays, width), bf16),
        ),
        "forward",
        scratch=(
            pltpu.VMEM((width, total), bf16),
            pltpu.VMEM((samples, width, 128), bf16),
            pltpu.VMEM((outs, samples, total), f32),
        ),
        smem=1,
        count=9,
    )(where_am_i, project, ray_all, w, b_hidden, sample_code[0], w_out[0], b_out, occupancy)

    forward = direction == 0
    group = (seg[:channels], seg[channels:])
    got = []
    for b in range(bits_of(owners)):
        packed = jnp.concatenate(group, 0)
        other = swap(packed, "slab", owners, 1 << b)
        got.append(other)
        theirs = (other[:channels], other[channels:])
        upper = ((me >> b) & 1) == 1
        first = jax.tree.map(lambda a, b: jnp.where(upper, b, a), group, theirs)
        second = jax.tree.map(lambda a, b: jnp.where(upper, a, b), group, theirs)
        group = merge(first, second, forward)

    small_rows = -(-(samples + width + 2 + outs) // 16) * 16
    color_own, ray_part, brick_part, small = call(
        functools.partial(backward_kernel, owners=owners, shares=shares),
        (
            jax.ShapeDtypeStruct((channels, rays // owners), f32),
            jax.ShapeDtypeStruct((rays, width), f32),
            jax.ShapeDtypeStruct((bricks, width), f32),
            jax.ShapeDtypeStruct((small_rows, width), f32),
        ),
        "backward",
        scratch=(
            pltpu.VMEM((samples // 8, outs * 8, total), bf16),
            pltpu.VMEM((outs, total, 128), f32),
            pltpu.VMEM((total, width), f32),
            pltpu.VMEM((samples, width), f32),
        ),
        smem=1,
        count=14,
    )(
        where_am_i,
        seg,
        jnp.stack(got),
        direction,
        target,
        coef,
        u,
        s,
        ids,
        chosen,
        ray_sorted,
        sample_code[0],
        w,
        w_out[0],
    )

    for b in range(bits_of(owners)):
        half = ray_part.shape[0] // 2
        ray_part = ray_part[:half] + swap(ray_part[half:].astype(bf16), "slab", owners, 1 << b)
    for b in range(bits_of(shares)):
        half = brick_part.shape[0] // 2
        brick_part = brick_part[:half] + swap(brick_part[half:].astype(bf16), "ray", shares, 1 << b)
        small = small + swap(small, "ray", shares, 1 << b)
    at = samples + width
    return (
        color_own,
        ray_part,
        brick_part[None],
        small[None, :samples],
        small[None, samples:at],
        small[at : at + 1],
        small[None, at + 1 : at + 1 + outs],
        small[at + 1 + outs : at + 2 + outs, :outs],
    )


def solution(mesh):
    in_specs = (
        P(("ray", "slab"), None),
        P("ray"),
        P(None, "ray"),
        P("slab", None, None),
        P("slab", None, None),
        P("slab", None, None),
        P("slab", None),
        P("slab", None, None),
        P("slab", None),
        P("slab", None, "ray"),
        P("slab", "ray"),
    )
    out_specs = (
        P(None, ("ray", "slab")),
        P(("ray", "slab"), None),
        P("slab", "ray", None),
        P("slab", None, None),
        P("slab", None, None),
        P("slab", None),
        P("slab", None, None),
        P("slab", None),
    )
    return jax.shard_map(body, mesh=mesh, in_specs=in_specs, out_specs=out_specs, check_vma=False)
```

```python
import functools

import jax
import jax.numpy as jnp
from jax import lax
from jax.experimental import pallas as pl
from jax.experimental.pallas import tpu as pltpu
from jax.sharding import PartitionSpec as P

step_length = 0.002
f32 = jnp.float32
bf16 = jnp.bfloat16
vmem_bytes = 24 * 1024 * 1024
exact = lax.Precision.HIGHEST


def bits_of(count):
    bits = count.bit_length() - 1
    assert count == 1 << bits
    return bits


def swap_order(count, descending):
    order = [0]
    for b in reversed(range(bits_of(count))) if descending else range(bits_of(count)):
        order = order + [t ^ (1 << b) for t in order]
    return order


def halving_order(count):
    order = [0]
    for b in reversed(range(bits_of(count))):
        order = order + [t ^ (1 << b) for t in order]
    return order


def split_dot(a, b, dot):
    high = a.astype(bf16)
    low = (a - high.astype(f32)).astype(bf16)
    return dot(high, b) + dot(low, b)


def nt_dot(a, b, precision=None):
    return lax.dot_general(
        a, b, (((1,), (1,)), ((), ())), precision=precision, preferred_element_type=f32
    )


def nn_dot(a, b, precision=None):
    return jnp.dot(a, b, precision=precision, preferred_element_type=f32)


def swap(array, axis, size, distance):
    return lax.ppermute(array, axis, [(i, i ^ distance) for i in range(size)])


def sum_dot(ones, b):
    high = b.astype(bf16)
    low = (b - high.astype(f32)).astype(bf16)
    return nn_dot(ones, high) + nn_dot(ones, low)


def call(kernel, out_shape, name, scratch=(), flops=0):
    def run(*operands):
        return pl.pallas_call(
            kernel,
            out_shape=out_shape,
            in_specs=[pl.BlockSpec(memory_space=pltpu.VMEM)] * len(operands),
            out_specs=jax.tree.map(lambda _: pl.BlockSpec(memory_space=pltpu.VMEM), out_shape),
            scratch_shapes=list(scratch),
            compiler_params=pltpu.CompilerParams(vmem_limit_bytes=vmem_bytes),
            cost_estimate=pl.CostEstimate(flops=flops, bytes_accessed=1 << 20, transcendentals=0),
            name=name,
        )(*operands)

    return run


def low_rows(width, samples):
    starts = {"w": 0, "sample": width, "w_out": width + samples}
    sizes = {"w": width, "sample": samples, "w_out": 16}
    return {name: slice(at, at + sizes[name]) for name, at in starts.items()}


def line_rows(slots, channels):
    return {
        "ids": 0,
        "occ": slots,
        "direction": slots + 1,
        "target": slots + 2,
        "b_out": slots + 2 + channels,
    }


def turn_kernel(brick_ref, ray_ref, brick_t_ref, own_ref):
    brick_t_ref[...] = brick_ref[...].astype(f32).T.astype(bf16)
    own_ref[...] = ray_ref[...]


def prepare_kernel(
    brick_t_ref,
    w_ref,
    sample_ref,
    w_out_ref,
    ids_ref,
    occ_ref,
    direction_ref,
    target_ref,
    b_ref,
    b_out_ref,
    low_ref,
    lines_ref,
    w_t_ref,
    s_ref,
    wide_ref,
    left_ref,
    chosen_ref,
    project_ref,
    *,
    rows,
    lines,
):
    slots, rays = ids_ref.shape
    width = w_t_ref.shape[0]
    samples = s_ref.shape[0]
    outs = w_out_ref.shape[0]
    bricks = brick_t_ref.shape[1]
    w = w_ref[...]
    w_out = w_out_ref[...].astype(f32)
    low_ref[rows["w"], :] = w
    low_ref[rows["sample"], :] = sample_ref[...]
    low_ref[rows["w_out"], :] = jnp.concatenate(
        [w_out, jnp.zeros((16 - outs, width), f32)], 0
    ).astype(bf16)
    lines_ref[:slots, :] = ids_ref[...].astype(f32)
    lines_ref[lines["occ"] : lines["occ"] + 1, :] = occ_ref[...].astype(f32)
    lines_ref[lines["direction"] : lines["direction"] + 1, :] = direction_ref[...].astype(f32)
    lines_ref[lines["target"] : lines["target"] + outs - 1, :] = target_ref[...]
    lines_ref[lines["b_out"] : lines["b_out"] + 1, :outs] = b_out_ref[...]
    w_t = w.astype(f32).T.astype(bf16)
    w_t_ref[...] = w_t
    s = nn_dot(sample_ref[...], w) + b_ref[...]
    s_ref[...] = s.astype(bf16).astype(f32)
    s_t = jnp.concatenate([s] * (128 // samples), 0).T
    for j in range(samples):
        wide_ref[j] = jnp.broadcast_to(s_t[:, j : j + 1], (width, 128)).astype(bf16)
    w_rows = jnp.concatenate(
        [jnp.broadcast_to(w_out[c : c + 1, :], (8, width)) for c in range(outs)], 0
    )
    row8 = lax.broadcasted_iota(jnp.int32, (outs * 8, width), 0) % 8
    for i in range(8):
        left_ref[:, i * width : (i + 1) * width] = jnp.where(row8 == i, w_rows, 0.0).astype(bf16)
    row = lax.broadcasted_iota(jnp.int32, (bricks, rays), 0)
    for k in range(slots):
        one_hot = jnp.where(row == ids_ref[k : k + 1, :], 1.0, 0.0).astype(bf16)
        chosen = nn_dot(brick_t_ref[...], one_hot).astype(bf16)
        chosen_ref[:, k * rays : (k + 1) * rays] = chosen
        project_ref[:, k * rays : (k + 1) * rays] = nn_dot(w_t, chosen)


def forward_kernel(*refs, owners, second, lines):
    ray_ref, project_ref, w_t_ref, wide_ref, left_ref, lines_ref, *refs = refs
    if second:
        before_refs, refs = refs[:4], refs[4:]
    seg_ref, kept_ref, u_ref, sorted_ref, order_ref, ut_ref, raw_ref = refs
    width, total = project_ref.shape
    samples = wide_ref.shape[0]
    outs = seg_ref.shape[0]
    half, rays = ray_ref.shape[0], lines_ref.shape[1]
    slots = total // rays
    blocks = owners // 2
    own = half // blocks
    me = lax.axis_index("slab")
    side = me // blocks
    if second:
        first_half = pl.multiple_of(side * half, half)
        for old, new in zip(before_refs[:2], (seg_ref, kept_ref)):
            for k in range(old.shape[-1] // half):
                lanes = pl.ds(pl.multiple_of(k * rays + first_half, half), half)
                new[..., lanes] = old[..., k * half : (k + 1) * half]
        for old, new in zip(before_refs[2:], (u_ref, sorted_ref)):
            for k in range(old.shape[0] // half):
                rows = pl.ds(pl.multiple_of(k * rays + first_half, half), half)
                new[rows, :] = old[k * half : (k + 1) * half, :]
        side = 1 - side
    here = pl.multiple_of(side * half, half)
    stride = rays if second else half
    base = here if second else 0

    def spot(offset, size):
        return pl.ds(pl.multiple_of(offset + base, 128), size) if second else pl.ds(offset, size)

    for i in range(blocks):
        place = pl.multiple_of(((me ^ i) & (blocks - 1)) * own, own)
        order_ref[pl.ds(place, own), :] = ray_ref[i * own : (i + 1) * own, :]
    sorted_ref[spot(0, half), :] = order_ref[...]
    ray_t = nt_dot(w_t_ref[...], order_ref[...])
    for k in range(slots):
        lanes = pl.ds(pl.multiple_of(k * rays + here, half), half)
        part = (project_ref[:, lanes] + ray_t).astype(bf16)
        ut_ref[:, k * half : (k + 1) * half] = part
        u_ref[spot(k * stride, half), :] = part.astype(f32).T.astype(bf16)
    b_out = [lines_ref[lines["b_out"], c] for c in range(outs)]

    def shade_block(block, carry):
        for n in range(slots * half // 256):
            lanes = slice(n * 256, n * 256 + 256)
            ut = ut_ref[:, lanes]
            acc = None
            for i in range(4):
                parts = []
                for h in range(2):
                    column = wide_ref[block * 8 + 2 * i + h]
                    column = jnp.concatenate([column, column], 1)
                    parts.append(jnp.maximum(ut + column, 0))
                left = left_ref[:, 2 * i * width : 2 * (i + 1) * width]
                term = nn_dot(left, jnp.concatenate(parts, 0))
                acc = term if acc is None else acc + term
            for c in range(outs):
                raw_ref[c, pl.ds(pl.multiple_of(block * 8, 8), 8), lanes] = (
                    acc[c * 8 : c * 8 + 8, :] + b_out[c]
                )
        return carry

    lax.fori_loop(0, samples // 8, shade_block, 0, unroll=4)
    r_i = lax.broadcasted_iota(jnp.int32, (samples, samples), 0)
    c_i = lax.broadcasted_iota(jnp.int32, (samples, samples), 1)
    earlier = jnp.where(c_i < r_i, 1.0, 0.0).astype(bf16)
    chunk = 128
    occ_row = lines["occ"]
    for n in range(half // chunk):
        occ = lines_ref[occ_row : occ_row + 1, pl.ds(pl.multiple_of(here + n * chunk, chunk), chunk)]
        raws = [
            raw_ref[0, :, k * half + n * chunk : k * half + (n + 1) * chunk] for k in range(slots)
        ]
        occupied = [(k < occ).astype(f32) for k in range(slots)]
        opticals = [
            step_length * (jnp.maximum(x, 0.0) + jnp.log1p(jnp.exp(-jnp.abs(x)))) * o
            for x, o in zip(raws, occupied)
        ]
        enters = sum_dot(earlier, jnp.concatenate(opticals, 1))
        before = jnp.zeros((1, chunk), f32)
        colors = [jnp.zeros((1, chunk), f32)] * (outs - 1)
        for k in range(slots):
            local = slice(k * half + n * chunk, k * half + (n + 1) * chunk)
            lanes = spot(k * stride + n * chunk, chunk)
            optical = opticals[k]
            entered = enters[:, k * chunk : (k + 1) * chunk] + before
            before = before + jnp.sum(optical, 0, keepdims=True)
            tanh = jnp.tanh(0.5 * optical)
            weight = jnp.exp(-entered) * (2.0 * tanh / (1.0 + tanh))
            for c in range(outs - 1):
                shading = jax.nn.sigmoid(raw_ref[c + 1, :, local])
                light = weight * shading
                colors[c] = colors[c] + jnp.sum(light, 0, keepdims=True)
                kept_ref[c, :, lanes] = shading
                kept_ref[outs + c, :, lanes] = light
            kept_ref[outs - 1, :, lanes] = jnp.exp(-(entered + optical))
            kept_ref[2 * outs - 1, :, lanes] = step_length * occupied[k] * jax.nn.sigmoid(raws[k])
        place = spot(n * chunk, chunk)
        for c in range(outs - 1):
            seg_ref[c : c + 1, place] = colors[c]
        seg_ref[outs - 1 : outs, place] = jnp.exp(-before)


def coefficient_kernel(seg_ref, kept_ref, coef_ref, turned_ref):
    outs, rays = seg_ref.shape
    samples, total = kept_ref.shape[1:]
    slots = total // rays
    r_i = lax.broadcasted_iota(jnp.int32, (samples, samples), 0)
    c_i = lax.broadcasted_iota(jnp.int32, (samples, samples), 1)
    later = jnp.where(c_i > r_i, 1.0, 0.0).astype(bf16)
    chunk = 128

    def keep(index, lanes, value):
        coef_ref[index, :, lanes] = value
        turned_ref[index, lanes, :] = jnp.concatenate([value] * (128 // samples), 0).T

    for n in range(rays // chunk):
        through = seg_ref[outs - 1 : outs, n * chunk : (n + 1) * chunk]
        after = [jnp.zeros((1, chunk), f32)] * (outs - 1)
        for k in reversed(range(slots)):
            lanes = slice(k * rays + n * chunk, k * rays + (n + 1) * chunk)
            passed = kept_ref[outs - 1, :, lanes]
            density = kept_ref[2 * outs - 1, :, lanes]
            lights = [kept_ref[outs + c, :, lanes] for c in range(outs - 1)]
            behinds = sum_dot(later, jnp.concatenate(lights, 1))
            for c in range(outs - 1):
                shading = kept_ref[c, :, lanes]
                light = lights[c]
                behind = behinds[:, c * chunk : (c + 1) * chunk] + after[c]
                after[c] = after[c] + jnp.sum(light, 0, keepdims=True)
                keep(c, lanes, density * (shading * passed - behind))
                keep(outs + c, lanes, light * (1.0 - shading))
            keep(outs - 1, lanes, density * through)


def basis_kernel(turned_ref, u_ref, s_ref, h1_ref, *, slot):
    count, rays, width = h1_ref.shape
    samples = s_ref.shape[0]
    negative = (-s_ref[...]).astype(bf16)
    one = jnp.ones((samples, width), bf16)
    zero = jnp.zeros((samples, width), bf16)
    lane = lax.broadcasted_iota(jnp.int32, (8, 8 * samples), 1) // samples
    row = lax.broadcasted_iota(jnp.int32, (8, 8 * samples), 0)
    block_mask = lane == row
    repeat = 8 * samples // 128
    step = 128

    def slot_block(block, carry):
        for h in range(step // 16):
            base = pl.multiple_of(block * step + h * 16, 16)
            u16 = u_ref[pl.ds(slot * rays + base, 16), :]
            for q in range(2):
                at = pl.multiple_of(block * step + h * 16 + q * 8, 8)
                left = [
                    jnp.where(
                        block_mask,
                        jnp.concatenate([turned_ref[c, pl.ds(slot * rays + at, 8), :]] * repeat, 1),
                        0.0,
                    )
                    for c in range(count)
                ]
                left = jnp.concatenate(left, 0).astype(bf16)
                tiles = [
                    jnp.where(
                        jnp.broadcast_to(u16[q * 8 + i : q * 8 + i + 1, :], (samples, width))
                        > negative,
                        one,
                        zero,
                    )
                    for i in range(8)
                ]
                h1 = nn_dot(left, jnp.concatenate(tiles, 0))
                for c in range(count):
                    h1_ref[c, pl.ds(at, 8), :] = h1[c * 8 : c * 8 + 8, :]
        return carry

    lax.fori_loop(0, rays // step, slot_block, 0)


def merge(first, second, forward):
    fc, ft = first
    sc, st = second
    return jnp.where(forward, fc + ft * sc, sc + st * fc), ft * st


def middle_kernel(*refs, owners, slots, rows, lines):
    bits = bits_of(owners)
    seg_ref, refs = refs[0], refs[1:]
    got_refs, refs = refs[:bits], refs[bits:]
    h1_refs, refs = refs[:slots], refs[slots:]
    lines_ref, low_ref, *refs = refs
    keep_ref, send_ref, moved_ref, slot_ref, cot_ref, ray_ref = refs
    me = lax.axis_index("slab")
    outs = seg_ref.shape[0]
    channels = outs - 1
    rays = lines_ref.shape[1]
    width = low_ref.shape[1]
    forward = lines_ref[lines["direction"] : lines["direction"] + 1, :] == 0.0
    target = lines_ref[lines["target"] : lines["target"] + channels, :]

    def pair(values):
        return values[:channels, :], values[channels : channels + 1, :]

    low = high = None
    for b in reversed(range(bits)):
        piece = pair(got_refs[b][...])
        is_low = ((me >> b) & 1) == 1
        piece = (jnp.where(is_low, piece[0], 0.0), jnp.where(is_low, piece[1], 1.0))
        low = piece if low is None else merge(low, piece, forward)
    for b in range(bits):
        piece = pair(got_refs[b][...])
        is_high = ((me >> b) & 1) == 0
        piece = (jnp.where(is_high, piece[0], 0.0), jnp.where(is_high, piece[1], 1.0))
        high = piece if high is None else merge(high, piece, forward)
    seg_color, seg_trans = pair(seg_ref[...])
    before_color = jnp.where(forward, low[0], high[0])
    before_trans = jnp.where(forward, low[1], high[1])
    after_color = jnp.where(forward, high[0], low[0])
    color = before_color + before_trans * (seg_color + seg_trans * after_color)
    residual = color - target
    color_cot = before_trans * residual
    trans_cot = -before_trans * jnp.sum(after_color * residual, 0, keepdims=True)
    cot_ref[:channels, :] = color_cot
    cot_ref[channels:outs, :] = trans_cot
    cot_ref[outs : outs + channels, :] = color
    cot_ref[outs + channels :, :] = jnp.zeros((8 - outs - channels, rays), f32)
    w_out = low_ref[rows["w_out"], :].astype(f32)
    w_rows = [w_out[c : c + 1, :] for c in range(outs)]
    w = low_ref[rows["w"], :]
    chunk = 128
    for n in range(rays // chunk):
        these = slice(n * chunk, (n + 1) * chunk)
        turned = cot_ref[:, these].T
        cots = [jnp.broadcast_to(turned[:, c : c + 1], (chunk, width)) for c in range(outs)]
        whole = None
        for k in range(slots):
            at = slice(k * rays + n * chunk, k * rays + (n + 1) * chunk)
            h1_ref = h1_refs[k]
            parts = [sum(cots[c] * h1_ref[c, these, :] for c in range(outs))]
            parts += [cots[c] * h1_ref[outs + c, these, :] for c in range(channels)]
            grad = sum(w_rows[c] * parts[c] for c in range(outs))
            slot_ref[at, :] = grad
            whole = grad if whole is None else whole + grad
            moved_ref[at, :] = split_dot(grad, w, nt_dot)
    own = rays // owners
    moved = moved_ref[:rays, :]
    for k in range(1, slots):
        moved = moved + moved_ref[k * rays : (k + 1) * rays, :]
    ray_ref[...] = moved
    for i, t in enumerate(halving_order(owners)):
        place = pl.multiple_of((me ^ t) * own, own)
        if i < owners // 2:
            keep_ref[i * own : (i + 1) * own, :] = ray_ref[pl.ds(place, own), :]
        else:
            at = i * own - rays // 2
            send_ref[at : at + own, :] = ray_ref[pl.ds(place, own), :].astype(bf16)


def brick_kernel(lines_ref, moved_ref, keep_ref, send_ref, *, shares):
    share = lax.axis_index("ray")
    rays = lines_ref.shape[1]
    total, width = moved_ref.shape
    slots = total // rays
    half = keep_ref.shape[0]
    part = 2 * half // shares
    moved = moved_ref[...]
    high = moved.astype(bf16)
    low = (moved - high.astype(f32)).astype(bf16)
    row = lax.broadcasted_iota(jnp.int32, (part, rays), 0).astype(f32)
    for i, t in enumerate(halving_order(shares)):
        first = ((share ^ t) * part).astype(f32)
        acc = jnp.zeros((part, width), f32)
        for k in range(slots):
            one_hot = jnp.where(row + first == lines_ref[k : k + 1, :], 1.0, 0.0).astype(bf16)
            rows = slice(k * rays, (k + 1) * rays)
            acc = acc + nn_dot(one_hot, high[rows]) + nn_dot(one_hot, low[rows])
        ref, at = (keep_ref, i * part) if i < shares // 2 else (send_ref, i * part - half)
        ref[at : at + part, :] = acc


def sample_kernel(
    cot_ref, coef_ref, u_ref, s_ref, low_ref, by_sample_ref, sums_ref, bias_ref, g_ref, *, first, rows
):
    outs = sums_ref.shape[0]
    channels = outs - 1
    rays = cot_ref.shape[1]
    total, width = u_ref.shape
    samples = by_sample_ref.shape[0]
    bias_sums = [jnp.zeros((1, 128), f32)] * outs
    for n in range(total // 128):
        lanes = slice(n * 128, n * 128 + 128)
        at = (n * 128) % rays
        cots = [cot_ref[c : c + 1, at : at + 128] for c in range(outs)]
        grads = [sum(cots[c] * coef_ref[c, first : first + samples, lanes] for c in range(outs))]
        for c in range(channels):
            grads.append(cots[c] * coef_ref[outs + c, first : first + samples, lanes])
        for c in range(outs):
            bias_sums[c] = bias_sums[c] + jnp.sum(grads[c], 0, keepdims=True)
        for j in range(0, samples, 8):
            g_ref[j // 8, :, lanes] = jnp.concatenate([g[j : j + 8] for g in grads], 0).astype(bf16)
    w_out = low_ref[rows["w_out"], :].astype(f32)
    w_rows = [w_out[c : c + 1, :] for c in range(outs)]
    row8 = lax.broadcasted_iota(jnp.int32, (8, width), 0)

    def sample_block(block, sums):
        left = g_ref[block]
        s8 = s_ref[pl.ds(pl.multiple_of(first + block * 8, 8), 8), :]
        acc = [jnp.zeros((8, width), f32)] * outs
        for i in range(0, 8, 2):
            edges = [(-s8[i + h : i + h + 1, :]).astype(bf16) for h in range(2)]
            h2 = None
            for n in range(total // 256):
                u = u_ref[n * 256 : n * 256 + 256, :]
                live = [
                    jnp.where(
                        u > jnp.broadcast_to(edge, u.shape),
                        jnp.ones(u.shape, bf16),
                        jnp.zeros(u.shape, bf16),
                    )
                    for edge in edges
                ]
                term = nn_dot(left[:, n * 256 : n * 256 + 256], jnp.concatenate(live, 1))
                h2 = term if h2 is None else h2 + term
            for c in range(outs):
                for h in range(2):
                    piece = h2[c * 8 : c * 8 + 8, h * width : (h + 1) * width]
                    acc[c] = acc[c] + jnp.where(row8 == i + h, piece, 0.0)
        by_sample_ref[pl.ds(pl.multiple_of(block * 8, 8), 8), :] = sum(
            w_rows[c] * acc[c] for c in range(outs)
        )
        return tuple(sums[c] + s8 * acc[c] for c in range(outs))

    sums = [jnp.zeros((8, width), f32)] * outs
    sums = lax.fori_loop(0, samples // 8, sample_block, tuple(sums), unroll=2)
    for c in range(outs):
        sums_ref[c] = sums[c]
        bias_ref[c : c + 1, :] = bias_sums[c]


def network_kernel(*refs, parts, slots, rows, owners):
    part_refs, refs = refs[: 3 * parts], refs[3 * parts :]
    h1_refs, refs = refs[:slots], refs[slots:]
    cot_ref, u_ref, slot_ref, chosen_ref, sorted_ref, low_ref, small_ref, color_ref = refs
    by_sample = jnp.concatenate([part_refs[3 * i][...] for i in range(parts)], 0)
    samples, width = by_sample.shape
    rays = sorted_ref.shape[0]
    outs = color_ref.shape[0] + 1
    channels = outs - 1
    own = rays // owners
    me = lax.axis_index("slab")
    r_i = lax.broadcasted_iota(jnp.int32, (rays, own), 0)
    c_i = lax.broadcasted_iota(jnp.int32, (rays, own), 1)
    pick = jnp.where(r_i == c_i + me * own, 1.0, 0.0).astype(f32)
    color_ref[...] = nn_dot(cot_ref[outs : outs + channels, :], pick, exact)
    sums = [jnp.zeros((8, width), f32)] * outs
    chunk = 128
    for n in range(rays // chunk):
        these = slice(n * chunk, (n + 1) * chunk)
        turned = cot_ref[:, these].T
        cots = [jnp.broadcast_to(turned[:, c : c + 1], (chunk, width)) for c in range(outs)]
        for k in range(slots):
            u = u_ref[k * rays + n * chunk : k * rays + (n + 1) * chunk, :].astype(f32)
            h1_ref = h1_refs[k]
            products = [sum(cots[c] * h1_ref[c, these, :] for c in range(outs))]
            products += [cots[c] * h1_ref[outs + c, these, :] for c in range(channels)]
            for c in range(outs):
                sums[c] = sums[c] + jnp.sum((u * products[c]).reshape(chunk // 8, 8, width), 0)
    w = low_ref[rows["w"], :]
    sample = low_ref[rows["sample"], :].astype(f32)
    slot = slot_ref[...]
    slot_ray = slot[:rays, :]
    for k in range(1, slots):
        slot_ray = slot_ray + slot[k * rays : (k + 1) * rays, :]
    ray_t = sorted_ref[...].astype(f32).T.astype(bf16)
    sample_t = jnp.concatenate([sample] * (128 // samples), 0).T[:, :samples]

    def flipped(a, b):
        return nn_dot(b, a)

    small_ref[:samples, :] = split_dot(by_sample, w, nt_dot)
    small_ref[samples : samples + width, :] = (
        split_dot(slot, chosen_ref[...], flipped)
        + split_dot(slot_ray, ray_t, flipped)
        + split_dot(by_sample, sample_t.astype(bf16), flipped)
    )
    at = samples + width
    small_ref[at : at + 1, :] = jnp.sum(by_sample, 0, keepdims=True)
    lane128 = lax.broadcasted_iota(jnp.int32, (1, 128), 1)
    bias = jnp.zeros((1, 128), f32)
    for c in range(outs):
        total = sums[c] + sum(part_refs[3 * i + 1][c] for i in range(parts))
        small_ref[at + 1 + c : at + 2 + c, :] = jnp.sum(total, 0, keepdims=True)
        row = sum(part_refs[3 * i + 2][c : c + 1, :] for i in range(parts))
        bias = bias + jnp.where(lane128 == c, jnp.sum(row, 1, keepdims=True), 0.0)
    small_ref[at + 1 + outs : at + 2 + outs, :] = bias
    rest = small_ref.shape[0] - (at + 2 + outs)
    small_ref[at + 2 + outs :, :] = jnp.zeros((rest, width), f32)


def finish_kernel(
    ray_ref,
    ray_got_ref,
    brick_ref,
    sent_ref,
    got_ref,
    ray_out_ref,
    brick_out_ref,
    sample_ref,
    w_ref,
    b_ref,
    w_out_ref,
    b_out_ref,
):
    ray_out_ref[...] = ray_ref[...] + ray_got_ref[...].astype(f32)
    part = brick_ref.shape[0]
    brick_out_ref[...] = brick_ref[...] + got_ref[:part, :].astype(f32)
    small = sent_ref[part:, :].astype(f32) + got_ref[part:, :].astype(f32)
    samples, width = sample_ref.shape
    outs = w_out_ref.shape[0]
    at = samples + width
    sample_ref[...] = small[:samples]
    w_ref[...] = small[samples:at]
    b_ref[...] = small[at : at + 1]
    w_out_ref[...] = small[at + 1 : at + 1 + outs]
    b_out_ref[...] = small[at + 1 + outs : at + 2 + outs, :outs]


def body(
    ray_code,
    direction,
    target,
    brick_code,
    sample_code,
    w_hidden,
    b_hidden,
    w_out,
    b_out,
    brick_ids,
    occupancy,
):
    owners = lax.axis_size("slab")
    shares = lax.axis_size("ray")
    me = lax.axis_index("slab")
    ids = brick_ids[0]
    slots, rays = ids.shape
    total = slots * rays
    bricks, width = brick_code.shape[1:]
    samples = sample_code.shape[1]
    outs = w_out.shape[1]
    channels = outs - 1
    count = outs + channels

    def shaped(*shape):
        return jax.ShapeDtypeStruct(shape, f32)

    def shaped16(*shape):
        return jax.ShapeDtypeStruct(shape, bf16)

    rows = low_rows(width, samples)
    lines = line_rows(slots, channels)
    brick_t, gathered = call(
        turn_kernel,
        (shaped16(width, bricks), shaped16(*ray_code.shape)),
        "turn",
        flops=1 << 34,
    )(brick_code[0], ray_code)
    low, packed, w_t, s, wide, left, chosen, project = call(
        functools.partial(prepare_kernel, rows=rows, lines=lines),
        (
            shaped16(rows["w_out"].stop, width),
            shaped(lines["b_out"] + 1, rays),
            shaped16(width, width),
            shaped(samples, width),
            shaped16(samples, width, 128),
            shaped16(outs * 8, 8 * width),
            shaped16(width, total),
            shaped(width, total),
        ),
        "prepare",
        flops=1 << 31,
    )(
        brick_t,
        w_hidden[0],
        sample_code[0],
        w_out[0],
        ids,
        occupancy,
        direction[None],
        target,
        b_hidden,
        b_out,
    )
    other = swap(ray_code, "slab", owners, 1)
    for b in range(1, bits_of(owners)):
        gathered = jnp.concatenate([gathered, other], 0)
        other = swap(gathered, "slab", owners, 1 << b)
    passes = ()
    for second, part in enumerate((gathered, other)):
        wide_rays = rays if second else rays // 2
        passes = call(
            functools.partial(forward_kernel, owners=owners, second=second, lines=lines),
            (
                shaped(outs, wide_rays),
                shaped(2 * outs, samples, slots * wide_rays),
                shaped16(slots * wide_rays, width),
                shaped16(wide_rays, width),
            ),
            "forward",
            scratch=(
                pltpu.VMEM((rays // 2, width), bf16),
                pltpu.VMEM((width, total // 2), bf16),
                pltpu.VMEM((outs, samples, total // 2), f32),
            ),
            flops=1 << 30,
        )(part, project, w_t, wide, left, packed, *passes)
    seg, kept, u, ray_sorted = passes

    coef, turned = call(
        coefficient_kernel,
        (shaped(count, samples, total), shaped(count, total, 128)),
        "coefficients",
        flops=1 << 31,
    )(seg, kept)
    basis = [
        call(
            functools.partial(basis_kernel, slot=k),
            shaped(count, rays, width),
            "basis",
            flops=1 << 31,
        )(turned, u, s)
        for k in range(slots)
    ]

    forward = packed[lines["direction"]][None] == 0.0
    group = (seg[:channels], seg[channels:])
    received = []
    for b in range(bits_of(owners)):
        sent = jnp.concatenate(group, 0) if b > 0 else seg
        other = swap(sent, "slab", owners, 1 << b)
        received.append(other)
        theirs = (other[:channels], other[channels:])
        upper = ((me >> b) & 1) == 1
        first = jax.tree.map(lambda a, b: jnp.where(upper, b, a), group, theirs)
        second = jax.tree.map(lambda a, b: jnp.where(upper, a, b), group, theirs)
        group = merge(first, second, forward)

    ray_keep, ray_send, moved, slot_grad, cots = call(
        functools.partial(middle_kernel, owners=owners, slots=slots, rows=rows, lines=lines),
        (
            shaped(rays // 2, width),
            shaped16(rays // 2, width),
            shaped(total, width),
            shaped(total, width),
            shaped(8, rays),
        ),
        "middle",
        scratch=(pltpu.VMEM((rays, width), f32),),
        flops=1 << 31,
    )(seg, *received, *basis, packed, low)
    def merged(keep, got):
        half = keep.shape[0] // 2
        return keep[:half] + got[:half].astype(f32), (keep[half:] + got[half:].astype(f32)).astype(bf16)

    def part_by_sample(i, cots):
        return call(
            functools.partial(sample_kernel, first=i * samples // parts, rows=rows),
            (
                shaped(samples // parts, width),
                shaped(outs, 8, width),
                shaped(outs, 128),
            ),
            "by_sample",
            scratch=(pltpu.VMEM((samples // parts // 8, outs * 8, total), bf16),),
            flops=1 << 28,
        )(cots, coef, u, s, low)

    parts = 2
    by_part = []
    later_cots = cots
    for b in range(bits_of(owners)):
        ray_got = swap(ray_send, "slab", owners, 1 << b)
        if b < parts:
            by_part += part_by_sample(b, later_cots)
        if b + 1 < bits_of(owners):
            ray_got, later_cots, moved = lax.optimization_barrier((ray_got, later_cots, moved))
            ray_keep, ray_send = merged(ray_keep, ray_got)
    brick_keep, brick_send = call(
        functools.partial(brick_kernel, shares=shares),
        (shaped(bricks // 2, width), shaped(bricks // 2, width)),
        "bricks",
        flops=1 << 28,
    )(packed, moved)
    small_rows = -(-(samples + width + 2 + outs) // 16) * 16
    small, color_own = call(
        functools.partial(network_kernel, parts=parts, slots=slots, rows=rows, owners=owners),
        (shaped(small_rows, width), shaped(channels, rays // owners)),
        "network",
        flops=1 << 28,
    )(*by_part, *basis, cots, u, slot_grad, chosen, ray_sorted, low)

    brick = brick_keep + swap(brick_send, "ray", shares, 1)
    small = small + swap(small, "ray", shares, 1)
    for b in range(1, bits_of(shares)):
        half = brick.shape[0] // 2
        sent = jnp.concatenate([brick[half:], small], 0).astype(bf16)
        other = swap(sent, "ray", shares, 1 << b)
        brick = brick[:half]
        if b + 1 < bits_of(shares):
            brick = brick + other[:half].astype(f32)
            small = sent[half:].astype(f32) + other[half:].astype(f32)
    ray_out, brick_out, sample_out, w_grad, b_grad, w_out_grad, b_out_grad = call(
        finish_kernel,
        (
            shaped(rays // owners, width),
            shaped(bricks // shares, width),
            shaped(samples, width),
            shaped(width, width),
            shaped(1, width),
            shaped(outs, width),
            shaped(1, outs),
        ),
        "finish",
    )(ray_keep, ray_got, brick, sent, other)
    return (
        color_own,
        ray_out,
        brick_out[None],
        sample_out[None],
        w_grad[None],
        b_grad,
        w_out_grad[None],
        b_out_grad,
    )


def solution(mesh):
    in_specs = (
        P(("ray", "slab"), None),
        P("ray"),
        P(None, "ray"),
        P("slab", None, None),
        P("slab", None, None),
        P("slab", None, None),
        P("slab", None),
        P("slab", None, None),
        P("slab", None),
        P("slab", None, "ray"),
        P("slab", "ray"),
    )
    out_specs = (
        P(None, ("ray", "slab")),
        P(("ray", "slab"), None),
        P("slab", "ray", None),
        P("slab", None, None),
        P("slab", None, None),
        P("slab", None),
        P("slab", None, None),
        P("slab", None),
    )
    return jax.shard_map(body, mesh=mesh, in_specs=in_specs, out_specs=out_specs, check_vma=False)
```

```python
import functools

import jax
import jax.numpy as jnp
from jax import lax
from jax.experimental import pallas as pl
from jax.experimental.pallas import tpu as pltpu
from jax.sharding import PartitionSpec as P

step_length = 0.002
f32 = jnp.float32
bf16 = jnp.bfloat16
vmem_bytes = 24 * 1024 * 1024
exact = lax.Precision.HIGHEST


def bits_of(count):
    bits = count.bit_length() - 1
    assert count == 1 << bits
    return bits


def gather_bits(owners, own):
    last = max(bits_of(128 // own), 0) if own < 128 else 0
    return [b for b in reversed(range(bits_of(owners))) if b != last] + [last]


def gather_order(owners, own):
    order = [0]
    for b in gather_bits(owners, own)[:-1]:
        order = order + [t ^ (1 << b) for t in order]
    return order


def split_dot(a, b, dot):
    high = a.astype(bf16)
    low = (a - high.astype(f32)).astype(bf16)
    return dot(high, b) + dot(low, b)


def nt_dot(a, b, precision=None):
    return lax.dot_general(
        a, b, (((1,), (1,)), ((), ())), precision=precision, preferred_element_type=f32
    )


def nn_dot(a, b, precision=None):
    return jnp.dot(a, b, precision=precision, preferred_element_type=f32)


def swap(array, axis, size, distance):
    return lax.ppermute(array, axis, [(i, i ^ distance) for i in range(size)])


def sum_dot(ones, b):
    high = b.astype(bf16)
    low = (b - high.astype(f32)).astype(bf16)
    return nn_dot(ones, high) + nn_dot(ones, low)


def call(kernel, out_shape, name, scratch=(), flops=0):
    def run(*operands):
        return pl.pallas_call(
            kernel,
            out_shape=out_shape,
            in_specs=[pl.BlockSpec(memory_space=pltpu.VMEM)] * len(operands),
            out_specs=jax.tree.map(lambda _: pl.BlockSpec(memory_space=pltpu.VMEM), out_shape),
            scratch_shapes=list(scratch),
            compiler_params=pltpu.CompilerParams(vmem_limit_bytes=vmem_bytes),
            cost_estimate=pl.CostEstimate(flops=flops, bytes_accessed=1 << 20, transcendentals=0),
            name=name,
        )(*operands)

    return run


def low_rows(width, samples):
    starts = {"w": 0, "sample": width, "w_out": width + samples}
    sizes = {"w": width, "sample": samples, "w_out": 16}
    return {name: slice(at, at + sizes[name]) for name, at in starts.items()}


def line_rows(slots, channels):
    return {
        "ids": 0,
        "occ": slots,
        "direction": slots + 1,
        "target": slots + 2,
        "b_out": slots + 2 + channels,
    }


def order_kernel(earlier_ref, later_ref):
    shape = earlier_ref.shape
    r_i = lax.broadcasted_iota(jnp.int32, shape, 0)
    c_i = lax.broadcasted_iota(jnp.int32, shape, 1)
    earlier_ref[...] = jnp.where(c_i < r_i, 1.0, 0.0).astype(bf16)
    later_ref[...] = jnp.where(c_i > r_i, 1.0, 0.0).astype(bf16)


def chosen_kernel(lines_ref, brick_ref, w_t_ref, chosen_ref, project_ref):
    total = chosen_ref.shape[1]
    rays = lines_ref.shape[1]
    bricks = brick_ref.shape[0]
    brick_t = brick_ref[...].astype(f32).T.astype(bf16)
    w_t = w_t_ref[...]
    row = lax.broadcasted_iota(jnp.int32, (bricks, rays), 0).astype(f32)
    for k in range(total // rays):
        one_hot = jnp.where(row == lines_ref[k : k + 1, :], 1.0, 0.0).astype(bf16)
        chosen = nn_dot(brick_t, one_hot).astype(bf16)
        chosen_ref[:, k * rays : (k + 1) * rays] = chosen
        project_ref[:, k * rays : (k + 1) * rays] = nn_dot(w_t, chosen)


def prepare_kernel(
    ray_ref,
    w_ref,
    sample_ref,
    w_out_ref,
    ids_ref,
    occ_ref,
    direction_ref,
    target_ref,
    b_ref,
    b_out_ref,
    own_ref,
    low_ref,
    lines_ref,
    w_t_ref,
    s_ref,
    wide_ref,
    left_ref,
    *,
    rows,
    lines,
):
    slots, rays = ids_ref.shape
    width = w_t_ref.shape[0]
    samples = s_ref.shape[0]
    outs = w_out_ref.shape[0]
    own_ref[...] = ray_ref[...]
    w = w_ref[...]
    w_out = w_out_ref[...].astype(f32)
    low_ref[rows["w"], :] = w
    low_ref[rows["sample"], :] = sample_ref[...]
    low_ref[rows["w_out"], :] = jnp.concatenate(
        [w_out, jnp.zeros((16 - outs, width), f32)], 0
    ).astype(bf16)
    lines_ref[:slots, :] = ids_ref[...].astype(f32)
    lines_ref[lines["occ"] : lines["occ"] + 1, :] = occ_ref[...].astype(f32)
    lines_ref[lines["direction"] : lines["direction"] + 1, :] = direction_ref[...].astype(f32)
    lines_ref[lines["target"] : lines["target"] + outs - 1, :] = target_ref[...]
    lines_ref[lines["b_out"] : lines["b_out"] + 1, :outs] = b_out_ref[...]
    w_t = w.astype(f32).T.astype(bf16)
    w_t_ref[...] = w_t
    s = nn_dot(sample_ref[...], w) + b_ref[...]
    s_ref[...] = s.astype(bf16).astype(f32)
    s_t = jnp.concatenate([s] * (128 // samples), 0).T
    for j in range(samples):
        wide_ref[j] = jnp.broadcast_to(s_t[:, j : j + 1], (width, 128)).astype(bf16)
    w_rows = jnp.concatenate(
        [jnp.broadcast_to(w_out[c : c + 1, :], (8, width)) for c in range(outs)], 0
    )
    row8 = lax.broadcasted_iota(jnp.int32, (outs * 8, width), 0) % 8
    for i in range(8):
        left_ref[:, i * width : (i + 1) * width] = jnp.where(row8 == i, w_rows, 0.0).astype(bf16)


def forward_kernel(*refs, owners, second, lines):
    ray_ref, project_ref, w_t_ref, wide_ref, left_ref, lines_ref, earlier_ref, *refs = refs
    if second:
        before_refs, refs = refs[:3], refs[3:]
    seg_ref, kept_ref, u_ref, sorted_ref, order_ref, ut_ref, raw_ref = refs
    width, total = project_ref.shape
    samples = wide_ref.shape[0]
    outs = seg_ref.shape[0]
    half, rays = ray_ref.shape[0], lines_ref.shape[1]
    slots = total // rays
    chunk = 128
    own = 2 * half // owners
    last = gather_bits(owners, own)[-1]
    me = lax.axis_index("slab")
    side = (me >> last) & 1

    def whole(n, k=0, side=side):
        return pl.ds(pl.multiple_of(k * rays + (2 * n + side) * chunk, chunk), chunk)

    if second:
        for n in range(half // chunk):
            part = slice(n * chunk, (n + 1) * chunk)
            seg_ref[:, whole(n)] = before_refs[0][:, part]
            sorted_ref[whole(n), :] = before_refs[2][part, :]
            for k in range(slots):
                u_ref[whole(n, k), :] = before_refs[1][k * half + n * chunk : k * half + (n + 1) * chunk, :]
        side = 1 - side

    def spot(n, k=0):
        at = k * half + n * chunk
        return whole(n, k, side) if second else slice(at, at + chunk)

    flip = (1 << last) if second else 0
    for i, t in enumerate(gather_order(owners, own)):
        owner = me ^ (t ^ flip)
        place = ((owner >> (last + 1)) << last) | (owner & ((1 << last) - 1))
        order_ref[pl.ds(pl.multiple_of(place * own, own), own), :] = ray_ref[
            i * own : (i + 1) * own, :
        ]
    ray_t = nt_dot(w_t_ref[...], order_ref[...])
    for n in range(half // chunk):
        sorted_ref[spot(n), :] = order_ref[n * chunk : (n + 1) * chunk, :]
        for k in range(slots):
            part = project_ref[:, whole(n, k, side)] + ray_t[:, n * chunk : (n + 1) * chunk]
            part = part.astype(bf16)
            ut_ref[:, k * half + n * chunk : k * half + (n + 1) * chunk] = part
            u_ref[spot(n, k), :] = part.astype(f32).T.astype(bf16)
    b_out = [lines_ref[lines["b_out"], c] for c in range(outs)]

    def shade_block(block, carry):
        for n in range(slots * half // 256):
            lanes = slice(n * 256, n * 256 + 256)
            ut = ut_ref[:, lanes]
            acc = None
            for i in range(4):
                parts = []
                for h in range(2):
                    column = wide_ref[block * 8 + 2 * i + h]
                    column = jnp.concatenate([column, column], 1)
                    parts.append(jnp.maximum(ut + column, 0))
                left = left_ref[:, 2 * i * width : 2 * (i + 1) * width]
                term = nn_dot(left, jnp.concatenate(parts, 0))
                acc = term if acc is None else acc + term
            for c in range(outs):
                raw_ref[c, pl.ds(pl.multiple_of(block * 8, 8), 8), lanes] = (
                    acc[c * 8 : c * 8 + 8, :] + b_out[c]
                )
        return carry

    lax.fori_loop(0, samples // 8, shade_block, 0, unroll=8)
    earlier = earlier_ref[...]
    occ_row = lines["occ"]
    for n in range(half // chunk):
        occ = lines_ref[occ_row : occ_row + 1, whole(n, 0, side)]
        raws = [
            raw_ref[0, :, k * half + n * chunk : k * half + (n + 1) * chunk] for k in range(slots)
        ]
        occupied = [(k < occ).astype(f32) for k in range(slots)]
        opticals = [
            step_length * (jnp.maximum(x, 0.0) + jnp.log1p(jnp.exp(-jnp.abs(x)))) * o
            for x, o in zip(raws, occupied)
        ]
        enters = sum_dot(earlier, jnp.concatenate(opticals, 1))
        before = jnp.zeros((1, chunk), f32)
        colors = [jnp.zeros((1, chunk), f32)] * (outs - 1)
        for k in range(slots):
            local = slice(k * half + n * chunk, k * half + (n + 1) * chunk)
            optical = opticals[k]
            entered = enters[:, k * chunk : (k + 1) * chunk] + before
            before = before + jnp.sum(optical, 0, keepdims=True)
            tanh = jnp.tanh(0.5 * optical)
            weight = jnp.exp(-entered) * (2.0 * tanh / (1.0 + tanh))
            for c in range(outs - 1):
                shading = jax.nn.sigmoid(raw_ref[c + 1, :, local])
                light = weight * shading
                colors[c] = colors[c] + jnp.sum(light, 0, keepdims=True)
                kept_ref[c, :, local] = shading
                kept_ref[outs + c, :, local] = light
            kept_ref[outs - 1, :, local] = jnp.exp(-(entered + optical))
            kept_ref[2 * outs - 1, :, local] = step_length * occupied[k] * jax.nn.sigmoid(raws[k])
        place = spot(n)
        for c in range(outs - 1):
            seg_ref[c : c + 1, place] = colors[c]
        seg_ref[outs - 1 : outs, place] = jnp.exp(-before)


def coefficient_kernel(seg_ref, first_ref, second_ref, later_ref, coef_ref, turned_ref, *, owners):
    outs, rays = seg_ref.shape
    samples, local = first_ref.shape[1:]
    half = rays // 2
    slots = local // half
    last = gather_bits(owners, rays // owners)[-1]
    side = (lax.axis_index("slab") >> last) & 1
    later = later_ref[...]
    chunk = 128

    def keep(index, lanes, value):
        coef_ref[index, :, lanes] = value
        turned_ref[index, lanes, :] = jnp.concatenate([value] * (128 // samples), 0).T

    for kept_ref, where in ((first_ref, side), (second_ref, 1 - side)):
        for n in range(half // chunk):
            base = (2 * n + where) * chunk
            through = seg_ref[outs - 1 : outs, pl.ds(pl.multiple_of(base, chunk), chunk)]
            after = [jnp.zeros((1, chunk), f32)] * (outs - 1)
            for k in reversed(range(slots)):
                lanes = pl.ds(pl.multiple_of(k * rays + base, chunk), chunk)
                at = slice(k * half + n * chunk, k * half + (n + 1) * chunk)
                passed = kept_ref[outs - 1, :, at]
                density = kept_ref[2 * outs - 1, :, at]
                lights = [kept_ref[outs + c, :, at] for c in range(outs - 1)]
                behinds = sum_dot(later, jnp.concatenate(lights, 1))
                for c in range(outs - 1):
                    shading = kept_ref[c, :, at]
                    light = lights[c]
                    behind = behinds[:, c * chunk : (c + 1) * chunk] + after[c]
                    after[c] = after[c] + jnp.sum(light, 0, keepdims=True)
                    keep(c, lanes, density * (shading * passed - behind))
                    keep(outs + c, lanes, light * (1.0 - shading))
                keep(outs - 1, lanes, density * through)


def basis_kernel(turned_ref, u_ref, s_ref, low_ref, h1_ref, moved_ref, *, first, row_of):
    count, rays, width = h1_ref.shape
    samples = s_ref.shape[0]
    negative = (-s_ref[...]).astype(bf16)
    one = jnp.ones((samples, width), bf16)
    zero = jnp.zeros((samples, width), bf16)
    lane = lax.broadcasted_iota(jnp.int32, (8, 8 * samples), 1) // samples
    row = lax.broadcasted_iota(jnp.int32, (8, 8 * samples), 0)
    block_mask = lane == row
    repeat = 8 * samples // 128
    step = 128
    outs = moved_ref.shape[0]
    w = low_ref[row_of["w"], :]
    w_out = low_ref[row_of["w_out"], :].astype(f32)
    w_rows = [w_out[c : c + 1, :] for c in range(outs)]

    def slot_block(block, carry):
        for h in range(step // 16):
            base = pl.multiple_of(block * step + h * 16, 16)
            u16 = u_ref[pl.ds(first + base, 16), :]
            for q in range(2):
                at = pl.multiple_of(block * step + h * 16 + q * 8, 8)
                left = [
                    jnp.where(
                        block_mask,
                        jnp.concatenate([turned_ref[c, pl.ds(first + at, 8), :]] * repeat, 1),
                        0.0,
                    )
                    for c in range(count)
                ]
                left = jnp.concatenate(left, 0).astype(bf16)
                tiles = [
                    jnp.where(
                        jnp.broadcast_to(u16[q * 8 + i : q * 8 + i + 1, :], (samples, width))
                        > negative,
                        one,
                        zero,
                    )
                    for i in range(8)
                ]
                h1 = nn_dot(left, jnp.concatenate(tiles, 0))
                for c in range(count):
                    h1_ref[c, pl.ds(at, 8), :] = h1[c * 8 : c * 8 + 8, :]
        return carry

    lax.fori_loop(0, rays // step, slot_block, 0)
    for c in range(outs):
        grad = w_rows[0] * h1_ref[c]
        if c + 1 < outs:
            grad = grad + w_rows[c + 1] * h1_ref[outs + c]
        moved_ref[c] = nt_dot(grad.astype(bf16), w)


def merge(first, second, forward):
    fc, ft = first
    sc, st = second
    return jnp.where(forward, fc + ft * sc, sc + st * fc), ft * st


def middle_kernel(*refs, owners, pieces, lines):
    bits = bits_of(owners)
    seg_ref, refs = refs[0], refs[1:]
    got_refs, refs = refs[:bits], refs[bits:]
    moved_refs, refs = refs[:pieces], refs[pieces:]
    lines_ref, keep_ref, send_ref, cot_ref, ray_ref = refs
    me = lax.axis_index("slab")
    outs = seg_ref.shape[0]
    channels = outs - 1
    rays = lines_ref.shape[1]
    span, width = moved_refs[0].shape[1:]
    slots = pieces * span // rays
    forward = lines_ref[lines["direction"] : lines["direction"] + 1, :] == 0.0
    target = lines_ref[lines["target"] : lines["target"] + channels, :]

    def pair(values):
        return values[:channels, :], values[channels : channels + 1, :]

    low = high = None
    for b in reversed(range(bits)):
        piece = pair(got_refs[b][...])
        is_low = ((me >> b) & 1) == 1
        piece = (jnp.where(is_low, piece[0], 0.0), jnp.where(is_low, piece[1], 1.0))
        low = piece if low is None else merge(low, piece, forward)
    for b in range(bits):
        piece = pair(got_refs[b][...])
        is_high = ((me >> b) & 1) == 0
        piece = (jnp.where(is_high, piece[0], 0.0), jnp.where(is_high, piece[1], 1.0))
        high = piece if high is None else merge(high, piece, forward)
    seg_color, seg_trans = pair(seg_ref[...])
    before_color = jnp.where(forward, low[0], high[0])
    before_trans = jnp.where(forward, low[1], high[1])
    after_color = jnp.where(forward, high[0], low[0])
    color = before_color + before_trans * (seg_color + seg_trans * after_color)
    residual = color - target
    color_cot = before_trans * residual
    trans_cot = -before_trans * jnp.sum(after_color * residual, 0, keepdims=True)
    cot_ref[:channels, :] = color_cot
    cot_ref[channels:outs, :] = trans_cot
    cot_ref[outs : outs + channels, :] = color
    cot_ref[outs + channels :, :] = jnp.zeros((8 - outs - channels, rays), f32)
    chunk = 128
    for n in range(rays // chunk):
        these = slice(n * chunk, (n + 1) * chunk)
        turned = cot_ref[:, these].T
        grad = None
        for c in range(outs):
            whole = None
            for k in range(slots):
                at = k * rays + n * chunk
                part = moved_refs[at // span][c, at % span : at % span + chunk, :]
                whole = part if whole is None else whole + part
            term = jnp.broadcast_to(turned[:, c : c + 1], (chunk, width)) * whole
            grad = term if grad is None else grad + term
        ray_ref[these, :] = grad
    own = rays // owners
    for i in range(owners):
        place = pl.multiple_of((me ^ i) * own, own)
        if i < owners // 2:
            keep_ref[i * own : (i + 1) * own, :] = ray_ref[pl.ds(place, own), :]
        else:
            at = i * own - rays // 2
            send_ref[at : at + own, :] = ray_ref[pl.ds(place, own), :].astype(bf16)


def brick_kernel(lines_ref, moved_ref, keep_ref, send_ref, *, shares):
    share = lax.axis_index("ray")
    rays = lines_ref.shape[1]
    total, width = moved_ref.shape
    slots = total // rays
    half = keep_ref.shape[0]
    part = 2 * half // shares
    moved = moved_ref[...].astype(bf16)
    row = lax.broadcasted_iota(jnp.int32, (part, rays), 0).astype(f32)
    for i in range(shares):
        first = ((share ^ i) * part).astype(f32)
        acc = jnp.zeros((part, width), f32)
        for k in range(slots):
            one_hot = jnp.where(row + first == lines_ref[k : k + 1, :], 1.0, 0.0).astype(bf16)
            rows = slice(k * rays, (k + 1) * rays)
            acc = acc + nn_dot(one_hot, moved[rows])
        ref, at = (keep_ref, i * part) if i < shares // 2 else (send_ref, i * part - half)
        ref[at : at + part, :] = acc


def sample_kernel(
    cot_ref, coef_ref, u_ref, s_ref, low_ref, by_sample_ref, sums_ref, bias_ref, g_ref, *, first, rows
):
    outs = sums_ref.shape[0]
    channels = outs - 1
    rays = cot_ref.shape[1]
    total, width = u_ref.shape
    samples = by_sample_ref.shape[0]
    bias_sums = [jnp.zeros((1, 128), f32)] * outs
    for n in range(total // 128):
        lanes = slice(n * 128, n * 128 + 128)
        at = (n * 128) % rays
        cots = [cot_ref[c : c + 1, at : at + 128] for c in range(outs)]
        grads = [sum(cots[c] * coef_ref[c, first : first + samples, lanes] for c in range(outs))]
        for c in range(channels):
            grads.append(cots[c] * coef_ref[outs + c, first : first + samples, lanes])
        for c in range(outs):
            bias_sums[c] = bias_sums[c] + jnp.sum(grads[c], 0, keepdims=True)
        for j in range(0, samples, 8):
            g_ref[j // 8, :, lanes] = jnp.concatenate([g[j : j + 8] for g in grads], 0).astype(bf16)
    w_out = low_ref[rows["w_out"], :].astype(f32)
    w_rows = [w_out[c : c + 1, :] for c in range(outs)]
    row8 = lax.broadcasted_iota(jnp.int32, (8, width), 0)

    def sample_block(block, sums):
        left = g_ref[block]
        s8 = s_ref[pl.ds(pl.multiple_of(first + block * 8, 8), 8), :]
        acc = [jnp.zeros((8, width), f32)] * outs
        for i in range(0, 8, 2):
            edges = [(-s8[i + h : i + h + 1, :]).astype(bf16) for h in range(2)]
            h2 = None
            for n in range(total // 256):
                u = u_ref[n * 256 : n * 256 + 256, :]
                live = [
                    jnp.where(
                        u > jnp.broadcast_to(edge, u.shape),
                        jnp.ones(u.shape, bf16),
                        jnp.zeros(u.shape, bf16),
                    )
                    for edge in edges
                ]
                term = nn_dot(left[:, n * 256 : n * 256 + 256], jnp.concatenate(live, 1))
                h2 = term if h2 is None else h2 + term
            for c in range(outs):
                for h in range(2):
                    piece = h2[c * 8 : c * 8 + 8, h * width : (h + 1) * width]
                    acc[c] = acc[c] + jnp.where(row8 == i + h, piece, 0.0)
        by_sample_ref[pl.ds(pl.multiple_of(block * 8, 8), 8), :] = sum(
            w_rows[c] * acc[c] for c in range(outs)
        )
        return tuple(sums[c] + s8 * acc[c] for c in range(outs))

    sums = [jnp.zeros((8, width), f32)] * outs
    sums = lax.fori_loop(0, samples // 8, sample_block, tuple(sums), unroll=4)
    for c in range(outs):
        sums_ref[c] = sums[c]
        bias_ref[c : c + 1, :] = bias_sums[c]


def slots_kernel(*refs, pieces, rows, owners):
    h1_refs, refs = refs[:pieces], refs[pieces:]
    basis_refs, refs = refs[:pieces], refs[pieces:]
    cot_ref, u_ref, chosen_ref, sorted_ref, low_ref, *refs = refs
    moved_ref, w_grad_ref, sums_ref, color_ref, slot_ref = refs
    rays, width = sorted_ref.shape
    span = h1_refs[0].shape[1]
    slots = pieces * span // rays
    outs = color_ref.shape[0] + 1
    channels = outs - 1
    own = rays // owners
    me = lax.axis_index("slab")
    r_i = lax.broadcasted_iota(jnp.int32, (rays, own), 0)
    c_i = lax.broadcasted_iota(jnp.int32, (rays, own), 1)
    pick = jnp.where(r_i == c_i + me * own, 1.0, 0.0).astype(bf16)
    color = cot_ref[outs : outs + channels, :]
    high = color.astype(bf16)
    middle = (color - high.astype(f32)).astype(bf16)
    low = (color - high.astype(f32) - middle.astype(f32)).astype(bf16)
    picked = nn_dot(jnp.concatenate([high, middle, low], 0), pick)
    color_ref[...] = picked[:channels] + picked[channels : 2 * channels] + picked[2 * channels :]
    w_out = low_ref[rows["w_out"], :].astype(f32)
    w_rows = [w_out[c : c + 1, :] for c in range(outs)]
    sums = [jnp.zeros((8, width), f32)] * outs
    chunk = 32
    for n in range(rays // chunk):
        if n % (128 // chunk) == 0:
            turned = cot_ref[:, n * chunk : n * chunk + 128].T
        at = (n * chunk) % 128
        cots = [
            jnp.broadcast_to(turned[at : at + chunk, c : c + 1], (chunk, width))
            for c in range(outs)
        ]
        for k in range(slots):
            at = k * rays + n * chunk
            u = u_ref[at : at + chunk, :].astype(f32)
            h1_ref, spot = h1_refs[at // span], slice(at % span, at % span + chunk)
            products = [sum(cots[c] * h1_ref[c, spot, :] for c in range(outs))]
            products += [cots[c] * h1_ref[outs + c, spot, :] for c in range(channels)]
            for c in range(outs):
                sums[c] = sums[c] + jnp.sum((u * products[c]).reshape(chunk // 8, 8, width), 0)
            slot_ref[at : at + chunk, :] = sum(w_rows[c] * products[c] for c in range(outs))
            basis_ref = basis_refs[at // span]
            moved_ref[at : at + chunk, :] = sum(cots[c] * basis_ref[c, spot, :] for c in range(outs))
    for c in range(outs):
        sums_ref[c] = sums[c]
    slot = slot_ref[...]
    slot_ray = slot[:rays, :]
    for k in range(1, slots):
        slot_ray = slot_ray + slot[k * rays : (k + 1) * rays, :]
    ray_t = sorted_ref[...].astype(f32).T.astype(bf16)
    w_grad_ref[...] = nn_dot(chosen_ref[...], slot.astype(bf16)) + nn_dot(ray_t, slot_ray.astype(bf16))


def flipped(a, b):
    return nn_dot(b, a)


def network_kernel(*refs, parts, rows):
    part_refs, refs = refs[: 3 * parts], refs[3 * parts :]
    w_grad_ref, sums_ref, low_ref, small_ref = refs
    by_sample = jnp.concatenate([part_refs[3 * i][...] for i in range(parts)], 0)
    samples, width = by_sample.shape
    outs = sums_ref.shape[0]
    w = low_ref[rows["w"], :]
    sample = low_ref[rows["sample"], :].astype(f32)
    sample_t = jnp.concatenate([sample] * (128 // samples), 0).T[:, :samples]
    small_ref[:samples, :] = split_dot(by_sample, w, nt_dot)
    small_ref[samples : samples + width, :] = w_grad_ref[...] + split_dot(
        by_sample, sample_t.astype(bf16), flipped
    )
    at = samples + width
    small_ref[at : at + 1, :] = jnp.sum(by_sample, 0, keepdims=True)
    lane128 = lax.broadcasted_iota(jnp.int32, (1, 128), 1)
    bias = jnp.zeros((1, 128), f32)
    for c in range(outs):
        total = sums_ref[c] + sum(part_refs[3 * i + 1][c] for i in range(parts))
        small_ref[at + 1 + c : at + 2 + c, :] = jnp.sum(total, 0, keepdims=True)
        row = sum(part_refs[3 * i + 2][c : c + 1, :] for i in range(parts))
        bias = bias + jnp.where(lane128 == c, jnp.sum(row, 1, keepdims=True), 0.0)
    small_ref[at + 1 + outs : at + 2 + outs, :] = bias
    rest = small_ref.shape[0] - (at + 2 + outs)
    small_ref[at + 2 + outs :, :] = jnp.zeros((rest, width), f32)


def finish_ray_kernel(keep_ref, got_ref, out_ref):
    out_ref[...] = keep_ref[...] + got_ref[...].astype(f32)


def finish_kernel(
    brick_ref,
    sent_ref,
    got_ref,
    brick_out_ref,
    sample_ref,
    w_ref,
    b_ref,
    w_out_ref,
    b_out_ref,
):
    part = brick_ref.shape[0]
    brick_out_ref[...] = brick_ref[...] + got_ref[:part, :].astype(f32)
    small = sent_ref[part:, :].astype(f32) + got_ref[part:, :].astype(f32)
    samples, width = sample_ref.shape
    outs = w_out_ref.shape[0]
    at = samples + width
    sample_ref[...] = small[:samples]
    w_ref[...] = small[samples:at]
    b_ref[...] = small[at : at + 1]
    w_out_ref[...] = small[at + 1 : at + 1 + outs]
    b_out_ref[...] = small[at + 1 + outs : at + 2 + outs, :outs]


def body(
    ray_code,
    direction,
    target,
    brick_code,
    sample_code,
    w_hidden,
    b_hidden,
    w_out,
    b_out,
    brick_ids,
    occupancy,
):
    owners = lax.axis_size("slab")
    shares = lax.axis_size("ray")
    me = lax.axis_index("slab")
    ids = brick_ids[0]
    slots, rays = ids.shape
    total = slots * rays
    bricks, width = brick_code.shape[1:]
    samples = sample_code.shape[1]
    outs = w_out.shape[1]
    channels = outs - 1
    count = outs + channels

    def shaped(*shape):
        return jax.ShapeDtypeStruct(shape, f32)

    def shaped16(*shape):
        return jax.ShapeDtypeStruct(shape, bf16)

    rows = low_rows(width, samples)
    lines = line_rows(slots, channels)
    earlier, later = call(
        order_kernel,
        (shaped16(samples, samples), shaped16(samples, samples)),
        "order",
        flops=1 << 34,
    )()
    gathered, low, packed, w_t, s, wide, left = call(
        functools.partial(prepare_kernel, rows=rows, lines=lines),
        (
            shaped16(*ray_code.shape),
            shaped16(rows["w_out"].stop, width),
            shaped(lines["b_out"] + 1, rays),
            shaped16(width, width),
            shaped(samples, width),
            shaped16(samples, width, 128),
            shaped16(outs * 8, 8 * width),
        ),
        "prepare",
        flops=1 << 31,
    )(
        ray_code,
        w_hidden[0],
        sample_code[0],
        w_out[0],
        ids,
        occupancy,
        direction[None],
        target,
        b_hidden,
        b_out,
    )
    turns = gather_bits(owners, ray_code.shape[0])
    other = swap(ray_code, "slab", owners, 1 << turns[0])
    other, lines_later = lax.optimization_barrier((other, packed))
    for b in turns[1:]:
        gathered = jnp.concatenate([gathered, other], 0)
        other = swap(gathered, "slab", owners, 1 << b)
    chosen, project = call(
        chosen_kernel,
        (shaped16(width, total), shaped(width, total)),
        "chosen",
        flops=1 << 29,
    )(lines_later, brick_code[0], w_t)
    passes = ()
    kept = []
    for second, part in enumerate((gathered, other)):
        wide_rays = rays if second else rays // 2
        seg, kept_half, *passes = call(
            functools.partial(forward_kernel, owners=owners, second=second, lines=lines),
            (
                shaped(outs, wide_rays),
                shaped(2 * outs, samples, total // 2),
                shaped16(slots * wide_rays, width),
                shaped16(wide_rays, width),
            ),
            "forward",
            scratch=(
                pltpu.VMEM((rays // 2, width), bf16),
                pltpu.VMEM((width, total // 2), bf16),
                pltpu.VMEM((outs, samples, total // 2), f32),
            ),
            flops=1 << 30,
        )(part, project, w_t, wide, left, packed, earlier, *passes)
        passes = (seg, *passes)
        kept.append(kept_half)
    seg, u, ray_sorted = passes

    coef, turned = call(
        functools.partial(coefficient_kernel, owners=owners),
        (shaped(count, samples, total), shaped(count, total, 128)),
        "coefficients",
        flops=1 << 30,
    )(seg, *kept, later)
    forward = packed[lines["direction"]][None] == 0.0
    group = (seg[:channels], seg[channels:])
    received = []
    basis = []
    pieces = 4
    piece = total // pieces
    bits = bits_of(owners)
    turned_later = turned
    for b in range(bits):
        sent = jnp.concatenate(group, 0) if b > 0 else seg
        other = swap(sent, "slab", owners, 1 << b)
        while len(basis) < min(pieces, pieces * (b + 1) // bits):
            basis.append(
                call(
                    functools.partial(basis_kernel, first=len(basis) * piece, row_of=rows),
                    (shaped(count, piece, width), shaped(outs, piece, width)),
                    "basis",
                    flops=1 << 29,
                )(turned_later, u, s, low)
            )
        other, turned_later = lax.optimization_barrier((other, turned_later))
        received.append(other)
        theirs = (other[:channels], other[channels:])
        upper = ((me >> b) & 1) == 1
        first = jax.tree.map(lambda a, b: jnp.where(upper, b, a), group, theirs)
        second = jax.tree.map(lambda a, b: jnp.where(upper, a, b), group, theirs)
        group = merge(first, second, forward)

    h1, moved_basis = zip(*basis)
    ray_keep, ray_send, cots = call(
        functools.partial(middle_kernel, owners=owners, pieces=pieces, lines=lines),
        (
            shaped(rays // 2, width),
            shaped16(rays // 2, width),
            shaped(8, rays),
        ),
        "middle",
        scratch=(pltpu.VMEM((rays, width), f32),),
        flops=1 << 29,
    )(seg, *received, *moved_basis, packed)
    moved, w_grad, sums, color_own = call(
        functools.partial(slots_kernel, pieces=pieces, rows=rows, owners=owners),
        (
            shaped(total, width),
            shaped(width, width),
            shaped(outs, 8, width),
            shaped(channels, rays // owners),
        ),
        "slots",
        scratch=(pltpu.VMEM((total, width), f32),),
        flops=1 << 28,
    )(*h1, *moved_basis, cots, u, chosen, ray_sorted, low)

    def merged(keep, got):
        half = keep.shape[0] // 2
        return keep[:half] + got[:half].astype(f32), (keep[half:] + got[half:].astype(f32)).astype(bf16)

    def part_by_sample(i, cots):
        return call(
            functools.partial(sample_kernel, first=i * samples // parts, rows=rows),
            (
                shaped(samples // parts, width),
                shaped(outs, 8, width),
                shaped(outs, 128),
            ),
            "by_sample",
            scratch=(pltpu.VMEM((samples // parts // 8, outs * 8, total), bf16),),
            flops=1 << 28,
        )(cots, coef, u, s, low)

    parts = 2
    by_part = []
    later_cots = cots
    for b in range(bits):
        if b + 1 == bits:
            brick_keep, brick_send = call(
                functools.partial(brick_kernel, shares=shares),
                (shaped(bricks // 2, width), shaped(bricks // 2, width)),
                "bricks",
                flops=1 << 28,
            )(packed, moved)
            small_rows = -(-(samples + width + 2 + outs) // 16) * 16
            small = call(
                functools.partial(network_kernel, parts=parts, rows=rows),
                shaped(small_rows, width),
                "network",
                flops=1 << 28,
            )(*by_part, w_grad, sums, low)
            held = (ray_send, brick_send, small)
            ray_send, brick_send, small = lax.optimization_barrier(held)
        ray_got = swap(ray_send, "slab", owners, owners >> (b + 1))
        if b < parts:
            by_part += part_by_sample(b, later_cots)
        if b + 1 < bits:
            held = (ray_got, later_cots, moved)
            ray_got, later_cots, moved = lax.optimization_barrier(held)
            ray_keep, ray_send = merged(ray_keep, ray_got)

    brick = brick_keep
    brick_sent = brick_send.astype(bf16)
    for b in reversed(range(bits_of(shares))):
        sent = jnp.concatenate([brick_sent, small.astype(bf16)], 0)
        other = swap(sent, "ray", shares, 1 << b)
        if b > 0:
            half = brick.shape[0]
            small = sent[half:].astype(f32) + other[half:].astype(f32)
            brick_sent = (brick[half // 2 :] + other[half // 2 : half].astype(f32)).astype(bf16)
            brick = brick[: half // 2] + other[: half // 2].astype(f32)
    ray_out = call(finish_ray_kernel, shaped(rays // owners, width), "finish_ray", flops=1 << 31)(
        ray_keep, ray_got
    )
    brick_out, sample_out, w_grad, b_grad, w_out_grad, b_out_grad = call(
        finish_kernel,
        (
            shaped(bricks // shares, width),
            shaped(samples, width),
            shaped(width, width),
            shaped(1, width),
            shaped(outs, width),
            shaped(1, outs),
        ),
        "finish",
    )(brick, sent, other)
    return (
        color_own,
        ray_out,
        brick_out[None],
        sample_out[None],
        w_grad[None],
        b_grad,
        w_out_grad[None],
        b_out_grad,
    )


def solution(mesh):
    in_specs = (
        P(("ray", "slab"), None),
        P("ray"),
        P(None, "ray"),
        P("slab", None, None),
        P("slab", None, None),
        P("slab", None, None),
        P("slab", None),
        P("slab", None, None),
        P("slab", None),
        P("slab", None, "ray"),
        P("slab", "ray"),
    )
    out_specs = (
        P(None, ("ray", "slab")),
        P(("ray", "slab"), None),
        P("slab", "ray", None),
        P("slab", None, None),
        P("slab", None, None),
        P("slab", None),
        P("slab", None, None),
        P("slab", None),
    )
    return jax.shard_map(body, mesh=mesh, in_specs=in_specs, out_specs=out_specs, check_vma=False)
```

```python
import functools

import jax
import jax.numpy as jnp
from jax import lax
from jax.experimental import pallas as pl
from jax.experimental.pallas import tpu as pltpu
from jax.sharding import PartitionSpec as P

step_length = 0.002
f32 = jnp.float32
bf16 = jnp.bfloat16
vmem_bytes = 24 * 1024 * 1024
exact = lax.Precision.HIGHEST


def bits_of(count):
    bits = count.bit_length() - 1
    assert count == 1 << bits
    return bits


def gather_bits(owners, own):
    last = max(bits_of(128 // own), 0) if own < 128 else 0
    return [b for b in reversed(range(bits_of(owners))) if b != last] + [last]


def gather_order(owners, own):
    order = [0]
    for b in gather_bits(owners, own)[:-1]:
        order = order + [t ^ (1 << b) for t in order]
    return order


def halving_bits(owners):
    bits = list(range(bits_of(owners)))
    return bits[1:-1] + bits[:1] + bits[1:][-1:]


def halving_order(owners):
    order = [0]
    for b in reversed(halving_bits(owners)):
        order = order + [t ^ (1 << b) for t in order]
    return order


def split_dot(a, b, dot):
    high = a.astype(bf16)
    low = (a - high.astype(f32)).astype(bf16)
    return dot(high, b) + dot(low, b)


def nt_dot(a, b, precision=None):
    return lax.dot_general(
        a, b, (((1,), (1,)), ((), ())), precision=precision, preferred_element_type=f32
    )


def nn_dot(a, b, precision=None):
    return jnp.dot(a, b, precision=precision, preferred_element_type=f32)


def swap(array, axis, size, distance):
    return lax.ppermute(array, axis, [(i, i ^ distance) for i in range(size)])


def sum_dot(ones, b):
    high = b.astype(bf16)
    low = (b - high.astype(f32)).astype(bf16)
    return nn_dot(ones, high) + nn_dot(ones, low)


def call(kernel, out_shape, name, scratch=(), flops=0):
    def run(*operands):
        return pl.pallas_call(
            kernel,
            out_shape=out_shape,
            in_specs=[pl.BlockSpec(memory_space=pltpu.VMEM)] * len(operands),
            out_specs=jax.tree.map(lambda _: pl.BlockSpec(memory_space=pltpu.VMEM), out_shape),
            scratch_shapes=list(scratch),
            compiler_params=pltpu.CompilerParams(vmem_limit_bytes=vmem_bytes),
            cost_estimate=pl.CostEstimate(flops=flops, bytes_accessed=1 << 20, transcendentals=0),
            name=name,
        )(*operands)

    return run


def low_rows(width, samples):
    starts = {"w": 0, "sample": width, "w_out": width + samples}
    sizes = {"w": width, "sample": samples, "w_out": 16}
    return {name: slice(at, at + sizes[name]) for name, at in starts.items()}


def line_rows(slots, channels):
    return {
        "ids": 0,
        "occ": slots,
        "direction": slots + 1,
        "target": slots + 2,
        "b_out": slots + 2 + channels,
    }


def order_kernel(earlier_ref, later_ref):
    shape = earlier_ref.shape
    r_i = lax.broadcasted_iota(jnp.int32, shape, 0)
    c_i = lax.broadcasted_iota(jnp.int32, shape, 1)
    earlier_ref[...] = jnp.where(c_i < r_i, 1.0, 0.0).astype(bf16)
    later_ref[...] = jnp.where(c_i > r_i, 1.0, 0.0).astype(bf16)


def chosen_kernel(lines_ref, brick_ref, w_t_ref, chosen_ref, project_ref):
    total = chosen_ref.shape[1]
    rays = lines_ref.shape[1]
    bricks = brick_ref.shape[0]
    brick_t = brick_ref[...].astype(f32).T.astype(bf16)
    w_t = w_t_ref[...]
    row = lax.broadcasted_iota(jnp.int32, (bricks, rays), 0).astype(f32)
    for k in range(total // rays):
        one_hot = jnp.where(row == lines_ref[k : k + 1, :], 1.0, 0.0).astype(bf16)
        chosen = nn_dot(brick_t, one_hot).astype(bf16)
        chosen_ref[:, k * rays : (k + 1) * rays] = chosen
        project_ref[:, k * rays : (k + 1) * rays] = nn_dot(w_t, chosen)


def prepare_kernel(
    ray_ref,
    w_ref,
    sample_ref,
    w_out_ref,
    ids_ref,
    occ_ref,
    direction_ref,
    target_ref,
    b_ref,
    b_out_ref,
    own_ref,
    low_ref,
    lines_ref,
    w_t_ref,
    s_ref,
    wide_ref,
    left_ref,
    *,
    rows,
    lines,
):
    slots, rays = ids_ref.shape
    width = w_t_ref.shape[0]
    samples = s_ref.shape[0]
    outs = w_out_ref.shape[0]
    own_ref[...] = ray_ref[...]
    w = w_ref[...]
    w_out = w_out_ref[...].astype(f32)
    low_ref[rows["w"], :] = w
    low_ref[rows["sample"], :] = sample_ref[...]
    low_ref[rows["w_out"], :] = jnp.concatenate(
        [w_out, jnp.zeros((16 - outs, width), f32)], 0
    ).astype(bf16)
    lines_ref[:slots, :] = ids_ref[...].astype(f32)
    lines_ref[lines["occ"] : lines["occ"] + 1, :] = occ_ref[...].astype(f32)
    lines_ref[lines["direction"] : lines["direction"] + 1, :] = direction_ref[...].astype(f32)
    lines_ref[lines["target"] : lines["target"] + outs - 1, :] = target_ref[...]
    lines_ref[lines["b_out"] : lines["b_out"] + 1, :outs] = b_out_ref[...]
    w_t = w.astype(f32).T.astype(bf16)
    w_t_ref[...] = w_t
    s = nn_dot(sample_ref[...], w) + b_ref[...]
    s_ref[...] = s.astype(bf16).astype(f32)
    s_t = jnp.concatenate([s] * (128 // samples), 0).T
    for j in range(samples):
        wide_ref[j] = jnp.broadcast_to(s_t[:, j : j + 1], (width, 128)).astype(bf16)
    w_rows = jnp.concatenate(
        [jnp.broadcast_to(w_out[c : c + 1, :], (8, width)) for c in range(outs)], 0
    )
    row8 = lax.broadcasted_iota(jnp.int32, (outs * 8, width), 0) % 8
    for i in range(8):
        left_ref[:, i * width : (i + 1) * width] = jnp.where(row8 == i, w_rows, 0.0).astype(bf16)


def forward_kernel(*refs, owners, second, lines):
    ray_ref, project_ref, w_t_ref, wide_ref, left_ref, lines_ref, earlier_ref, *refs = refs
    if second:
        before_refs, refs = refs[:3], refs[3:]
    seg_ref, kept_ref, u_ref, sorted_ref, order_ref, ut_ref, raw_ref = refs
    width, total = project_ref.shape
    samples = wide_ref.shape[0]
    outs = seg_ref.shape[0]
    half, rays = ray_ref.shape[0], lines_ref.shape[1]
    slots = total // rays
    chunk = 128
    own = 2 * half // owners
    last = gather_bits(owners, own)[-1]
    me = lax.axis_index("slab")
    side = (me >> last) & 1

    def whole(n, k=0, side=side):
        return pl.ds(pl.multiple_of(k * rays + (2 * n + side) * chunk, chunk), chunk)

    if second:
        for n in range(half // chunk):
            part = slice(n * chunk, (n + 1) * chunk)
            seg_ref[:, whole(n)] = before_refs[0][:, part]
            sorted_ref[whole(n), :] = before_refs[2][part, :]
            for k in range(slots):
                u_ref[whole(n, k), :] = before_refs[1][k * half + n * chunk : k * half + (n + 1) * chunk, :]
        side = 1 - side

    def spot(n, k=0):
        at = k * half + n * chunk
        return whole(n, k, side) if second else slice(at, at + chunk)

    flip = (1 << last) if second else 0
    for i, t in enumerate(gather_order(owners, own)):
        owner = me ^ (t ^ flip)
        place = ((owner >> (last + 1)) << last) | (owner & ((1 << last) - 1))
        order_ref[pl.ds(pl.multiple_of(place * own, own), own), :] = ray_ref[
            i * own : (i + 1) * own, :
        ]
    ray_t = nt_dot(w_t_ref[...], order_ref[...])
    for n in range(half // chunk):
        sorted_ref[spot(n), :] = order_ref[n * chunk : (n + 1) * chunk, :]
        for k in range(slots):
            part = project_ref[:, whole(n, k, side)] + ray_t[:, n * chunk : (n + 1) * chunk]
            part = part.astype(bf16)
            ut_ref[:, k * half + n * chunk : k * half + (n + 1) * chunk] = part
            u_ref[spot(n, k), :] = part.astype(f32).T.astype(bf16)
    b_out = [lines_ref[lines["b_out"], c] for c in range(outs)]

    def shade_block(block, carry):
        for n in range(slots * half // 256):
            lanes = slice(n * 256, n * 256 + 256)
            ut = ut_ref[:, lanes]
            acc = None
            for i in range(4):
                parts = []
                for h in range(2):
                    column = wide_ref[block * 8 + 2 * i + h]
                    column = jnp.concatenate([column, column], 1)
                    parts.append(jnp.maximum(ut + column, 0))
                left = left_ref[:, 2 * i * width : 2 * (i + 1) * width]
                term = nn_dot(left, jnp.concatenate(parts, 0))
                acc = term if acc is None else acc + term
            for c in range(outs):
                raw_ref[c, pl.ds(pl.multiple_of(block * 8, 8), 8), lanes] = (
                    acc[c * 8 : c * 8 + 8, :] + b_out[c]
                )
        return carry

    lax.fori_loop(0, samples // 8, shade_block, 0, unroll=8)
    earlier = earlier_ref[...]
    occ_row = lines["occ"]
    for n in range(half // chunk):
        occ = lines_ref[occ_row : occ_row + 1, whole(n, 0, side)]
        raws = [
            raw_ref[0, :, k * half + n * chunk : k * half + (n + 1) * chunk] for k in range(slots)
        ]
        occupied = [(k < occ).astype(f32) for k in range(slots)]
        opticals = [
            step_length * (jnp.maximum(x, 0.0) + jnp.log1p(jnp.exp(-jnp.abs(x)))) * o
            for x, o in zip(raws, occupied)
        ]
        enters = sum_dot(earlier, jnp.concatenate(opticals, 1))
        before = jnp.zeros((1, chunk), f32)
        colors = [jnp.zeros((1, chunk), f32)] * (outs - 1)
        for k in range(slots):
            local = slice(k * half + n * chunk, k * half + (n + 1) * chunk)
            optical = opticals[k]
            entered = enters[:, k * chunk : (k + 1) * chunk] + before
            before = before + jnp.sum(optical, 0, keepdims=True)
            tanh = jnp.tanh(0.5 * optical)
            weight = jnp.exp(-entered) * (2.0 * tanh / (1.0 + tanh))
            for c in range(outs - 1):
                shading = jax.nn.sigmoid(raw_ref[c + 1, :, local])
                light = weight * shading
                colors[c] = colors[c] + jnp.sum(light, 0, keepdims=True)
                kept_ref[c, :, local] = shading
                kept_ref[outs + c, :, local] = light
            kept_ref[outs - 1, :, local] = jnp.exp(-(entered + optical))
            kept_ref[2 * outs - 1, :, local] = step_length * occupied[k] * jax.nn.sigmoid(raws[k])
        place = spot(n)
        for c in range(outs - 1):
            seg_ref[c : c + 1, place] = colors[c]
        seg_ref[outs - 1 : outs, place] = jnp.exp(-before)


def coefficient_kernel(seg_ref, first_ref, second_ref, later_ref, coef_ref, turned_ref, *, owners):
    outs, rays = seg_ref.shape
    samples, local = first_ref.shape[1:]
    half = rays // 2
    slots = local // half
    last = gather_bits(owners, rays // owners)[-1]
    side = (lax.axis_index("slab") >> last) & 1
    later = later_ref[...]
    chunk = 128

    def keep(index, lanes, value):
        coef_ref[index, :, lanes] = value
        turned_ref[index, lanes, :] = jnp.concatenate([value] * (128 // samples), 0).T

    for kept_ref, where in ((first_ref, side), (second_ref, 1 - side)):
        for n in range(half // chunk):
            base = (2 * n + where) * chunk
            through = seg_ref[outs - 1 : outs, pl.ds(pl.multiple_of(base, chunk), chunk)]
            after = [jnp.zeros((1, chunk), f32)] * (outs - 1)
            for k in reversed(range(slots)):
                lanes = pl.ds(pl.multiple_of(k * rays + base, chunk), chunk)
                at = slice(k * half + n * chunk, k * half + (n + 1) * chunk)
                passed = kept_ref[outs - 1, :, at]
                density = kept_ref[2 * outs - 1, :, at]
                lights = [kept_ref[outs + c, :, at] for c in range(outs - 1)]
                behinds = sum_dot(later, jnp.concatenate(lights, 1))
                for c in range(outs - 1):
                    shading = kept_ref[c, :, at]
                    light = lights[c]
                    behind = behinds[:, c * chunk : (c + 1) * chunk] + after[c]
                    after[c] = after[c] + jnp.sum(light, 0, keepdims=True)
                    keep(c, lanes, density * (shading * passed - behind))
                    keep(outs + c, lanes, light * (1.0 - shading))
                keep(outs - 1, lanes, density * through)


def basis_kernel(turned_ref, u_ref, s_ref, low_ref, h1_ref, moved_ref, *, first, row_of):
    count, rays, width = h1_ref.shape
    samples = s_ref.shape[0]
    negative = (-s_ref[...]).astype(bf16)
    one = jnp.ones((samples, width), bf16)
    zero = jnp.zeros((samples, width), bf16)
    lane = lax.broadcasted_iota(jnp.int32, (8, 8 * samples), 1) // samples
    row = lax.broadcasted_iota(jnp.int32, (8, 8 * samples), 0)
    block_mask = lane == row
    repeat = 8 * samples // 128
    step = 128
    outs = moved_ref.shape[0]
    w = low_ref[row_of["w"], :]
    w_out = low_ref[row_of["w_out"], :].astype(f32)
    w_rows = [w_out[c : c + 1, :] for c in range(outs)]

    def slot_block(block, carry):
        for h in range(step // 16):
            base = pl.multiple_of(block * step + h * 16, 16)
            u16 = u_ref[pl.ds(first + base, 16), :]
            for q in range(2):
                at = pl.multiple_of(block * step + h * 16 + q * 8, 8)
                left = [
                    jnp.where(
                        block_mask,
                        jnp.concatenate([turned_ref[c, pl.ds(first + at, 8), :]] * repeat, 1),
                        0.0,
                    )
                    for c in range(count)
                ]
                left = jnp.concatenate(left, 0).astype(bf16)
                tiles = [
                    jnp.where(
                        jnp.broadcast_to(u16[q * 8 + i : q * 8 + i + 1, :], (samples, width))
                        > negative,
                        one,
                        zero,
                    )
                    for i in range(8)
                ]
                h1 = nn_dot(left, jnp.concatenate(tiles, 0))
                for c in range(count):
                    h1_ref[c, pl.ds(at, 8), :] = h1[c * 8 : c * 8 + 8, :]
        return carry

    lax.fori_loop(0, rays // step, slot_block, 0)
    for c in range(outs):
        grad = w_rows[0] * h1_ref[c]
        if c + 1 < outs:
            grad = grad + w_rows[c + 1] * h1_ref[outs + c]
        moved_ref[c] = nt_dot(grad.astype(bf16), w)


def basis_cuts(total, bits):
    eighth = total // 8
    return [0, eighth, 5 * eighth, total] if bits > 2 else [0, total]


def basis_part(refs, row):
    for ref in refs:
        if row < ref.shape[1]:
            return ref, row
        row -= ref.shape[1]


def merge(first, second, forward):
    fc, ft = first
    sc, st = second
    return jnp.where(forward, fc + ft * sc, sc + st * fc), ft * st


def middle_kernel(*refs, owners, pieces, lines):
    bits = bits_of(owners)
    seg_ref, refs = refs[0], refs[1:]
    got_refs, refs = refs[:bits], refs[bits:]
    moved_refs, refs = refs[:pieces], refs[pieces:]
    lines_ref, keep_ref, send_ref, cot_ref, cot_t_ref, ray_ref = refs
    me = lax.axis_index("slab")
    outs = seg_ref.shape[0]
    channels = outs - 1
    rays = lines_ref.shape[1]
    width = moved_refs[0].shape[2]
    slots = sum(ref.shape[1] for ref in moved_refs) // rays
    forward = lines_ref[lines["direction"] : lines["direction"] + 1, :] == 0.0
    target = lines_ref[lines["target"] : lines["target"] + channels, :]

    def pair(values):
        return values[:channels, :], values[channels : channels + 1, :]

    low = high = None
    for b in reversed(range(bits)):
        piece = pair(got_refs[b][...])
        is_low = ((me >> b) & 1) == 1
        piece = (jnp.where(is_low, piece[0], 0.0), jnp.where(is_low, piece[1], 1.0))
        low = piece if low is None else merge(low, piece, forward)
    for b in range(bits):
        piece = pair(got_refs[b][...])
        is_high = ((me >> b) & 1) == 0
        piece = (jnp.where(is_high, piece[0], 0.0), jnp.where(is_high, piece[1], 1.0))
        high = piece if high is None else merge(high, piece, forward)
    seg_color, seg_trans = pair(seg_ref[...])
    before_color = jnp.where(forward, low[0], high[0])
    before_trans = jnp.where(forward, low[1], high[1])
    after_color = jnp.where(forward, high[0], low[0])
    color = before_color + before_trans * (seg_color + seg_trans * after_color)
    residual = color - target
    color_cot = before_trans * residual
    trans_cot = -before_trans * jnp.sum(after_color * residual, 0, keepdims=True)
    cot_ref[:channels, :] = color_cot
    cot_ref[channels:outs, :] = trans_cot
    cot_ref[outs : outs + channels, :] = color
    cot_ref[outs + channels :, :] = jnp.zeros((8 - outs - channels, rays), f32)
    chunk = 128
    for n in range(rays // chunk):
        these = slice(n * chunk, (n + 1) * chunk)
        turned = cot_ref[:, these].T
        cot_t_ref[these, :] = turned
        grad = None
        for c in range(outs):
            whole = None
            for k in range(slots):
                ref, at = basis_part(moved_refs, k * rays + n * chunk)
                part = ref[c, at : at + chunk, :]
                whole = part if whole is None else whole + part
            term = jnp.broadcast_to(turned[:, c : c + 1], (chunk, width)) * whole
            grad = term if grad is None else grad + term
        ray_ref[these, :] = grad
    own = rays // owners
    for i, t in enumerate(halving_order(owners)):
        place = pl.multiple_of((me ^ t) * own, own)
        if i < owners // 2:
            keep_ref[i * own : (i + 1) * own, :] = ray_ref[pl.ds(place, own), :]
        else:
            at = i * own - rays // 2
            send_ref[at : at + own, :] = ray_ref[pl.ds(place, own), :].astype(bf16)


def brick_kernel(lines_ref, moved_ref, keep_ref, send_ref, *, shares):
    share = lax.axis_index("ray")
    rays = lines_ref.shape[1]
    total, width = moved_ref.shape
    slots = total // rays
    half = keep_ref.shape[0]
    part = 2 * half // shares
    moved = moved_ref[...]
    row = lax.broadcasted_iota(jnp.int32, (part, rays), 0).astype(f32)
    for i in range(shares):
        first = ((share ^ i) * part).astype(f32)
        acc = jnp.zeros((part, width), f32)
        for k in range(slots):
            one_hot = jnp.where(row + first == lines_ref[k : k + 1, :], 1.0, 0.0).astype(bf16)
            rows = slice(k * rays, (k + 1) * rays)
            acc = acc + nn_dot(one_hot, moved[rows])
        ref, at = (keep_ref, i * part) if i < shares // 2 else (send_ref, i * part - half)
        ref[at : at + part, :] = acc


def sample_kernel(
    cot_ref, coef_ref, u_ref, s_ref, low_ref, by_sample_ref, sums_ref, bias_ref, g_ref, *, first, rows
):
    outs = sums_ref.shape[0]
    channels = outs - 1
    rays = cot_ref.shape[1]
    total, width = u_ref.shape
    samples = by_sample_ref.shape[0]
    bias_sums = [jnp.zeros((1, 128), f32)] * outs
    for n in range(total // 128):
        lanes = slice(n * 128, n * 128 + 128)
        at = (n * 128) % rays
        cots = [cot_ref[c : c + 1, at : at + 128] for c in range(outs)]
        grads = [sum(cots[c] * coef_ref[c, first : first + samples, lanes] for c in range(outs))]
        for c in range(channels):
            grads.append(cots[c] * coef_ref[outs + c, first : first + samples, lanes])
        for c in range(outs):
            bias_sums[c] = bias_sums[c] + jnp.sum(grads[c], 0, keepdims=True)
        for j in range(0, samples, 8):
            g_ref[j // 8, :, lanes] = jnp.concatenate([g[j : j + 8] for g in grads], 0).astype(bf16)
    w_out = low_ref[rows["w_out"], :].astype(f32)
    w_rows = [w_out[c : c + 1, :] for c in range(outs)]
    row8 = lax.broadcasted_iota(jnp.int32, (8, width), 0)

    def sample_block(block, sums):
        left = g_ref[block]
        s8 = s_ref[pl.ds(pl.multiple_of(first + block * 8, 8), 8), :]
        acc = [jnp.zeros((8, width), f32)] * outs
        for i in range(0, 8, 2):
            edges = [(-s8[i + h : i + h + 1, :]).astype(bf16) for h in range(2)]
            h2 = None
            for n in range(total // 256):
                u = u_ref[n * 256 : n * 256 + 256, :]
                live = [
                    jnp.where(
                        u > jnp.broadcast_to(edge, u.shape),
                        jnp.ones(u.shape, bf16),
                        jnp.zeros(u.shape, bf16),
                    )
                    for edge in edges
                ]
                term = nn_dot(left[:, n * 256 : n * 256 + 256], jnp.concatenate(live, 1))
                h2 = term if h2 is None else h2 + term
            for c in range(outs):
                for h in range(2):
                    piece = h2[c * 8 : c * 8 + 8, h * width : (h + 1) * width]
                    acc[c] = acc[c] + jnp.where(row8 == i + h, piece, 0.0)
        by_sample_ref[pl.ds(pl.multiple_of(block * 8, 8), 8), :] = sum(
            w_rows[c] * acc[c] for c in range(outs)
        )
        return tuple(sums[c] + s8 * acc[c] for c in range(outs))

    sums = [jnp.zeros((8, width), f32)] * outs
    sums = lax.fori_loop(0, samples // 8, sample_block, tuple(sums), unroll=4)
    for c in range(outs):
        sums_ref[c] = sums[c]
        bias_ref[c : c + 1, :] = bias_sums[c]


def inputs_kernel(chosen_ref, sorted_ref, inputs_ref):
    total = chosen_ref.shape[1]
    ray_t = sorted_ref[...].astype(f32).T
    inputs = chosen_ref[...].astype(f32) + jnp.concatenate([ray_t] * (total // ray_t.shape[1]), 1)
    inputs_ref[...] = inputs.astype(bf16)


def slots_kernel(*refs, pieces, rows):
    h1_refs, refs = refs[:pieces], refs[pieces:]
    basis_refs, refs = refs[:pieces], refs[pieces:]
    cot_t_ref, u_ref, inputs_ref, low_ref, *refs = refs
    moved_ref, w_grad_ref, sums_ref, slot_ref = refs
    rays = cot_t_ref.shape[0]
    total, width = u_ref.shape
    outs = sums_ref.shape[0]
    w_out = low_ref[rows["w_out"], :].astype(f32)
    w_rows = [w_out[c : c + 1, :] for c in range(outs)]
    chunk = 32
    sums = [jnp.zeros((8, width), f32)] * outs
    for n in range(rays // chunk):
        turned = cot_t_ref[n * chunk : (n + 1) * chunk, :]
        cots = [jnp.broadcast_to(turned[:, c : c + 1], (chunk, width)) for c in range(outs)]
        for k in range(total // rays):
            whole = slice(k * rays + n * chunk, k * rays + (n + 1) * chunk)
            u = u_ref[whole, :].astype(f32)
            h1_ref, at = basis_part(h1_refs, whole.start)
            basis_ref, at = basis_part(basis_refs, whole.start)
            here = slice(at, at + chunk)
            products = [sum(cots[c] * h1_ref[c, here, :] for c in range(outs))]
            products += [cots[c] * h1_ref[outs + c, here, :] for c in range(outs - 1)]
            for c in range(outs):
                sums[c] = sums[c] + jnp.sum((u * products[c]).reshape(chunk // 8, 8, width), 0)
            slot_ref[whole, :] = sum(w_rows[c] * products[c] for c in range(outs)).astype(bf16)
            moved = sum(cots[c] * basis_ref[c, here, :] for c in range(outs))
            moved_ref[whole, :] = moved.astype(bf16)
    for c in range(outs):
        sums_ref[c] = sums[c]
    w_grad_ref[...] = nn_dot(inputs_ref[...], slot_ref[...])


def flipped(a, b):
    return nn_dot(b, a)


def network_kernel(*refs, parts, rows):
    part_refs, refs = refs[: 3 * parts], refs[3 * parts :]
    w_grad_ref, sums_ref, low_ref, small_ref = refs
    by_sample = jnp.concatenate([part_refs[3 * i][...] for i in range(parts)], 0)
    samples, width = by_sample.shape
    outs = sums_ref.shape[0]
    w = low_ref[rows["w"], :]
    sample = low_ref[rows["sample"], :].astype(f32)
    sample_t = jnp.concatenate([sample] * (128 // samples), 0).T[:, :samples]
    small_ref[:samples, :] = split_dot(by_sample, w, nt_dot)
    small_ref[samples : samples + width, :] = w_grad_ref[...] + split_dot(
        by_sample, sample_t.astype(bf16), flipped
    )
    at = samples + width
    small_ref[at : at + 1, :] = jnp.sum(by_sample, 0, keepdims=True)
    lane128 = lax.broadcasted_iota(jnp.int32, (1, 128), 1)
    bias = jnp.zeros((1, 128), f32)
    for c in range(outs):
        total = sums_ref[c] + sum(part_refs[3 * i + 1][c] for i in range(parts))
        small_ref[at + 1 + c : at + 2 + c, :] = jnp.sum(total, 0, keepdims=True)
        row = sum(part_refs[3 * i + 2][c : c + 1, :] for i in range(parts))
        bias = bias + jnp.where(lane128 == c, jnp.sum(row, 1, keepdims=True), 0.0)
    small_ref[at + 1 + outs : at + 2 + outs, :] = bias
    rest = small_ref.shape[0] - (at + 2 + outs)
    small_ref[at + 2 + outs :, :] = jnp.zeros((rest, width), f32)


def ray_sum_kernel(keep_ref, got_ref, cot_ref, out_ref, color_ref):
    out_ref[...] = keep_ref[...] + got_ref[...].astype(f32)
    channels, own = color_ref.shape
    rays = cot_ref.shape[1]
    me = lax.axis_index("slab")
    r_i = lax.broadcasted_iota(jnp.int32, (rays, own), 0)
    c_i = lax.broadcasted_iota(jnp.int32, (rays, own), 1)
    pick = jnp.where(r_i == c_i + me * own, 1.0, 0.0).astype(bf16)
    color = cot_ref[channels + 1 : 2 * channels + 1, :]
    high = color.astype(bf16)
    middle = (color - high.astype(f32)).astype(bf16)
    low = (color - high.astype(f32) - middle.astype(f32)).astype(bf16)
    picked = nn_dot(jnp.concatenate([high, middle, low], 0), pick)
    color_ref[...] = picked[:channels] + picked[channels : 2 * channels] + picked[2 * channels :]


def finish_kernel(
    ray_ref,
    color_ref,
    brick_ref,
    sent_ref,
    got_ref,
    color_out_ref,
    ray_out_ref,
    brick_out_ref,
    sample_ref,
    w_ref,
    b_ref,
    w_out_ref,
    b_out_ref,
):
    ray_out_ref[...] = ray_ref[...]
    color_out_ref[...] = color_ref[...]
    part = brick_ref.shape[0]
    brick_out_ref[...] = brick_ref[...] + got_ref[:part, :].astype(f32)
    small = sent_ref[part:, :].astype(f32) + got_ref[part:, :].astype(f32)
    samples, width = sample_ref.shape
    outs = w_out_ref.shape[0]
    at = samples + width
    sample_ref[...] = small[:samples]
    w_ref[...] = small[samples:at]
    b_ref[...] = small[at : at + 1]
    w_out_ref[...] = small[at + 1 : at + 1 + outs]
    b_out_ref[...] = small[at + 1 + outs : at + 2 + outs, :outs]


def body(
    ray_code,
    direction,
    target,
    brick_code,
    sample_code,
    w_hidden,
    b_hidden,
    w_out,
    b_out,
    brick_ids,
    occupancy,
):
    owners = lax.axis_size("slab")
    shares = lax.axis_size("ray")
    me = lax.axis_index("slab")
    ids = brick_ids[0]
    slots, rays = ids.shape
    total = slots * rays
    bricks, width = brick_code.shape[1:]
    samples = sample_code.shape[1]
    outs = w_out.shape[1]
    channels = outs - 1
    count = outs + channels

    def shaped(*shape):
        return jax.ShapeDtypeStruct(shape, f32)

    def shaped16(*shape):
        return jax.ShapeDtypeStruct(shape, bf16)

    rows = low_rows(width, samples)
    lines = line_rows(slots, channels)
    earlier, later = call(
        order_kernel,
        (shaped16(samples, samples), shaped16(samples, samples)),
        "order",
        flops=1 << 34,
    )()
    gathered, low, packed, w_t, s, wide, left = call(
        functools.partial(prepare_kernel, rows=rows, lines=lines),
        (
            shaped16(*ray_code.shape),
            shaped16(rows["w_out"].stop, width),
            shaped(lines["b_out"] + 1, rays),
            shaped16(width, width),
            shaped(samples, width),
            shaped16(samples, width, 128),
            shaped16(outs * 8, 8 * width),
        ),
        "prepare",
        flops=1 << 31,
    )(
        ray_code,
        w_hidden[0],
        sample_code[0],
        w_out[0],
        ids,
        occupancy,
        direction[None],
        target,
        b_hidden,
        b_out,
    )
    turns = gather_bits(owners, ray_code.shape[0])
    other = swap(ray_code, "slab", owners, 1 << turns[0])
    other, lines_later = lax.optimization_barrier((other, packed))
    for b in turns[1:]:
        gathered = jnp.concatenate([gathered, other], 0)
        other = swap(gathered, "slab", owners, 1 << b)
    chosen, project = call(
        chosen_kernel,
        (shaped16(width, total), shaped(width, total)),
        "chosen",
        flops=1 << 29,
    )(lines_later, brick_code[0], w_t)
    passes = ()
    kept = []
    for second, part in enumerate((gathered, other)):
        wide_rays = rays if second else rays // 2
        seg, kept_half, *passes = call(
            functools.partial(forward_kernel, owners=owners, second=second, lines=lines),
            (
                shaped(outs, wide_rays),
                shaped(2 * outs, samples, total // 2),
                shaped16(slots * wide_rays, width),
                shaped16(wide_rays, width),
            ),
            "forward",
            scratch=(
                pltpu.VMEM((rays // 2, width), bf16),
                pltpu.VMEM((width, total // 2), bf16),
                pltpu.VMEM((outs, samples, total // 2), f32),
            ),
            flops=1 << 30,
        )(part, project, w_t, wide, left, packed, earlier, *passes)
        passes = (seg, *passes)
        kept.append(kept_half)
    seg, u, ray_sorted = passes

    coef, turned = call(
        functools.partial(coefficient_kernel, owners=owners),
        (shaped(count, samples, total), shaped(count, total, 128)),
        "coefficients",
        flops=1 << 30,
    )(seg, *kept, later)
    forward = packed[lines["direction"]][None] == 0.0
    group = (seg[:channels], seg[channels:])
    received = []
    basis = []
    bits = bits_of(owners)
    cuts = basis_cuts(total, bits)
    pieces = len(cuts) - 1
    turned_later, chosen_later = turned, chosen
    for b in range(bits):
        sent = jnp.concatenate(group, 0) if b > 0 else seg
        other = swap(sent, "slab", owners, 1 << b)
        if b < pieces:
            piece = cuts[b + 1] - cuts[b]
            basis.append(
                call(
                    functools.partial(basis_kernel, first=cuts[b], row_of=rows),
                    (shaped(count, piece, width), shaped(outs, piece, width)),
                    "basis",
                    flops=1 << 29,
                )(turned_later, u, s, low)
            )
        if b + 1 == bits:
            inputs = call(inputs_kernel, shaped16(width, total), "inputs", flops=1 << 28)(
                chosen_later, ray_sorted
            )
            other, inputs = lax.optimization_barrier((other, inputs))
        other, turned_later, chosen_later = lax.optimization_barrier(
            (other, turned_later, chosen_later)
        )
        received.append(other)
        theirs = (other[:channels], other[channels:])
        upper = ((me >> b) & 1) == 1
        first = jax.tree.map(lambda a, b: jnp.where(upper, b, a), group, theirs)
        second = jax.tree.map(lambda a, b: jnp.where(upper, a, b), group, theirs)
        group = merge(first, second, forward)

    h1, moved_basis = zip(*basis)
    ray_keep, ray_send, cots, cots_t = call(
        functools.partial(middle_kernel, owners=owners, pieces=pieces, lines=lines),
        (
            shaped(rays // 2, width),
            shaped16(rays // 2, width),
            shaped(8, rays),
            shaped(rays, 8),
        ),
        "middle",
        scratch=(pltpu.VMEM((rays, width), f32),),
        flops=1 << 29,
    )(seg, *received, *moved_basis, packed)
    moved, w_grad, sums = call(
        functools.partial(slots_kernel, pieces=pieces, rows=rows),
        (
            shaped16(total, width),
            shaped(width, width),
            shaped(outs, 8, width),
        ),
        "slots",
        scratch=(pltpu.VMEM((total, width), bf16),),
        flops=1 << 28,
    )(*h1, *moved_basis, cots_t, u, inputs, low)

    def merged(keep, got):
        half = keep.shape[0] // 2
        return keep[:half] + got[:half].astype(f32), (keep[half:] + got[half:].astype(f32)).astype(bf16)

    def part_by_sample(i, cots):
        return call(
            functools.partial(sample_kernel, first=i * samples // parts, rows=rows),
            (
                shaped(samples // parts, width),
                shaped(outs, 8, width),
                shaped(outs, 128),
            ),
            "by_sample",
            scratch=(pltpu.VMEM((samples // parts // 8, outs * 8, total), bf16),),
            flops=1 << 28,
        )(cots, coef, u, s, low)

    parts = 2
    by_part = []
    later_cots = cots
    for b in range(bits):
        if b + 1 == bits:
            brick_keep, brick_send = call(
                functools.partial(brick_kernel, shares=shares),
                (shaped(bricks // 2, width), shaped(bricks // 2, width)),
                "bricks",
                flops=1 << 28,
            )(packed, moved)
            small_rows = -(-(samples + width + 2 + outs) // 16) * 16
            small = call(
                functools.partial(network_kernel, parts=parts, rows=rows),
                shaped(small_rows, width),
                "network",
                flops=1 << 28,
            )(*by_part, w_grad, sums, low)
            held = (ray_send, brick_send, small)
            ray_send, brick_send, small = lax.optimization_barrier(held)
        ray_got = swap(ray_send, "slab", owners, 1 << halving_bits(owners)[b])
        if b < parts:
            by_part += part_by_sample(b, later_cots)
        if b + 1 < bits:
            held = (ray_got, later_cots, moved)
            ray_got, later_cots, moved = lax.optimization_barrier(held)
            ray_keep, ray_send = merged(ray_keep, ray_got)

    brick = brick_keep
    brick_sent = brick_send.astype(bf16)
    for b in reversed(range(bits_of(shares))):
        sent = jnp.concatenate([brick_sent, small.astype(bf16)], 0)
        other = swap(sent, "ray", shares, 1 << b)
        if b > 0:
            half = brick.shape[0]
            small = sent[half:].astype(f32) + other[half:].astype(f32)
            brick_sent = (brick[half // 2 :] + other[half // 2 : half].astype(f32)).astype(bf16)
            brick = brick[: half // 2] + other[: half // 2].astype(f32)
    ray_sum, color_own = call(
        ray_sum_kernel,
        (shaped(rays // owners, width), shaped(channels, rays // owners)),
        "ray_sum",
        flops=1 << 31,
    )(ray_keep, ray_got, cots)
    color_out, ray_out, brick_out, sample_out, w_grad, b_grad, w_out_grad, b_out_grad = call(
        finish_kernel,
        (
            shaped(channels, rays // owners),
            shaped(rays // owners, width),
            shaped(bricks // shares, width),
            shaped(samples, width),
            shaped(width, width),
            shaped(1, width),
            shaped(outs, width),
            shaped(1, outs),
        ),
        "finish",
    )(ray_sum, color_own, brick, sent, other)
    return (
        color_out,
        ray_out,
        brick_out[None],
        sample_out[None],
        w_grad[None],
        b_grad,
        w_out_grad[None],
        b_out_grad,
    )


def solution(mesh):
    in_specs = (
        P(("ray", "slab"), None),
        P("ray"),
        P(None, "ray"),
        P("slab", None, None),
        P("slab", None, None),
        P("slab", None, None),
        P("slab", None),
        P("slab", None, None),
        P("slab", None),
        P("slab", None, "ray"),
        P("slab", "ray"),
    )
    out_specs = (
        P(None, ("ray", "slab")),
        P(("ray", "slab"), None),
        P("slab", "ray", None),
        P("slab", None, None),
        P("slab", None, None),
        P("slab", None),
        P("slab", None, None),
        P("slab", None),
    )
    return jax.shard_map(body, mesh=mesh, in_specs=in_specs, out_specs=out_specs, check_vma=False)
```

```python
import functools

import jax
import jax.numpy as jnp
from jax import lax
from jax.experimental import pallas as pl
from jax.experimental.pallas import tpu as pltpu
from jax.sharding import PartitionSpec as P

step_length = 0.002
f32 = jnp.float32
bf16 = jnp.bfloat16
vmem_bytes = 24 * 1024 * 1024
exact = lax.Precision.HIGHEST


def bits_of(count):
    bits = count.bit_length() - 1
    assert count == 1 << bits
    return bits


def gather_bits(owners, own):
    last = max(bits_of(128 // own), 0) if own < 128 else 0
    return [b for b in reversed(range(bits_of(owners))) if b != last] + [last]


def gather_order(owners, own):
    order = [0]
    for b in gather_bits(owners, own)[:-1]:
        order = order + [t ^ (1 << b) for t in order]
    return order


def halving_bits(owners):
    bits = list(range(bits_of(owners)))
    return bits[1:-1] + bits[:1] + bits[1:][-1:]


def halving_order(owners):
    order = [0]
    for b in reversed(halving_bits(owners)):
        order = order + [t ^ (1 << b) for t in order]
    return order


def split_dot(a, b, dot):
    high = a.astype(bf16)
    low = (a - high.astype(f32)).astype(bf16)
    return dot(high, b) + dot(low, b)


def nt_dot(a, b, precision=None):
    return lax.dot_general(
        a, b, (((1,), (1,)), ((), ())), precision=precision, preferred_element_type=f32
    )


def nn_dot(a, b, precision=None):
    return jnp.dot(a, b, precision=precision, preferred_element_type=f32)


def swap(array, axis, size, distance):
    return lax.ppermute(array, axis, [(i, i ^ distance) for i in range(size)])


def sum_dot(ones, b):
    high = b.astype(bf16)
    low = (b - high.astype(f32)).astype(bf16)
    return nn_dot(ones, high) + nn_dot(ones, low)


def call(kernel, out_shape, name, scratch=(), flops=0):
    def run(*operands):
        return pl.pallas_call(
            kernel,
            out_shape=out_shape,
            in_specs=[pl.BlockSpec(memory_space=pltpu.VMEM)] * len(operands),
            out_specs=jax.tree.map(lambda _: pl.BlockSpec(memory_space=pltpu.VMEM), out_shape),
            scratch_shapes=list(scratch),
            compiler_params=pltpu.CompilerParams(vmem_limit_bytes=vmem_bytes),
            cost_estimate=pl.CostEstimate(flops=flops, bytes_accessed=1 << 10, transcendentals=0),
            name=name,
        )(*operands)

    return run


def low_rows(width, samples):
    starts = {"w": 0, "sample": width, "w_out": width + samples}
    sizes = {"w": width, "sample": samples, "w_out": 16}
    return {name: slice(at, at + sizes[name]) for name, at in starts.items()}


def line_rows(slots, channels):
    return {
        "ids": 0,
        "occ": slots,
        "direction": slots + 1,
        "target": slots + 2,
        "b_out": slots + 2 + channels,
    }


def order_kernel(earlier_ref, later_ref):
    shape = earlier_ref.shape
    r_i = lax.broadcasted_iota(jnp.int32, shape, 0)
    c_i = lax.broadcasted_iota(jnp.int32, shape, 1)
    earlier_ref[...] = jnp.where(c_i < r_i, 1.0, 0.0).astype(bf16)
    later_ref[...] = jnp.where(c_i > r_i, 1.0, 0.0).astype(bf16)


def chosen_kernel(lines_ref, brick_ref, w_t_ref, chosen_ref, project_ref):
    total = chosen_ref.shape[1]
    rays = lines_ref.shape[1]
    bricks = brick_ref.shape[0]
    brick_t = brick_ref[...].astype(f32).T.astype(bf16)
    w_t = w_t_ref[...]
    row = lax.broadcasted_iota(jnp.int32, (bricks, rays), 0).astype(f32)
    for k in range(total // rays):
        one_hot = jnp.where(row == lines_ref[k : k + 1, :], 1.0, 0.0).astype(bf16)
        chosen = nn_dot(brick_t, one_hot).astype(bf16)
        chosen_ref[:, k * rays : (k + 1) * rays] = chosen
        project_ref[:, k * rays : (k + 1) * rays] = nn_dot(w_t, chosen)


def prepare_kernel(
    ray_ref,
    w_ref,
    sample_ref,
    w_out_ref,
    ids_ref,
    occ_ref,
    direction_ref,
    target_ref,
    b_ref,
    b_out_ref,
    own_ref,
    low_ref,
    lines_ref,
    w_t_ref,
    s_ref,
    wide_ref,
    left_ref,
    *,
    rows,
    lines,
):
    slots, rays = ids_ref.shape
    width = w_t_ref.shape[0]
    samples = s_ref.shape[0]
    outs = w_out_ref.shape[0]
    own_ref[...] = ray_ref[...]
    w = w_ref[...]
    w_out = w_out_ref[...].astype(f32)
    low_ref[rows["w"], :] = w
    low_ref[rows["sample"], :] = sample_ref[...]
    low_ref[rows["w_out"], :] = jnp.concatenate(
        [w_out, jnp.zeros((16 - outs, width), f32)], 0
    ).astype(bf16)
    lines_ref[:slots, :] = ids_ref[...].astype(f32)
    lines_ref[lines["occ"] : lines["occ"] + 1, :] = occ_ref[...].astype(f32)
    lines_ref[lines["direction"] : lines["direction"] + 1, :] = direction_ref[...].astype(f32)
    lines_ref[lines["target"] : lines["target"] + outs - 1, :] = target_ref[...]
    lines_ref[lines["b_out"] : lines["b_out"] + 1, :outs] = b_out_ref[...]
    w_t = w.astype(f32).T.astype(bf16)
    w_t_ref[...] = w_t
    s = nn_dot(sample_ref[...], w) + b_ref[...]
    s_ref[...] = s.astype(bf16).astype(f32)
    s_t = jnp.concatenate([s] * (128 // samples), 0).T
    for j in range(samples):
        wide_ref[j] = jnp.broadcast_to(s_t[:, j : j + 1], (width, 128)).astype(bf16)
    w_rows = jnp.concatenate(
        [jnp.broadcast_to(w_out[c : c + 1, :], (8, width)) for c in range(outs)], 0
    )
    row8 = lax.broadcasted_iota(jnp.int32, (outs * 8, width), 0) % 8
    for i in range(8):
        left_ref[:, i * width : (i + 1) * width] = jnp.where(row8 == i, w_rows, 0.0).astype(bf16)


def forward_kernel(*refs, owners, second, lines):
    ray_ref, project_ref, w_t_ref, wide_ref, left_ref, lines_ref, earlier_ref, *refs = refs
    if second:
        before_refs, refs = refs[:3], refs[3:]
    seg_ref, kept_ref, u_ref, sorted_ref, order_ref, ut_ref, raw_ref = refs
    width, total = project_ref.shape
    samples = wide_ref.shape[0]
    outs = seg_ref.shape[0]
    half, rays = ray_ref.shape[0], lines_ref.shape[1]
    slots = total // rays
    chunk = 128
    own = 2 * half // owners
    last = gather_bits(owners, own)[-1]
    me = lax.axis_index("slab")
    side = (me >> last) & 1

    def whole(n, k=0, side=side):
        return pl.ds(pl.multiple_of(k * rays + (2 * n + side) * chunk, chunk), chunk)

    if second:
        for n in range(half // chunk):
            part = slice(n * chunk, (n + 1) * chunk)
            seg_ref[:, whole(n)] = before_refs[0][:, part]
            sorted_ref[whole(n), :] = before_refs[2][part, :]
            for k in range(slots):
                u_ref[whole(n, k), :] = before_refs[1][k * half + n * chunk : k * half + (n + 1) * chunk, :]
        side = 1 - side

    def spot(n, k=0):
        at = k * half + n * chunk
        return whole(n, k, side) if second else slice(at, at + chunk)

    flip = (1 << last) if second else 0
    for i, t in enumerate(gather_order(owners, own)):
        owner = me ^ (t ^ flip)
        place = ((owner >> (last + 1)) << last) | (owner & ((1 << last) - 1))
        order_ref[pl.ds(pl.multiple_of(place * own, own), own), :] = ray_ref[
            i * own : (i + 1) * own, :
        ]
    ray_t = nt_dot(w_t_ref[...], order_ref[...])
    for n in range(half // chunk):
        sorted_ref[spot(n), :] = order_ref[n * chunk : (n + 1) * chunk, :]
        for k in range(slots):
            part = project_ref[:, whole(n, k, side)] + ray_t[:, n * chunk : (n + 1) * chunk]
            part = part.astype(bf16)
            ut_ref[:, k * half + n * chunk : k * half + (n + 1) * chunk] = part
            u_ref[spot(n, k), :] = part.astype(f32).T.astype(bf16)
    b_out = [lines_ref[lines["b_out"], c] for c in range(outs)]

    def shade_block(block, carry):
        for n in range(slots * half // 256):
            lanes = slice(n * 256, n * 256 + 256)
            ut = ut_ref[:, lanes]
            acc = None
            for i in range(4):
                parts = []
                for h in range(2):
                    column = wide_ref[block * 8 + 2 * i + h]
                    column = jnp.concatenate([column, column], 1)
                    parts.append(jnp.maximum(ut + column, 0))
                left = left_ref[:, 2 * i * width : 2 * (i + 1) * width]
                term = nn_dot(left, jnp.concatenate(parts, 0))
                acc = term if acc is None else acc + term
            for c in range(outs):
                raw_ref[c, pl.ds(pl.multiple_of(block * 8, 8), 8), lanes] = (
                    acc[c * 8 : c * 8 + 8, :] + b_out[c]
                )
        return carry

    lax.fori_loop(0, samples // 8, shade_block, 0, unroll=8)
    earlier = earlier_ref[...]
    occ_row = lines["occ"]
    for n in range(half // chunk):
        occ = lines_ref[occ_row : occ_row + 1, whole(n, 0, side)]
        raws = [
            raw_ref[0, :, k * half + n * chunk : k * half + (n + 1) * chunk] for k in range(slots)
        ]
        occupied = [(k < occ).astype(f32) for k in range(slots)]
        opticals = [
            step_length * (jnp.maximum(x, 0.0) + jnp.log1p(jnp.exp(-jnp.abs(x)))) * o
            for x, o in zip(raws, occupied)
        ]
        enters = sum_dot(earlier, jnp.concatenate(opticals, 1))
        before = jnp.zeros((1, chunk), f32)
        colors = [jnp.zeros((1, chunk), f32)] * (outs - 1)
        for k in range(slots):
            local = slice(k * half + n * chunk, k * half + (n + 1) * chunk)
            optical = opticals[k]
            entered = enters[:, k * chunk : (k + 1) * chunk] + before
            before = before + jnp.sum(optical, 0, keepdims=True)
            tanh = jnp.tanh(0.5 * optical)
            weight = jnp.exp(-entered) * (2.0 * tanh / (1.0 + tanh))
            for c in range(outs - 1):
                shading = jax.nn.sigmoid(raw_ref[c + 1, :, local])
                light = weight * shading
                colors[c] = colors[c] + jnp.sum(light, 0, keepdims=True)
                kept_ref[c, :, local] = shading
                kept_ref[outs + c, :, local] = light
            kept_ref[outs - 1, :, local] = jnp.exp(-(entered + optical))
            kept_ref[2 * outs - 1, :, local] = step_length * occupied[k] * jax.nn.sigmoid(raws[k])
        place = spot(n)
        for c in range(outs - 1):
            seg_ref[c : c + 1, place] = colors[c]
        seg_ref[outs - 1 : outs, place] = jnp.exp(-before)


def coefficient_kernel(seg_ref, first_ref, second_ref, later_ref, coef_ref, turned_ref, *, owners):
    outs, rays = seg_ref.shape
    samples, local = first_ref.shape[1:]
    half = rays // 2
    slots = local // half
    last = gather_bits(owners, rays // owners)[-1]
    side = (lax.axis_index("slab") >> last) & 1
    later = later_ref[...]
    chunk = 128

    def keep(index, lanes, value):
        coef_ref[index, :, lanes] = value
        turned_ref[index, lanes, :] = jnp.concatenate([value] * (128 // samples), 0).T

    for kept_ref, where in ((first_ref, side), (second_ref, 1 - side)):
        for n in range(half // chunk):
            base = (2 * n + where) * chunk
            through = seg_ref[outs - 1 : outs, pl.ds(pl.multiple_of(base, chunk), chunk)]
            after = [jnp.zeros((1, chunk), f32)] * (outs - 1)
            for k in reversed(range(slots)):
                lanes = pl.ds(pl.multiple_of(k * rays + base, chunk), chunk)
                at = slice(k * half + n * chunk, k * half + (n + 1) * chunk)
                passed = kept_ref[outs - 1, :, at]
                density = kept_ref[2 * outs - 1, :, at]
                lights = [kept_ref[outs + c, :, at] for c in range(outs - 1)]
                behinds = sum_dot(later, jnp.concatenate(lights, 1))
                for c in range(outs - 1):
                    shading = kept_ref[c, :, at]
                    light = lights[c]
                    behind = behinds[:, c * chunk : (c + 1) * chunk] + after[c]
                    after[c] = after[c] + jnp.sum(light, 0, keepdims=True)
                    keep(c, lanes, density * (shading * passed - behind))
                    keep(outs + c, lanes, light * (1.0 - shading))
                keep(outs - 1, lanes, density * through)


def basis_kernel(turned_ref, u_ref, s_ref, low_ref, h1_ref, moved_ref, *, first, row_of):
    count, rays, width = h1_ref.shape
    samples = s_ref.shape[0]
    negative = (-s_ref[...]).astype(bf16)
    one = jnp.ones((samples, width), bf16)
    zero = jnp.zeros((samples, width), bf16)
    lane = lax.broadcasted_iota(jnp.int32, (8, 8 * samples), 1) // samples
    row = lax.broadcasted_iota(jnp.int32, (8, 8 * samples), 0)
    block_mask = lane == row
    repeat = 8 * samples // 128
    step = 128
    outs = moved_ref.shape[0]
    w = low_ref[row_of["w"], :]
    w_out = low_ref[row_of["w_out"], :].astype(f32)
    w_rows = [w_out[c : c + 1, :] for c in range(outs)]

    def slot_block(block, carry):
        for h in range(step // 16):
            base = pl.multiple_of(block * step + h * 16, 16)
            u16 = u_ref[pl.ds(first + base, 16), :]
            for q in range(2):
                at = pl.multiple_of(block * step + h * 16 + q * 8, 8)
                left = [
                    jnp.where(
                        block_mask,
                        jnp.concatenate([turned_ref[c, pl.ds(first + at, 8), :]] * repeat, 1),
                        0.0,
                    )
                    for c in range(count)
                ]
                left = jnp.concatenate(left, 0).astype(bf16)
                tiles = [
                    jnp.where(
                        jnp.broadcast_to(u16[q * 8 + i : q * 8 + i + 1, :], (samples, width))
                        > negative,
                        one,
                        zero,
                    )
                    for i in range(8)
                ]
                h1 = nn_dot(left, jnp.concatenate(tiles, 0))
                for c in range(count):
                    h1_ref[c, pl.ds(at, 8), :] = h1[c * 8 : c * 8 + 8, :]
        return carry

    lax.fori_loop(0, rays // step, slot_block, 0)
    for c in range(outs):
        grad = w_rows[0] * h1_ref[c]
        if c + 1 < outs:
            grad = grad + w_rows[c + 1] * h1_ref[outs + c]
        moved_ref[c] = nt_dot(grad.astype(bf16), w)


def basis_cuts(total, bits):
    eighth = total // 8
    return [0, eighth, 5 * eighth, total] if bits > 2 else [0, total]


def basis_part(refs, row):
    for ref in refs:
        if row < ref.shape[1]:
            return ref, row
        row -= ref.shape[1]


def merge(first, second, forward):
    fc, ft = first
    sc, st = second
    return jnp.where(forward, fc + ft * sc, sc + st * fc), ft * st


def middle_kernel(*refs, owners, pieces, lines):
    bits = bits_of(owners)
    seg_ref, refs = refs[0], refs[1:]
    got_refs, refs = refs[:bits], refs[bits:]
    moved_refs, refs = refs[:pieces], refs[pieces:]
    lines_ref, keep_ref, send_ref, cot_ref, spread_ref, ray_ref = refs
    me = lax.axis_index("slab")
    outs = seg_ref.shape[0]
    channels = outs - 1
    rays = lines_ref.shape[1]
    width = moved_refs[0].shape[2]
    slots = sum(ref.shape[1] for ref in moved_refs) // rays
    forward = lines_ref[lines["direction"] : lines["direction"] + 1, :] == 0.0
    target = lines_ref[lines["target"] : lines["target"] + channels, :]

    def pair(values):
        return values[:channels, :], values[channels : channels + 1, :]

    low = high = None
    for b in reversed(range(bits)):
        piece = pair(got_refs[b][...])
        is_low = ((me >> b) & 1) == 1
        piece = (jnp.where(is_low, piece[0], 0.0), jnp.where(is_low, piece[1], 1.0))
        low = piece if low is None else merge(low, piece, forward)
    for b in range(bits):
        piece = pair(got_refs[b][...])
        is_high = ((me >> b) & 1) == 0
        piece = (jnp.where(is_high, piece[0], 0.0), jnp.where(is_high, piece[1], 1.0))
        high = piece if high is None else merge(high, piece, forward)
    seg_color, seg_trans = pair(seg_ref[...])
    before_color = jnp.where(forward, low[0], high[0])
    before_trans = jnp.where(forward, low[1], high[1])
    after_color = jnp.where(forward, high[0], low[0])
    color = before_color + before_trans * (seg_color + seg_trans * after_color)
    residual = color - target
    color_cot = before_trans * residual
    trans_cot = -before_trans * jnp.sum(after_color * residual, 0, keepdims=True)
    cot_ref[:channels, :] = color_cot
    cot_ref[channels:outs, :] = trans_cot
    cot_ref[outs : outs + channels, :] = color
    cot_ref[outs + channels :, :] = jnp.zeros((8 - outs - channels, rays), f32)
    chunk = 128
    values = jnp.concatenate([color_cot, trans_cot], 0)
    rounded = values.astype(bf16).astype(f32)
    values = jnp.concatenate([rounded, values - rounded], 0)
    row = lax.broadcasted_iota(jnp.int32, (2 * outs, outs * width), 0) % outs
    lane = lax.broadcasted_iota(jnp.int32, (2 * outs, outs * width), 1) // width
    spread = jnp.where(row == lane, 1.0, 0.0).astype(bf16)
    for n in range(rays // chunk):
        these = slice(n * chunk, (n + 1) * chunk)
        spread_ref[these, :] = nn_dot(values[:, these].T.astype(bf16), spread)
        grad = None
        for c in range(outs):
            whole = None
            for k in range(slots):
                ref, at = basis_part(moved_refs, k * rays + n * chunk)
                part = ref[c, at : at + chunk, :]
                whole = part if whole is None else whole + part
            term = spread_ref[these, c * width : (c + 1) * width] * whole
            grad = term if grad is None else grad + term
        ray_ref[these, :] = grad
    own = rays // owners
    for i, t in enumerate(halving_order(owners)):
        place = pl.multiple_of((me ^ t) * own, own)
        if i < owners // 2:
            keep_ref[i * own : (i + 1) * own, :] = ray_ref[pl.ds(place, own), :]
        else:
            at = i * own - rays // 2
            send_ref[at : at + own, :] = ray_ref[pl.ds(place, own), :].astype(bf16)


def brick_kernel(lines_ref, moved_ref, keep_ref, send_ref, *, shares):
    share = lax.axis_index("ray")
    rays = lines_ref.shape[1]
    total, width = moved_ref.shape
    slots = total // rays
    half = keep_ref.shape[0]
    part = 2 * half // shares
    moved = moved_ref[...]
    row = lax.broadcasted_iota(jnp.int32, (part, rays), 0).astype(f32)
    for i in range(shares):
        first = ((share ^ i) * part).astype(f32)
        acc = jnp.zeros((part, width), f32)
        for k in range(slots):
            one_hot = jnp.where(row + first == lines_ref[k : k + 1, :], 1.0, 0.0).astype(bf16)
            rows = slice(k * rays, (k + 1) * rays)
            acc = acc + nn_dot(one_hot, moved[rows])
        ref, at = (keep_ref, i * part) if i < shares // 2 else (send_ref, i * part - half)
        ref[at : at + part, :] = acc


def sample_kernel(
    cot_ref, coef_ref, u_ref, s_ref, low_ref, by_sample_ref, sums_ref, bias_ref, g_ref, *, first, rows
):
    outs = sums_ref.shape[0]
    channels = outs - 1
    rays = cot_ref.shape[1]
    total, width = u_ref.shape
    samples = by_sample_ref.shape[0]
    bias_sums = [jnp.zeros((1, 128), f32)] * outs
    for n in range(total // 128):
        lanes = slice(n * 128, n * 128 + 128)
        at = (n * 128) % rays
        cots = [cot_ref[c : c + 1, at : at + 128] for c in range(outs)]
        grads = [sum(cots[c] * coef_ref[c, first : first + samples, lanes] for c in range(outs))]
        for c in range(channels):
            grads.append(cots[c] * coef_ref[outs + c, first : first + samples, lanes])
        for c in range(outs):
            bias_sums[c] = bias_sums[c] + jnp.sum(grads[c], 0, keepdims=True)
        for j in range(0, samples, 8):
            g_ref[j // 8, :, lanes] = jnp.concatenate([g[j : j + 8] for g in grads], 0).astype(bf16)
    w_out = low_ref[rows["w_out"], :].astype(f32)
    w_rows = [w_out[c : c + 1, :] for c in range(outs)]
    row8 = lax.broadcasted_iota(jnp.int32, (8, width), 0)

    def sample_block(block, sums):
        left = g_ref[block]
        s8 = s_ref[pl.ds(pl.multiple_of(first + block * 8, 8), 8), :]
        acc = [jnp.zeros((8, width), f32)] * outs
        for i in range(0, 8, 2):
            edges = [(-s8[i + h : i + h + 1, :]).astype(bf16) for h in range(2)]
            h2 = None
            for n in range(total // 256):
                u = u_ref[n * 256 : n * 256 + 256, :]
                live = [
                    jnp.where(
                        u > jnp.broadcast_to(edge, u.shape),
                        jnp.ones(u.shape, bf16),
                        jnp.zeros(u.shape, bf16),
                    )
                    for edge in edges
                ]
                term = nn_dot(left[:, n * 256 : n * 256 + 256], jnp.concatenate(live, 1))
                h2 = term if h2 is None else h2 + term
            for c in range(outs):
                for h in range(2):
                    piece = h2[c * 8 : c * 8 + 8, h * width : (h + 1) * width]
                    acc[c] = acc[c] + jnp.where(row8 == i + h, piece, 0.0)
        by_sample_ref[pl.ds(pl.multiple_of(block * 8, 8), 8), :] = sum(
            w_rows[c] * acc[c] for c in range(outs)
        )
        return tuple(sums[c] + s8 * acc[c] for c in range(outs))

    sums = [jnp.zeros((8, width), f32)] * outs
    sums = lax.fori_loop(0, samples // 8, sample_block, tuple(sums), unroll=4)
    for c in range(outs):
        sums_ref[c] = sums[c]
        bias_ref[c : c + 1, :] = bias_sums[c]


def inputs_kernel(chosen_ref, sorted_ref, inputs_ref):
    total = chosen_ref.shape[1]
    ray_t = sorted_ref[...].astype(f32).T
    inputs = chosen_ref[...].astype(f32) + jnp.concatenate([ray_t] * (total // ray_t.shape[1]), 1)
    inputs_ref[...] = inputs.astype(bf16)


def slots_kernel(*refs, pieces, rows):
    h1_refs, refs = refs[:pieces], refs[pieces:]
    basis_refs, refs = refs[:pieces], refs[pieces:]
    spread_ref, u_ref, inputs_ref, low_ref, *refs = refs
    moved_ref, w_grad_ref, sums_ref, slot_ref = refs
    rays = spread_ref.shape[0]
    total, width = u_ref.shape
    outs = sums_ref.shape[0]
    w_out = low_ref[rows["w_out"], :].astype(f32)
    w_rows = [w_out[c : c + 1, :] for c in range(outs)]
    chunk = 32
    sums = [jnp.zeros((8, width), f32)] * outs
    for n in range(rays // chunk):
        these = slice(n * chunk, (n + 1) * chunk)
        cots = [spread_ref[these, c * width : (c + 1) * width] for c in range(outs)]
        for k in range(total // rays):
            whole = slice(k * rays + n * chunk, k * rays + (n + 1) * chunk)
            u = u_ref[whole, :].astype(f32)
            h1_ref, at = basis_part(h1_refs, whole.start)
            basis_ref, at = basis_part(basis_refs, whole.start)
            here = slice(at, at + chunk)
            products = [sum(cots[c] * h1_ref[c, here, :] for c in range(outs))]
            products += [cots[c] * h1_ref[outs + c, here, :] for c in range(outs - 1)]
            for c in range(outs):
                sums[c] = sums[c] + jnp.sum((u * products[c]).reshape(chunk // 8, 8, width), 0)
            slot_ref[whole, :] = sum(w_rows[c] * products[c] for c in range(outs)).astype(bf16)
            moved = sum(cots[c] * basis_ref[c, here, :] for c in range(outs))
            moved_ref[whole, :] = moved.astype(bf16)
    for c in range(outs):
        sums_ref[c] = sums[c]
    w_grad_ref[...] = nn_dot(inputs_ref[...], slot_ref[...])


def flipped(a, b):
    return nn_dot(b, a)


def network_kernel(*refs, parts, rows):
    part_refs, refs = refs[: 3 * parts], refs[3 * parts :]
    w_grad_ref, sums_ref, low_ref, small_ref = refs
    by_sample = jnp.concatenate([part_refs[3 * i][...] for i in range(parts)], 0)
    samples, width = by_sample.shape
    outs = sums_ref.shape[0]
    w = low_ref[rows["w"], :]
    sample = low_ref[rows["sample"], :].astype(f32)
    sample_t = jnp.concatenate([sample] * (128 // samples), 0).T[:, :samples]
    small_ref[:samples, :] = split_dot(by_sample, w, nt_dot)
    small_ref[samples : samples + width, :] = w_grad_ref[...] + split_dot(
        by_sample, sample_t.astype(bf16), flipped
    )
    at = samples + width
    small_ref[at : at + 1, :] = jnp.sum(by_sample, 0, keepdims=True)
    lane128 = lax.broadcasted_iota(jnp.int32, (1, 128), 1)
    bias = jnp.zeros((1, 128), f32)
    for c in range(outs):
        total = sums_ref[c] + sum(part_refs[3 * i + 1][c] for i in range(parts))
        small_ref[at + 1 + c : at + 2 + c, :] = jnp.sum(total, 0, keepdims=True)
        row = sum(part_refs[3 * i + 2][c : c + 1, :] for i in range(parts))
        bias = bias + jnp.where(lane128 == c, jnp.sum(row, 1, keepdims=True), 0.0)
    small_ref[at + 1 + outs : at + 2 + outs, :] = bias
    rest = small_ref.shape[0] - (at + 2 + outs)
    small_ref[at + 2 + outs :, :] = jnp.zeros((rest, width), f32)


def ray_sum_kernel(keep_ref, got_ref, cot_ref, out_ref, color_ref):
    out_ref[...] = keep_ref[...] + got_ref[...].astype(f32)
    channels, own = color_ref.shape
    rays = cot_ref.shape[1]
    me = lax.axis_index("slab")
    r_i = lax.broadcasted_iota(jnp.int32, (rays, own), 0)
    c_i = lax.broadcasted_iota(jnp.int32, (rays, own), 1)
    pick = jnp.where(r_i == c_i + me * own, 1.0, 0.0).astype(bf16)
    color = cot_ref[channels + 1 : 2 * channels + 1, :]
    high = color.astype(bf16)
    middle = (color - high.astype(f32)).astype(bf16)
    low = (color - high.astype(f32) - middle.astype(f32)).astype(bf16)
    picked = nn_dot(jnp.concatenate([high, middle, low], 0), pick)
    color_ref[...] = picked[:channels] + picked[channels : 2 * channels] + picked[2 * channels :]


def finish_kernel(
    ray_ref,
    color_ref,
    brick_ref,
    sent_ref,
    got_ref,
    color_out_ref,
    ray_out_ref,
    brick_out_ref,
    sample_ref,
    w_ref,
    b_ref,
    w_out_ref,
    b_out_ref,
):
    ray_out_ref[...] = ray_ref[...]
    color_out_ref[...] = color_ref[...]
    part = brick_ref.shape[0]
    brick_out_ref[...] = brick_ref[...] + got_ref[:part, :].astype(f32)
    small = sent_ref[part:, :].astype(f32) + got_ref[part:, :].astype(f32)
    samples, width = sample_ref.shape
    outs = w_out_ref.shape[0]
    at = samples + width
    sample_ref[...] = small[:samples]
    w_ref[...] = small[samples:at]
    b_ref[...] = small[at : at + 1]
    w_out_ref[...] = small[at + 1 : at + 1 + outs]
    b_out_ref[...] = small[at + 1 + outs : at + 2 + outs, :outs]


def body(
    ray_code,
    direction,
    target,
    brick_code,
    sample_code,
    w_hidden,
    b_hidden,
    w_out,
    b_out,
    brick_ids,
    occupancy,
):
    owners = lax.axis_size("slab")
    shares = lax.axis_size("ray")
    me = lax.axis_index("slab")
    ids = brick_ids[0]
    slots, rays = ids.shape
    total = slots * rays
    bricks, width = brick_code.shape[1:]
    samples = sample_code.shape[1]
    outs = w_out.shape[1]
    channels = outs - 1
    count = outs + channels

    def shaped(*shape):
        return jax.ShapeDtypeStruct(shape, f32)

    def shaped16(*shape):
        return jax.ShapeDtypeStruct(shape, bf16)

    rows = low_rows(width, samples)
    lines = line_rows(slots, channels)
    earlier, later = call(
        order_kernel,
        (shaped16(samples, samples), shaped16(samples, samples)),
        "order",
        flops=1 << 34,
    )()
    gathered, low, packed, w_t, s, wide, left = call(
        functools.partial(prepare_kernel, rows=rows, lines=lines),
        (
            shaped16(*ray_code.shape),
            shaped16(rows["w_out"].stop, width),
            shaped(lines["b_out"] + 1, rays),
            shaped16(width, width),
            shaped(samples, width),
            shaped16(samples, width, 128),
            shaped16(outs * 8, 8 * width),
        ),
        "prepare",
        flops=1 << 31,
    )(
        ray_code,
        w_hidden[0],
        sample_code[0],
        w_out[0],
        ids,
        occupancy,
        direction[None],
        target,
        b_hidden,
        b_out,
    )
    turns = gather_bits(owners, ray_code.shape[0])
    other = swap(ray_code, "slab", owners, 1 << turns[0])
    other, lines_later = lax.optimization_barrier((other, packed))
    for b in turns[1:]:
        gathered = jnp.concatenate([gathered, other], 0)
        other = swap(gathered, "slab", owners, 1 << b)
    chosen, project = call(
        chosen_kernel,
        (shaped16(width, total), shaped(width, total)),
        "chosen",
        flops=1 << 29,
    )(lines_later, brick_code[0], w_t)
    passes = ()
    kept = []
    for second, part in enumerate((gathered, other)):
        wide_rays = rays if second else rays // 2
        seg, kept_half, *passes = call(
            functools.partial(forward_kernel, owners=owners, second=second, lines=lines),
            (
                shaped(outs, wide_rays),
                shaped(2 * outs, samples, total // 2),
                shaped16(slots * wide_rays, width),
                shaped16(wide_rays, width),
            ),
            "forward",
            scratch=(
                pltpu.VMEM((rays // 2, width), bf16),
                pltpu.VMEM((width, total // 2), bf16),
                pltpu.VMEM((outs, samples, total // 2), f32),
            ),
            flops=1 << 30,
        )(part, project, w_t, wide, left, packed, earlier, *passes)
        passes = (seg, *passes)
        kept.append(kept_half)
    seg, u, ray_sorted = passes

    coef, turned = call(
        functools.partial(coefficient_kernel, owners=owners),
        (shaped(count, samples, total), shaped(count, total, 128)),
        "coefficients",
        flops=1 << 30,
    )(seg, *kept, later)
    forward = packed[lines["direction"]][None] == 0.0
    group = (seg[:channels], seg[channels:])
    received = []
    basis = []
    bits = bits_of(owners)
    cuts = basis_cuts(total, bits)
    pieces = len(cuts) - 1
    turned_later, chosen_later = turned, chosen
    for b in range(bits):
        sent = jnp.concatenate(group, 0) if b > 0 else seg
        other = swap(sent, "slab", owners, 1 << b)
        if b < pieces:
            piece = cuts[b + 1] - cuts[b]
            basis.append(
                call(
                    functools.partial(basis_kernel, first=cuts[b], row_of=rows),
                    (shaped(count, piece, width), shaped(outs, piece, width)),
                    "basis",
                    flops=1 << 29,
                )(turned_later, u, s, low)
            )
        if b + 1 == bits:
            inputs = call(inputs_kernel, shaped16(width, total), "inputs", flops=1 << 20)(
                chosen_later, ray_sorted
            )
            other, inputs = lax.optimization_barrier((other, inputs))
        other, turned_later, chosen_later = lax.optimization_barrier(
            (other, turned_later, chosen_later)
        )
        received.append(other)
        theirs = (other[:channels], other[channels:])
        upper = ((me >> b) & 1) == 1
        first = jax.tree.map(lambda a, b: jnp.where(upper, b, a), group, theirs)
        second = jax.tree.map(lambda a, b: jnp.where(upper, a, b), group, theirs)
        group = merge(first, second, forward)

    h1, moved_basis = zip(*basis)
    ray_keep, ray_send, cots, spread = call(
        functools.partial(middle_kernel, owners=owners, pieces=pieces, lines=lines),
        (
            shaped(rays // 2, width),
            shaped16(rays // 2, width),
            shaped(8, rays),
            shaped(rays, outs * width),
        ),
        "middle",
        scratch=(pltpu.VMEM((rays, width), f32),),
        flops=1 << 29,
    )(seg, *received, *moved_basis, packed)
    moved, w_grad, sums = call(
        functools.partial(slots_kernel, pieces=pieces, rows=rows),
        (
            shaped16(total, width),
            shaped(width, width),
            shaped(outs, 8, width),
        ),
        "slots",
        scratch=(pltpu.VMEM((total, width), bf16),),
        flops=1 << 20,
    )(*h1, *moved_basis, spread, u, inputs, low)

    def merged(keep, got):
        half = keep.shape[0] // 2
        return keep[:half] + got[:half].astype(f32), (keep[half:] + got[half:].astype(f32)).astype(bf16)

    def part_by_sample(i, cots):
        return call(
            functools.partial(sample_kernel, first=i * samples // parts, rows=rows),
            (
                shaped(samples // parts, width),
                shaped(outs, 8, width),
                shaped(outs, 128),
            ),
            "by_sample",
            scratch=(pltpu.VMEM((samples // parts // 8, outs * 8, total), bf16),),
            flops=1 << 20,
        )(cots, coef, u, s, low)

    parts = 2
    by_part = []
    later_cots = cots
    for b in range(bits):
        if b + 1 == bits:
            small_rows = -(-(samples + width + 2 + outs) // 16) * 16
            small = call(
                functools.partial(network_kernel, parts=parts, rows=rows),
                shaped(small_rows, width),
                "network",
                flops=1 << 20,
            )(*by_part, w_grad, sums, low)
            ray_send, small = lax.optimization_barrier((ray_send, small))
        ray_got = swap(ray_send, "slab", owners, 1 << halving_bits(owners)[b])
        if b < parts:
            by_part += part_by_sample(b, later_cots)
        if b == 1:
            brick_keep, brick_send = call(
                functools.partial(brick_kernel, shares=shares),
                (shaped(bricks // 2, width), shaped(bricks // 2, width)),
                "bricks",
                flops=1 << 20,
            )(packed, moved)
            w_grad, brick_send = lax.optimization_barrier((w_grad, brick_send))
        if b + 1 < bits:
            held = (ray_got, later_cots, moved, by_part)
            ray_got, later_cots, moved, by_part = lax.optimization_barrier(held)
            ray_keep, ray_send = merged(ray_keep, ray_got)

    brick = brick_keep
    brick_sent = brick_send.astype(bf16)
    for b in reversed(range(bits_of(shares))):
        sent = jnp.concatenate([brick_sent, small.astype(bf16)], 0)
        other = swap(sent, "ray", shares, 1 << b)
        if b > 0:
            half = brick.shape[0]
            small = sent[half:].astype(f32) + other[half:].astype(f32)
            brick_sent = (brick[half // 2 :] + other[half // 2 : half].astype(f32)).astype(bf16)
            brick = brick[: half // 2] + other[: half // 2].astype(f32)
    ray_sum, color_own = call(
        ray_sum_kernel,
        (shaped(rays // owners, width), shaped(channels, rays // owners)),
        "ray_sum",
        flops=1 << 31,
    )(ray_keep, ray_got, cots)
    color_out, ray_out, brick_out, sample_out, w_grad, b_grad, w_out_grad, b_out_grad = call(
        finish_kernel,
        (
            shaped(channels, rays // owners),
            shaped(rays // owners, width),
            shaped(bricks // shares, width),
            shaped(samples, width),
            shaped(width, width),
            shaped(1, width),
            shaped(outs, width),
            shaped(1, outs),
        ),
        "finish",
    )(ray_sum, color_own, brick, sent, other)
    return (
        color_out,
        ray_out,
        brick_out[None],
        sample_out[None],
        w_grad[None],
        b_grad,
        w_out_grad[None],
        b_out_grad,
    )


def solution(mesh):
    in_specs = (
        P(("ray", "slab"), None),
        P("ray"),
        P(None, "ray"),
        P("slab", None, None),
        P("slab", None, None),
        P("slab", None, None),
        P("slab", None),
        P("slab", None, None),
        P("slab", None),
        P("slab", None, "ray"),
        P("slab", "ray"),
    )
    out_specs = (
        P(None, ("ray", "slab")),
        P(("ray", "slab"), None),
        P("slab", "ray", None),
        P("slab", None, None),
        P("slab", None, None),
        P("slab", None),
        P("slab", None, None),
        P("slab", None),
    )
    return jax.shard_map(body, mesh=mesh, in_specs=in_specs, out_specs=out_specs, check_vma=False)
```

```python
import functools

import jax
import jax.numpy as jnp
from jax import lax
from jax.experimental import pallas as pl
from jax.experimental.pallas import tpu as pltpu
from jax.sharding import PartitionSpec as P

step_length = 0.002
f32 = jnp.float32
bf16 = jnp.bfloat16
vmem_bytes = 24 * 1024 * 1024
exact = lax.Precision.HIGHEST


def bits_of(count):
    bits = count.bit_length() - 1
    assert count == 1 << bits
    return bits


def gather_bits(owners, own):
    last = max(bits_of(128 // own), 0) if own < 128 else 0
    return [b for b in reversed(range(bits_of(owners))) if b != last] + [last]


def gather_order(owners, own):
    order = [0]
    for b in gather_bits(owners, own)[:-1]:
        order = order + [t ^ (1 << b) for t in order]
    return order


def halving_bits(owners):
    bits = list(range(bits_of(owners)))
    return bits[1:-1] + bits[:1] + bits[1:][-1:]


def halving_order(owners):
    order = [0]
    for b in reversed(halving_bits(owners)):
        order = order + [t ^ (1 << b) for t in order]
    return order


def split_dot(a, b, dot):
    high = a.astype(bf16)
    low = (a - high.astype(f32)).astype(bf16)
    return dot(high, b) + dot(low, b)


def nt_dot(a, b, precision=None):
    return lax.dot_general(
        a, b, (((1,), (1,)), ((), ())), precision=precision, preferred_element_type=f32
    )


def nn_dot(a, b, precision=None):
    return jnp.dot(a, b, precision=precision, preferred_element_type=f32)


def swap(array, axis, size, distance):
    return lax.ppermute(array, axis, [(i, i ^ distance) for i in range(size)])


def sum_dot(ones, b):
    high = b.astype(bf16)
    low = (b - high.astype(f32)).astype(bf16)
    return nn_dot(ones, high) + nn_dot(ones, low)


def call(kernel, out_shape, name, scratch=(), flops=0):
    def run(*operands):
        return pl.pallas_call(
            kernel,
            out_shape=out_shape,
            in_specs=[pl.BlockSpec(memory_space=pltpu.VMEM)] * len(operands),
            out_specs=jax.tree.map(lambda _: pl.BlockSpec(memory_space=pltpu.VMEM), out_shape),
            scratch_shapes=list(scratch),
            compiler_params=pltpu.CompilerParams(vmem_limit_bytes=vmem_bytes),
            cost_estimate=pl.CostEstimate(flops=flops, bytes_accessed=1 << 10, transcendentals=0),
            name=name,
        )(*operands)

    return run


def low_rows(width, samples):
    starts = {"w": 0, "sample": width, "w_out": width + samples}
    sizes = {"w": width, "sample": samples, "w_out": 16}
    return {name: slice(at, at + sizes[name]) for name, at in starts.items()}


def line_rows(slots, channels):
    return {
        "ids": 0,
        "occ": slots,
        "direction": slots + 1,
        "target": slots + 2,
        "b_out": slots + 2 + channels,
    }


def order_kernel(earlier_ref, later_ref):
    shape = earlier_ref.shape
    r_i = lax.broadcasted_iota(jnp.int32, shape, 0)
    c_i = lax.broadcasted_iota(jnp.int32, shape, 1)
    earlier_ref[...] = jnp.where(c_i < r_i, 1.0, 0.0).astype(bf16)
    later_ref[...] = jnp.where(c_i > r_i, 1.0, 0.0).astype(bf16)


def chosen_kernel(lines_ref, brick_ref, w_t_ref, chosen_ref, project_ref):
    total = chosen_ref.shape[1]
    rays = lines_ref.shape[1]
    bricks = brick_ref.shape[0]
    brick_t = brick_ref[...].astype(f32).T.astype(bf16)
    w_t = w_t_ref[...]
    row = lax.broadcasted_iota(jnp.int32, (bricks, rays), 0).astype(f32)
    for k in range(total // rays):
        one_hot = jnp.where(row == lines_ref[k : k + 1, :], 1.0, 0.0).astype(bf16)
        chosen = nn_dot(brick_t, one_hot).astype(bf16)
        chosen_ref[:, k * rays : (k + 1) * rays] = chosen
        project_ref[:, k * rays : (k + 1) * rays] = nn_dot(w_t, chosen)


def prepare_kernel(
    ray_ref,
    w_ref,
    sample_ref,
    w_out_ref,
    ids_ref,
    occ_ref,
    direction_ref,
    target_ref,
    b_ref,
    b_out_ref,
    own_ref,
    low_ref,
    lines_ref,
    w_t_ref,
    s_ref,
    wide_ref,
    left_ref,
    *,
    rows,
    lines,
):
    slots, rays = ids_ref.shape
    width = w_t_ref.shape[0]
    samples = s_ref.shape[0]
    outs = w_out_ref.shape[0]
    own_ref[...] = ray_ref[...]
    w = w_ref[...]
    w_out = w_out_ref[...].astype(f32)
    low_ref[rows["w"], :] = w
    low_ref[rows["sample"], :] = sample_ref[...]
    low_ref[rows["w_out"], :] = jnp.concatenate(
        [w_out, jnp.zeros((16 - outs, width), f32)], 0
    ).astype(bf16)
    lines_ref[:slots, :] = ids_ref[...].astype(f32)
    lines_ref[lines["occ"] : lines["occ"] + 1, :] = occ_ref[...].astype(f32)
    lines_ref[lines["direction"] : lines["direction"] + 1, :] = direction_ref[...].astype(f32)
    lines_ref[lines["target"] : lines["target"] + outs - 1, :] = target_ref[...]
    lines_ref[lines["b_out"] : lines["b_out"] + 1, :outs] = b_out_ref[...]
    w_t = w.astype(f32).T.astype(bf16)
    w_t_ref[...] = w_t
    s = nn_dot(sample_ref[...], w) + b_ref[...]
    s_ref[...] = s.astype(bf16).astype(f32)
    s_t = jnp.concatenate([s] * (128 // samples), 0).T
    for j in range(samples):
        wide_ref[j] = jnp.broadcast_to(s_t[:, j : j + 1], (width, 128)).astype(bf16)
    w_rows = jnp.concatenate(
        [jnp.broadcast_to(w_out[c : c + 1, :], (8, width)) for c in range(outs)], 0
    )
    row8 = lax.broadcasted_iota(jnp.int32, (outs * 8, width), 0) % 8
    for i in range(8):
        left_ref[:, i * width : (i + 1) * width] = jnp.where(row8 == i, w_rows, 0.0).astype(bf16)


def forward_kernel(*refs, owners, second, lines):
    ray_ref, project_ref, w_t_ref, wide_ref, left_ref, lines_ref, earlier_ref, *refs = refs
    if second:
        before_refs, refs = refs[:2], refs[2:]
    seg_ref, kept_ref, ut_ref, sorted_ref, order_ref, raw_ref = refs
    width, total = project_ref.shape
    samples = wide_ref.shape[0]
    outs = seg_ref.shape[0]
    half, rays = ray_ref.shape[0], lines_ref.shape[1]
    slots = total // rays
    chunk = 128
    own = 2 * half // owners
    last = gather_bits(owners, own)[-1]
    me = lax.axis_index("slab")
    side = (me >> last) & 1

    def whole(n, k=0, side=side):
        return pl.ds(pl.multiple_of(k * rays + (2 * n + side) * chunk, chunk), chunk)

    if second:
        for n in range(half // chunk):
            part = slice(n * chunk, (n + 1) * chunk)
            seg_ref[:, whole(n)] = before_refs[0][:, part]
            sorted_ref[whole(n), :] = before_refs[1][part, :]
        side = 1 - side

    def spot(n, k=0):
        at = k * half + n * chunk
        return whole(n, k, side) if second else slice(at, at + chunk)

    flip = (1 << last) if second else 0
    for i, t in enumerate(gather_order(owners, own)):
        owner = me ^ (t ^ flip)
        place = ((owner >> (last + 1)) << last) | (owner & ((1 << last) - 1))
        order_ref[pl.ds(pl.multiple_of(place * own, own), own), :] = ray_ref[
            i * own : (i + 1) * own, :
        ]
    ray_t = nt_dot(w_t_ref[...], order_ref[...])
    for n in range(half // chunk):
        sorted_ref[spot(n), :] = order_ref[n * chunk : (n + 1) * chunk, :]
        for k in range(slots):
            part = project_ref[:, whole(n, k, side)] + ray_t[:, n * chunk : (n + 1) * chunk]
            ut_ref[:, k * half + n * chunk : k * half + (n + 1) * chunk] = part.astype(bf16)
    b_out = [lines_ref[lines["b_out"], c] for c in range(outs)]

    def shade_block(block, carry):
        for n in range(slots * half // 256):
            lanes = slice(n * 256, n * 256 + 256)
            ut = ut_ref[:, lanes]
            acc = None
            for i in range(4):
                parts = []
                for h in range(2):
                    column = wide_ref[block * 8 + 2 * i + h]
                    column = jnp.concatenate([column, column], 1)
                    parts.append(jnp.maximum(ut + column, 0))
                left = left_ref[:, 2 * i * width : 2 * (i + 1) * width]
                term = nn_dot(left, jnp.concatenate(parts, 0))
                acc = term if acc is None else acc + term
            for c in range(outs):
                raw_ref[c, pl.ds(pl.multiple_of(block * 8, 8), 8), lanes] = (
                    acc[c * 8 : c * 8 + 8, :] + b_out[c]
                )
        return carry

    lax.fori_loop(0, samples // 8, shade_block, 0, unroll=8)
    earlier = earlier_ref[...]
    occ_row = lines["occ"]
    for n in range(half // chunk):
        occ = lines_ref[occ_row : occ_row + 1, whole(n, 0, side)]
        raws = [
            raw_ref[0, :, k * half + n * chunk : k * half + (n + 1) * chunk] for k in range(slots)
        ]
        occupied = [(k < occ).astype(f32) for k in range(slots)]
        opticals = [
            step_length * (jnp.maximum(x, 0.0) + jnp.log1p(jnp.exp(-jnp.abs(x)))) * o
            for x, o in zip(raws, occupied)
        ]
        enters = sum_dot(earlier, jnp.concatenate(opticals, 1))
        before = jnp.zeros((1, chunk), f32)
        colors = [jnp.zeros((1, chunk), f32)] * (outs - 1)
        for k in range(slots):
            local = slice(k * half + n * chunk, k * half + (n + 1) * chunk)
            optical = opticals[k]
            entered = enters[:, k * chunk : (k + 1) * chunk] + before
            before = before + jnp.sum(optical, 0, keepdims=True)
            tanh = jnp.tanh(0.5 * optical)
            weight = jnp.exp(-entered) * (2.0 * tanh / (1.0 + tanh))
            for c in range(outs - 1):
                shading = jax.nn.sigmoid(raw_ref[c + 1, :, local])
                light = weight * shading
                colors[c] = colors[c] + jnp.sum(light, 0, keepdims=True)
                kept_ref[c, :, local] = shading
                kept_ref[outs + c, :, local] = light
            kept_ref[outs - 1, :, local] = entered + optical
            kept_ref[2 * outs - 1, :, local] = raws[k]
        place = spot(n)
        for c in range(outs - 1):
            seg_ref[c : c + 1, place] = colors[c]
        seg_ref[outs - 1 : outs, place] = jnp.exp(-before)


def coefficient_kernel(
    seg_ref,
    first_ref,
    second_ref,
    first_ut_ref,
    second_ut_ref,
    later_ref,
    lines_ref,
    coef_ref,
    turned_ref,
    u_ref,
    *,
    owners,
    lines,
):
    outs, rays = seg_ref.shape
    samples, local = first_ref.shape[1:]
    half = rays // 2
    slots = local // half
    last = gather_bits(owners, rays // owners)[-1]
    side = (lax.axis_index("slab") >> last) & 1
    later = later_ref[...]
    chunk = 128

    def keep(index, lanes, value):
        coef_ref[index, :, lanes] = value
        value = value.astype(bf16)
        turned_ref[index, lanes, :] = jnp.concatenate([value] * (128 // samples), 0).T

    for kept_ref, ut_ref, where in (
        (first_ref, first_ut_ref, side),
        (second_ref, second_ut_ref, 1 - side),
    ):
        for n in range(half // chunk):
            base = (2 * n + where) * chunk
            through = seg_ref[outs - 1 : outs, pl.ds(pl.multiple_of(base, chunk), chunk)]
            occ = lines_ref[lines["occ"] : lines["occ"] + 1, pl.ds(pl.multiple_of(base, chunk), chunk)]
            after = [jnp.zeros((1, chunk), f32)] * (outs - 1)
            for k in reversed(range(slots)):
                lanes = pl.ds(pl.multiple_of(k * rays + base, chunk), chunk)
                at = slice(k * half + n * chunk, k * half + (n + 1) * chunk)
                u_ref[lanes, :] = ut_ref[:, at].T
                passed = jnp.exp(-kept_ref[outs - 1, :, at])
                occupied = (k < occ).astype(f32)
                density = step_length * occupied * jax.nn.sigmoid(kept_ref[2 * outs - 1, :, at])
                lights = [kept_ref[outs + c, :, at] for c in range(outs - 1)]
                behinds = sum_dot(later, jnp.concatenate(lights, 1))
                for c in range(outs - 1):
                    shading = kept_ref[c, :, at]
                    light = lights[c]
                    behind = behinds[:, c * chunk : (c + 1) * chunk] + after[c]
                    after[c] = after[c] + jnp.sum(light, 0, keepdims=True)
                    keep(c, lanes, density * (shading * passed - behind))
                    keep(outs + c, lanes, light * (1.0 - shading))
                keep(outs - 1, lanes, density * through)


def basis_kernel(turned_ref, u_ref, s_ref, low_ref, h1_ref, moved_ref, *, first, row_of):
    count, rays, width = h1_ref.shape
    samples = s_ref.shape[0]
    negative = (-s_ref[...]).astype(bf16)
    one = jnp.ones((samples, width), bf16)
    zero = jnp.zeros((samples, width), bf16)
    lane = lax.broadcasted_iota(jnp.int32, (8, 8 * samples), 1) // samples
    row = lax.broadcasted_iota(jnp.int32, (8, 8 * samples), 0)
    block_mask = lane == row
    repeat = 8 * samples // 128
    step = 128
    outs = moved_ref.shape[0]
    w = low_ref[row_of["w"], :]
    w_out = low_ref[row_of["w_out"], :].astype(f32)
    w_rows = [w_out[c : c + 1, :] for c in range(outs)]

    def slot_block(block, carry):
        for h in range(step // 16):
            base = pl.multiple_of(block * step + h * 16, 16)
            u16 = u_ref[pl.ds(first + base, 16), :]
            rows16 = [turned_ref[c, pl.ds(first + base, 16), :].astype(f32) for c in range(count)]
            for q in range(2):
                at = pl.multiple_of(block * step + h * 16 + q * 8, 8)
                left = [
                    jnp.where(
                        block_mask,
                        jnp.concatenate([rows16[c][q * 8 : q * 8 + 8]] * repeat, 1),
                        0.0,
                    )
                    for c in range(count)
                ]
                left = jnp.concatenate(left, 0).astype(bf16)
                tiles = [
                    jnp.where(
                        jnp.broadcast_to(u16[q * 8 + i : q * 8 + i + 1, :], (samples, width))
                        > negative,
                        one,
                        zero,
                    )
                    for i in range(8)
                ]
                h1 = nn_dot(left, jnp.concatenate(tiles, 0))
                for c in range(count):
                    h1_ref[c, pl.ds(at, 8), :] = h1[c * 8 : c * 8 + 8, :]
        return carry

    lax.fori_loop(0, rays // step, slot_block, 0)
    for c in range(outs):
        grad = w_rows[0] * h1_ref[c]
        if c + 1 < outs:
            grad = grad + w_rows[c + 1] * h1_ref[outs + c]
        moved_ref[c] = nt_dot(grad.astype(bf16), w)


def basis_cuts(total, bits):
    eighth = total // 8
    return [0, 2 * eighth, 5 * eighth, total] if bits > 2 else [0, total]


def basis_part(refs, row):
    for ref in refs:
        if row < ref.shape[1]:
            return ref, row
        row -= ref.shape[1]


def merge(first, second, forward):
    fc, ft = first
    sc, st = second
    return jnp.where(forward, fc + ft * sc, sc + st * fc), ft * st


def middle_kernel(*refs, owners, pieces, lines):
    bits = bits_of(owners)
    seg_ref, refs = refs[0], refs[1:]
    got_refs, refs = refs[:bits], refs[bits:]
    moved_refs, refs = refs[:pieces], refs[pieces:]
    lines_ref, keep_ref, send_ref, cot_ref, spread_ref, ray_ref = refs
    me = lax.axis_index("slab")
    outs = seg_ref.shape[0]
    channels = outs - 1
    rays = lines_ref.shape[1]
    width = moved_refs[0].shape[2]
    slots = sum(ref.shape[1] for ref in moved_refs) // rays
    forward = lines_ref[lines["direction"] : lines["direction"] + 1, :] == 0.0
    target = lines_ref[lines["target"] : lines["target"] + channels, :]

    def pair(values):
        return values[:channels, :], values[channels : channels + 1, :]

    low = high = None
    for b in reversed(range(bits)):
        piece = pair(got_refs[b][...])
        is_low = ((me >> b) & 1) == 1
        piece = (jnp.where(is_low, piece[0], 0.0), jnp.where(is_low, piece[1], 1.0))
        low = piece if low is None else merge(low, piece, forward)
    for b in range(bits):
        piece = pair(got_refs[b][...])
        is_high = ((me >> b) & 1) == 0
        piece = (jnp.where(is_high, piece[0], 0.0), jnp.where(is_high, piece[1], 1.0))
        high = piece if high is None else merge(high, piece, forward)
    seg_color, seg_trans = pair(seg_ref[...])
    before_color = jnp.where(forward, low[0], high[0])
    before_trans = jnp.where(forward, low[1], high[1])
    after_color = jnp.where(forward, high[0], low[0])
    color = before_color + before_trans * (seg_color + seg_trans * after_color)
    residual = color - target
    color_cot = before_trans * residual
    trans_cot = -before_trans * jnp.sum(after_color * residual, 0, keepdims=True)
    cot_ref[:channels, :] = color_cot
    cot_ref[channels:outs, :] = trans_cot
    cot_ref[outs : outs + channels, :] = color
    cot_ref[outs + channels :, :] = jnp.zeros((8 - outs - channels, rays), f32)
    chunk = 128
    values = jnp.concatenate([color_cot, trans_cot], 0)
    rounded = values.astype(bf16).astype(f32)
    values = jnp.concatenate([rounded, values - rounded], 0)
    row = lax.broadcasted_iota(jnp.int32, (2 * outs, outs * width), 0) % outs
    lane = lax.broadcasted_iota(jnp.int32, (2 * outs, outs * width), 1) // width
    spread = jnp.where(row == lane, 1.0, 0.0).astype(bf16)
    for n in range(rays // chunk):
        these = slice(n * chunk, (n + 1) * chunk)
        spread_ref[these, :] = nn_dot(values[:, these].T.astype(bf16), spread)
        grad = None
        for c in range(outs):
            whole = None
            for k in range(slots):
                ref, at = basis_part(moved_refs, k * rays + n * chunk)
                part = ref[c, at : at + chunk, :]
                whole = part if whole is None else whole + part
            term = spread_ref[these, c * width : (c + 1) * width] * whole
            grad = term if grad is None else grad + term
        ray_ref[these, :] = grad
    own = rays // owners
    for i, t in enumerate(halving_order(owners)):
        place = pl.multiple_of((me ^ t) * own, own)
        if i < owners // 2:
            keep_ref[i * own : (i + 1) * own, :] = ray_ref[pl.ds(place, own), :]
        else:
            at = i * own - rays // 2
            send_ref[at : at + own, :] = ray_ref[pl.ds(place, own), :].astype(bf16)


def brick_kernel(lines_ref, moved_ref, out_ref, *, first, shares):
    share = lax.axis_index("ray")
    rays = lines_ref.shape[1]
    total, width = moved_ref.shape
    owners = shares // 2
    part = out_ref.shape[0] // owners
    moved = moved_ref[...]
    row = lax.broadcasted_iota(jnp.int32, (part, rays), 0).astype(f32)
    for i in range(owners):
        begin = ((share ^ (first + i)) * part).astype(f32)
        acc = jnp.zeros((part, width), f32)
        for k in range(total // rays):
            one_hot = jnp.where(row + begin == lines_ref[k : k + 1, :], 1.0, 0.0).astype(bf16)
            acc = acc + nn_dot(one_hot, moved[k * rays : (k + 1) * rays])
        out_ref[i * part : (i + 1) * part, :] = acc.astype(out_ref.dtype)


def sample_kernel(
    cot_ref, coef_ref, u_ref, s_ref, low_ref, by_sample_ref, sums_ref, bias_ref, g_ref, *, first, rows
):
    outs = sums_ref.shape[0]
    channels = outs - 1
    rays = cot_ref.shape[1]
    total, width = u_ref.shape
    samples = by_sample_ref.shape[0]
    bias_sums = [jnp.zeros((1, 128), f32)] * outs
    for n in range(total // 128):
        lanes = slice(n * 128, n * 128 + 128)
        at = (n * 128) % rays
        cots = [cot_ref[c : c + 1, at : at + 128] for c in range(outs)]
        grads = [sum(cots[c] * coef_ref[c, first : first + samples, lanes] for c in range(outs))]
        for c in range(channels):
            grads.append(cots[c] * coef_ref[outs + c, first : first + samples, lanes])
        for c in range(outs):
            bias_sums[c] = bias_sums[c] + jnp.sum(grads[c], 0, keepdims=True)
        for j in range(0, samples, 8):
            g_ref[j // 8, :, lanes] = jnp.concatenate([g[j : j + 8] for g in grads], 0).astype(bf16)
    w_out = low_ref[rows["w_out"], :].astype(f32)
    w_rows = [w_out[c : c + 1, :] for c in range(outs)]
    row8 = lax.broadcasted_iota(jnp.int32, (8, width), 0)

    def sample_block(block, sums):
        left = g_ref[block]
        s8 = s_ref[pl.ds(pl.multiple_of(first + block * 8, 8), 8), :]
        acc = [jnp.zeros((8, width), f32)] * outs
        for i in range(0, 8, 2):
            edges = [(-s8[i + h : i + h + 1, :]).astype(bf16) for h in range(2)]
            h2 = None
            for n in range(total // 256):
                u = u_ref[n * 256 : n * 256 + 256, :]
                live = [
                    jnp.where(
                        u > jnp.broadcast_to(edge, u.shape),
                        jnp.ones(u.shape, bf16),
                        jnp.zeros(u.shape, bf16),
                    )
                    for edge in edges
                ]
                term = nn_dot(left[:, n * 256 : n * 256 + 256], jnp.concatenate(live, 1))
                h2 = term if h2 is None else h2 + term
            for c in range(outs):
                for h in range(2):
                    piece = h2[c * 8 : c * 8 + 8, h * width : (h + 1) * width]
                    acc[c] = acc[c] + jnp.where(row8 == i + h, piece, 0.0)
        by_sample_ref[pl.ds(pl.multiple_of(block * 8, 8), 8), :] = sum(
            w_rows[c] * acc[c] for c in range(outs)
        )
        return tuple(sums[c] + s8 * acc[c] for c in range(outs))

    sums = [jnp.zeros((8, width), f32)] * outs
    sums = lax.fori_loop(0, samples // 8, sample_block, tuple(sums), unroll=4)
    for c in range(outs):
        sums_ref[c] = sums[c]
        bias_ref[c : c + 1, :] = bias_sums[c]


def inputs_kernel(chosen_ref, sorted_ref, inputs_ref):
    total = chosen_ref.shape[1]
    ray_t = sorted_ref[...].astype(f32).T
    inputs = chosen_ref[...].astype(f32) + jnp.concatenate([ray_t] * (total // ray_t.shape[1]), 1)
    inputs_ref[...] = inputs.astype(bf16)


def slots_kernel(*refs, pieces, rows):
    h1_refs, refs = refs[:pieces], refs[pieces:]
    basis_refs, refs = refs[:pieces], refs[pieces:]
    spread_ref, u_ref, inputs_ref, low_ref, *refs = refs
    moved_ref, w_grad_ref, sums_ref, slot_ref = refs
    rays = spread_ref.shape[0]
    total, width = u_ref.shape
    outs = sums_ref.shape[0]
    w_out = low_ref[rows["w_out"], :].astype(f32)
    w_rows = [w_out[c : c + 1, :] for c in range(outs)]
    chunk = 32
    sums = [jnp.zeros((8, width), f32)] * outs
    for n in range(rays // chunk):
        these = slice(n * chunk, (n + 1) * chunk)
        cots = [spread_ref[these, c * width : (c + 1) * width] for c in range(outs)]
        for k in range(total // rays):
            whole = slice(k * rays + n * chunk, k * rays + (n + 1) * chunk)
            u = u_ref[whole, :].astype(f32)
            h1_ref, at = basis_part(h1_refs, whole.start)
            basis_ref, at = basis_part(basis_refs, whole.start)
            here = slice(at, at + chunk)
            products = [sum(cots[c] * h1_ref[c, here, :] for c in range(outs))]
            products += [cots[c] * h1_ref[outs + c, here, :] for c in range(outs - 1)]
            for c in range(outs):
                sums[c] = sums[c] + jnp.sum((u * products[c]).reshape(chunk // 8, 8, width), 0)
            slot_ref[whole, :] = sum(w_rows[c] * products[c] for c in range(outs)).astype(bf16)
            moved = sum(cots[c] * basis_ref[c, here, :] for c in range(outs))
            moved_ref[whole, :] = moved.astype(bf16)
    for c in range(outs):
        sums_ref[c] = sums[c]
    w_grad_ref[...] = nn_dot(inputs_ref[...], slot_ref[...])


def flipped(a, b):
    return nn_dot(b, a)


def network_kernel(*refs, parts, rows):
    part_refs, refs = refs[: 3 * parts], refs[3 * parts :]
    w_grad_ref, sums_ref, low_ref, small_ref = refs
    by_sample = jnp.concatenate([part_refs[3 * i][...] for i in range(parts)], 0)
    samples, width = by_sample.shape
    outs = sums_ref.shape[0]
    w = low_ref[rows["w"], :]
    sample = low_ref[rows["sample"], :].astype(f32)
    sample_t = jnp.concatenate([sample] * (128 // samples), 0).T[:, :samples]
    small_ref[:samples, :] = split_dot(by_sample, w, nt_dot)
    small_ref[samples : samples + width, :] = w_grad_ref[...] + split_dot(
        by_sample, sample_t.astype(bf16), flipped
    )
    at = samples + width
    small_ref[at : at + 1, :] = jnp.sum(by_sample, 0, keepdims=True)
    lane128 = lax.broadcasted_iota(jnp.int32, (1, 128), 1)
    bias = jnp.zeros((1, 128), f32)
    for c in range(outs):
        total = sums_ref[c] + sum(part_refs[3 * i + 1][c] for i in range(parts))
        small_ref[at + 1 + c : at + 2 + c, :] = jnp.sum(total, 0, keepdims=True)
        row = sum(part_refs[3 * i + 2][c : c + 1, :] for i in range(parts))
        bias = bias + jnp.where(lane128 == c, jnp.sum(row, 1, keepdims=True), 0.0)
    small_ref[at + 1 + outs : at + 2 + outs, :] = bias
    rest = small_ref.shape[0] - (at + 2 + outs)
    small_ref[at + 2 + outs :, :] = jnp.zeros((rest, width), f32)


def ray_sum_kernel(keep_ref, got_ref, cot_ref, out_ref, color_ref):
    out_ref[...] = keep_ref[...] + got_ref[...].astype(f32)
    channels, own = color_ref.shape
    rays = cot_ref.shape[1]
    me = lax.axis_index("slab")
    r_i = lax.broadcasted_iota(jnp.int32, (rays, own), 0)
    c_i = lax.broadcasted_iota(jnp.int32, (rays, own), 1)
    pick = jnp.where(r_i == c_i + me * own, 1.0, 0.0).astype(bf16)
    color = cot_ref[channels + 1 : 2 * channels + 1, :]
    high = color.astype(bf16)
    middle = (color - high.astype(f32)).astype(bf16)
    low = (color - high.astype(f32) - middle.astype(f32)).astype(bf16)
    picked = nn_dot(jnp.concatenate([high, middle, low], 0), pick)
    color_ref[...] = picked[:channels] + picked[channels : 2 * channels] + picked[2 * channels :]


def finish_kernel(
    ray_ref,
    color_ref,
    brick_ref,
    sent_ref,
    got_ref,
    color_out_ref,
    ray_out_ref,
    brick_out_ref,
    sample_ref,
    w_ref,
    b_ref,
    w_out_ref,
    b_out_ref,
):
    ray_out_ref[...] = ray_ref[...]
    color_out_ref[...] = color_ref[...]
    part = brick_ref.shape[0]
    brick_out_ref[...] = brick_ref[...] + got_ref[:part, :].astype(f32)
    small = sent_ref[part:, :].astype(f32) + got_ref[part:, :].astype(f32)
    samples, width = sample_ref.shape
    outs = w_out_ref.shape[0]
    at = samples + width
    sample_ref[...] = small[:samples]
    w_ref[...] = small[samples:at]
    b_ref[...] = small[at : at + 1]
    w_out_ref[...] = small[at + 1 : at + 1 + outs]
    b_out_ref[...] = small[at + 1 + outs : at + 2 + outs, :outs]


def body(
    ray_code,
    direction,
    target,
    brick_code,
    sample_code,
    w_hidden,
    b_hidden,
    w_out,
    b_out,
    brick_ids,
    occupancy,
):
    owners = lax.axis_size("slab")
    shares = lax.axis_size("ray")
    me = lax.axis_index("slab")
    ids = brick_ids[0]
    slots, rays = ids.shape
    total = slots * rays
    bricks, width = brick_code.shape[1:]
    samples = sample_code.shape[1]
    outs = w_out.shape[1]
    channels = outs - 1
    count = outs + channels

    def shaped(*shape):
        return jax.ShapeDtypeStruct(shape, f32)

    def shaped16(*shape):
        return jax.ShapeDtypeStruct(shape, bf16)

    rows = low_rows(width, samples)
    lines = line_rows(slots, channels)
    earlier, later = call(
        order_kernel,
        (shaped16(samples, samples), shaped16(samples, samples)),
        "order",
        flops=1 << 34,
    )()
    gathered, low, packed, w_t, s, wide, left = call(
        functools.partial(prepare_kernel, rows=rows, lines=lines),
        (
            shaped16(*ray_code.shape),
            shaped16(rows["w_out"].stop, width),
            shaped(lines["b_out"] + 1, rays),
            shaped16(width, width),
            shaped(samples, width),
            shaped16(samples, width, 128),
            shaped16(outs * 8, 8 * width),
        ),
        "prepare",
        flops=1 << 31,
    )(
        ray_code,
        w_hidden[0],
        sample_code[0],
        w_out[0],
        ids,
        occupancy,
        direction[None],
        target,
        b_hidden,
        b_out,
    )
    turns = gather_bits(owners, ray_code.shape[0])
    other = swap(ray_code, "slab", owners, 1 << turns[0])
    other, lines_later = lax.optimization_barrier((other, packed))
    for b in turns[1:]:
        gathered = jnp.concatenate([gathered, other], 0)
        other = swap(gathered, "slab", owners, 1 << b)
    chosen, project = call(
        chosen_kernel,
        (shaped16(width, total), shaped(width, total)),
        "chosen",
        flops=1 << 29,
    )(lines_later, brick_code[0], w_t)
    passes = ()
    kept = []
    uts = []
    for second, part in enumerate((gathered, other)):
        wide_rays = rays if second else rays // 2
        seg, kept_half, ut_half, ray_sorted = call(
            functools.partial(forward_kernel, owners=owners, second=second, lines=lines),
            (
                shaped(outs, wide_rays),
                shaped(2 * outs, samples, total // 2),
                shaped16(width, total // 2),
                shaped16(wide_rays, width),
            ),
            "forward",
            scratch=(
                pltpu.VMEM((rays // 2, width), bf16),
                pltpu.VMEM((outs, samples, total // 2), f32),
            ),
            flops=1 << 30,
        )(part, project, w_t, wide, left, packed, earlier, *passes)
        passes = (seg, ray_sorted)
        kept.append(kept_half)
        uts.append(ut_half)

    coef, turned, u = call(
        functools.partial(coefficient_kernel, owners=owners, lines=lines),
        (
            shaped(count, samples, total),
            shaped16(count, total, 128),
            shaped16(total, width),
        ),
        "coefficients",
        flops=1 << 30,
    )(seg, *kept, *uts, later, packed)

    forward = packed[lines["direction"]][None] == 0.0
    group = (seg[:channels], seg[channels:])
    received = []
    basis = []
    bits = bits_of(owners)
    cuts = basis_cuts(total, bits)
    pieces = len(cuts) - 1
    turned_later, chosen_later = turned, chosen
    for b in range(bits):
        sent = jnp.concatenate(group, 0) if b > 0 else seg
        other = swap(sent, "slab", owners, 1 << b)
        if b < pieces:
            piece = cuts[b + 1] - cuts[b]
            basis.append(
                call(
                    functools.partial(basis_kernel, first=cuts[b], row_of=rows),
                    (shaped(count, piece, width), shaped(outs, piece, width)),
                    "basis",
                    flops=1 << 29,
                )(turned_later, u, s, low)
            )
        if b + 1 == bits:
            inputs = call(inputs_kernel, shaped16(width, total), "inputs", flops=1 << 20)(
                chosen_later, ray_sorted
            )
            other, inputs = lax.optimization_barrier((other, inputs))
        other, turned_later, chosen_later = lax.optimization_barrier(
            (other, turned_later, chosen_later)
        )
        received.append(other)
        theirs = (other[:channels], other[channels:])
        upper = ((me >> b) & 1) == 1
        first = jax.tree.map(lambda a, b: jnp.where(upper, b, a), group, theirs)
        second = jax.tree.map(lambda a, b: jnp.where(upper, a, b), group, theirs)
        group = merge(first, second, forward)

    h1, moved_basis = zip(*basis)
    ray_keep, ray_send, cots, spread = call(
        functools.partial(middle_kernel, owners=owners, pieces=pieces, lines=lines),
        (
            shaped(rays // 2, width),
            shaped16(rays // 2, width),
            shaped(8, rays),
            shaped(rays, outs * width),
        ),
        "middle",
        scratch=(pltpu.VMEM((rays, width), f32),),
        flops=1 << 29,
    )(seg, *received, *moved_basis, packed)
    moved, w_grad, sums = call(
        functools.partial(slots_kernel, pieces=pieces, rows=rows),
        (
            shaped16(total, width),
            shaped(width, width),
            shaped(outs, 8, width),
        ),
        "slots",
        scratch=(pltpu.VMEM((total, width), bf16),),
        flops=1 << 20,
    )(*h1, *moved_basis, spread, u, inputs, low)

    def merged(keep, got):
        half = keep.shape[0] // 2
        return keep[:half] + got[:half].astype(f32), (keep[half:] + got[half:].astype(f32)).astype(bf16)

    def part_by_sample(i, cots):
        return call(
            functools.partial(sample_kernel, first=i * samples // parts, rows=rows),
            (
                shaped(samples // parts, width),
                shaped(outs, 8, width),
                shaped(outs, 128),
            ),
            "by_sample",
            scratch=(pltpu.VMEM((samples // parts // 8, outs * 8, total), bf16),),
            flops=1 << 20,
        )(cots, coef, u, s, low)

    def by_brick(first, moved, shape):
        return call(
            functools.partial(brick_kernel, first=first, shares=shares),
            shape,
            "bricks",
            flops=1 << 20,
        )(packed, moved)

    parts = 2
    by_part = []
    later_cots = cots
    for b in range(bits):
        if b + 1 == bits:
            small_rows = -(-(samples + width + 2 + outs) // 16) * 16
            small = call(
                functools.partial(network_kernel, parts=parts, rows=rows),
                shaped(small_rows, width),
                "network",
                flops=1 << 20,
            )(*by_part, w_grad, sums, low)
            ray_send, small = lax.optimization_barrier((ray_send, small))
        ray_got = swap(ray_send, "slab", owners, 1 << halving_bits(owners)[b])
        if b < parts:
            by_part += part_by_sample(b, later_cots)
        if b == 1:
            brick_sent = by_brick(shares // 2, moved, shaped16(bricks // 2, width))
            w_grad, brick_sent = lax.optimization_barrier((w_grad, brick_sent))
        if b + 1 < bits:
            held = (ray_got, later_cots, moved, by_part)
            ray_got, later_cots, moved, by_part = lax.optimization_barrier(held)
            ray_keep, ray_send = merged(ray_keep, ray_got)

    small = small.astype(bf16)
    for b in reversed(range(bits_of(shares))):
        sent = jnp.concatenate([brick_sent, small], 0)
        if 1 << (b + 1) == shares:
            sent, moved = lax.optimization_barrier((sent, moved))
            brick = by_brick(0, moved, shaped(bricks // 2, width))
        other = swap(sent, "ray", shares, 1 << b)
        if b > 0:
            half = brick.shape[0]
            small = (sent[half:].astype(f32) + other[half:].astype(f32)).astype(bf16)
            brick_sent = (brick[half // 2 :] + other[half // 2 : half].astype(f32)).astype(bf16)
            brick = brick[: half // 2] + other[: half // 2].astype(f32)
    ray_sum, color_own = call(
        ray_sum_kernel,
        (shaped(rays // owners, width), shaped(channels, rays // owners)),
        "ray_sum",
        flops=1 << 31,
    )(ray_keep, ray_got, cots)
    color_out, ray_out, brick_out, sample_out, w_grad, b_grad, w_out_grad, b_out_grad = call(
        finish_kernel,
        (
            shaped(channels, rays // owners),
            shaped(rays // owners, width),
            shaped(bricks // shares, width),
            shaped(samples, width),
            shaped(width, width),
            shaped(1, width),
            shaped(outs, width),
            shaped(1, outs),
        ),
        "finish",
    )(ray_sum, color_own, brick, sent, other)
    return (
        color_out,
        ray_out,
        brick_out[None],
        sample_out[None],
        w_grad[None],
        b_grad,
        w_out_grad[None],
        b_out_grad,
    )


def solution(mesh):
    in_specs = (
        P(("ray", "slab"), None),
        P("ray"),
        P(None, "ray"),
        P("slab", None, None),
        P("slab", None, None),
        P("slab", None, None),
        P("slab", None),
        P("slab", None, None),
        P("slab", None),
        P("slab", None, "ray"),
        P("slab", "ray"),
    )
    out_specs = (
        P(None, ("ray", "slab")),
        P(("ray", "slab"), None),
        P("slab", "ray", None),
        P("slab", None, None),
        P("slab", None, None),
        P("slab", None),
        P("slab", None, None),
        P("slab", None),
    )
    return jax.shard_map(body, mesh=mesh, in_specs=in_specs, out_specs=out_specs, check_vma=False)
```

```python
import functools

import jax
import jax.numpy as jnp
from jax import lax
from jax.experimental import pallas as pl
from jax.experimental.pallas import tpu as pltpu
from jax.sharding import PartitionSpec as P

step_length = 0.002
f32 = jnp.float32
bf16 = jnp.bfloat16
vmem_bytes = 24 * 1024 * 1024


def bits_of(count):
    bits = count.bit_length() - 1
    assert count == 1 << bits
    return bits


def gather_bits(owners, own):
    last = max(bits_of(128 // own), 0) if own < 128 else 0
    return [b for b in reversed(range(bits_of(owners))) if b != last] + [last]


def gather_order(owners, own):
    order = [0]
    for b in gather_bits(owners, own)[:-1]:
        order = order + [t ^ (1 << b) for t in order]
    return order


def halving_bits(owners):
    bits = list(range(bits_of(owners)))
    return bits[1:-1] + bits[:1] + bits[1:][-1:]


def halving_order(owners):
    order = [0]
    for b in reversed(halving_bits(owners)):
        order = order + [t ^ (1 << b) for t in order]
    return order


def nt_dot(a, b, precision=None):
    return lax.dot_general(
        a, b, (((1,), (1,)), ((), ())), precision=precision, preferred_element_type=f32
    )


def nn_dot(a, b, precision=None):
    return jnp.dot(a, b, precision=precision, preferred_element_type=f32)


def swap(array, axis, size, distance):
    return lax.ppermute(array, axis, [(i, i ^ distance) for i in range(size)])


def sum_dot(ones, b):
    high = b.astype(bf16)
    low = (b - high.astype(f32)).astype(bf16)
    return nn_dot(ones, high) + nn_dot(ones, low)


def call(kernel, out_shape, name, scratch=(), flops=0):
    def run(*operands):
        return pl.pallas_call(
            kernel,
            out_shape=out_shape,
            in_specs=[pl.BlockSpec(memory_space=pltpu.VMEM)] * len(operands),
            out_specs=jax.tree.map(lambda _: pl.BlockSpec(memory_space=pltpu.VMEM), out_shape),
            scratch_shapes=list(scratch),
            compiler_params=pltpu.CompilerParams(vmem_limit_bytes=vmem_bytes),
            cost_estimate=pl.CostEstimate(flops=flops, bytes_accessed=1 << 10, transcendentals=0),
            name=name,
        )(*operands)

    return run


def low_rows(width, samples):
    starts = {"w": 0, "sample": width, "w_out": width + samples}
    sizes = {"w": width, "sample": samples, "w_out": 16}
    return {name: slice(at, at + sizes[name]) for name, at in starts.items()}


def line_rows(slots, channels):
    return {
        "ids": 0,
        "occ": slots,
        "direction": slots + 1,
        "target": slots + 2,
        "b_out": slots + 2 + channels,
    }


def order_kernel(earlier_ref, later_ref):
    shape = earlier_ref.shape
    r_i = lax.broadcasted_iota(jnp.int32, shape, 0)
    c_i = lax.broadcasted_iota(jnp.int32, shape, 1)
    earlier_ref[...] = jnp.where(c_i < r_i, 1.0, 0.0).astype(bf16)
    later_ref[...] = jnp.where(c_i > r_i, 1.0, 0.0).astype(bf16)


def chosen_kernel(lines_ref, brick_ref, w_t_ref, chosen_ref, project_ref):
    total = chosen_ref.shape[1]
    rays = lines_ref.shape[1]
    bricks = brick_ref.shape[0]
    brick_t = brick_ref[...].astype(f32).T.astype(bf16)
    w_t = w_t_ref[...]
    row = lax.broadcasted_iota(jnp.int32, (bricks, rays), 0).astype(f32)
    for k in range(total // rays):
        one_hot = jnp.where(row == lines_ref[k : k + 1, :], 1.0, 0.0).astype(bf16)
        chosen = nn_dot(brick_t, one_hot).astype(bf16)
        chosen_ref[:, k * rays : (k + 1) * rays] = chosen
        project_ref[:, k * rays : (k + 1) * rays] = nn_dot(w_t, chosen)


def prepare_kernel(
    ray_ref,
    w_ref,
    sample_ref,
    w_out_ref,
    ids_ref,
    occ_ref,
    direction_ref,
    target_ref,
    b_ref,
    b_out_ref,
    own_ref,
    low_ref,
    lines_ref,
    w_t_ref,
    s_ref,
    wide_ref,
    left_ref,
    *,
    rows,
    lines,
):
    slots, rays = ids_ref.shape
    width = w_t_ref.shape[0]
    samples = s_ref.shape[0]
    outs = w_out_ref.shape[0]
    own_ref[...] = ray_ref[...]
    w = w_ref[...]
    w_out = w_out_ref[...].astype(f32)
    low_ref[rows["w"], :] = w
    low_ref[rows["sample"], :] = sample_ref[...]
    low_ref[rows["w_out"], :] = jnp.concatenate(
        [w_out, jnp.zeros((16 - outs, width), f32)], 0
    ).astype(bf16)
    lines_ref[:slots, :] = ids_ref[...].astype(f32)
    lines_ref[lines["occ"] : lines["occ"] + 1, :] = occ_ref[...].astype(f32)
    lines_ref[lines["direction"] : lines["direction"] + 1, :] = direction_ref[...].astype(f32)
    lines_ref[lines["target"] : lines["target"] + outs - 1, :] = target_ref[...]
    lines_ref[lines["b_out"] : lines["b_out"] + 1, :outs] = b_out_ref[...]
    w_t = w.astype(f32).T.astype(bf16)
    w_t_ref[...] = w_t
    s = nn_dot(sample_ref[...], w) + b_ref[...]
    s_ref[...] = s.astype(bf16).astype(f32)
    s_t = jnp.concatenate([s] * (128 // samples), 0).T
    for j in range(samples):
        wide_ref[j] = jnp.broadcast_to(s_t[:, j : j + 1], (width, 128)).astype(bf16)
    w_rows = jnp.concatenate(
        [jnp.broadcast_to(w_out[c : c + 1, :], (8, width)) for c in range(outs)], 0
    )
    row8 = lax.broadcasted_iota(jnp.int32, (outs * 8, width), 0) % 8
    for i in range(8):
        left_ref[:, i * width : (i + 1) * width] = jnp.where(row8 == i, w_rows, 0.0).astype(bf16)


def forward_kernel(*refs, owners, second, lines):
    ray_ref, project_ref, w_t_ref, wide_ref, left_ref, lines_ref, earlier_ref, *refs = refs
    if second:
        before_refs, refs = refs[:2], refs[2:]
    seg_ref, kept_ref, ut_ref, sorted_ref, order_ref, raw_ref = refs
    width, total = project_ref.shape
    samples = wide_ref.shape[0]
    outs = seg_ref.shape[0]
    half, rays = ray_ref.shape[0], lines_ref.shape[1]
    slots = total // rays
    chunk = 128
    own = 2 * half // owners
    last = gather_bits(owners, own)[-1]
    me = lax.axis_index("slab")
    side = (me >> last) & 1

    def whole(n, k=0, side=side):
        return pl.ds(pl.multiple_of(k * rays + (2 * n + side) * chunk, chunk), chunk)

    if second:
        for n in range(half // chunk):
            part = slice(n * chunk, (n + 1) * chunk)
            seg_ref[:, whole(n)] = before_refs[0][:, part]
            sorted_ref[whole(n), :] = before_refs[1][part, :]
        side = 1 - side

    def spot(n, k=0):
        at = k * half + n * chunk
        return whole(n, k, side) if second else slice(at, at + chunk)

    flip = (1 << last) if second else 0
    for i, t in enumerate(gather_order(owners, own)):
        owner = me ^ (t ^ flip)
        place = ((owner >> (last + 1)) << last) | (owner & ((1 << last) - 1))
        order_ref[pl.ds(pl.multiple_of(place * own, own), own), :] = ray_ref[
            i * own : (i + 1) * own, :
        ]
    ray_t = nt_dot(w_t_ref[...], order_ref[...])
    for n in range(half // chunk):
        sorted_ref[spot(n), :] = order_ref[n * chunk : (n + 1) * chunk, :]
        for k in range(slots):
            part = project_ref[:, whole(n, k, side)] + ray_t[:, n * chunk : (n + 1) * chunk]
            ut_ref[:, k * half + n * chunk : k * half + (n + 1) * chunk] = part.astype(bf16)
    b_out = [lines_ref[lines["b_out"], c] for c in range(outs)]

    def shade(n):
        ut = [ut_ref[:, k * half + n * chunk : k * half + (n + 1) * chunk] for k in range(slots)]
        ut = jnp.concatenate(ut, 1)
        for block in range(samples // 8):
            acc = None
            for i in range(4):
                parts = []
                for h in range(2):
                    column = wide_ref[block * 8 + 2 * i + h]
                    column = jnp.concatenate([column] * slots, 1)
                    parts.append(jnp.maximum(ut + column, 0))
                left = left_ref[:, 2 * i * width : 2 * (i + 1) * width]
                term = nn_dot(left, jnp.concatenate(parts, 0))
                acc = term if acc is None else acc + term
            for c in range(outs):
                raw_ref[c, n, block * 8 : block * 8 + 8, :] = acc[c * 8 : c * 8 + 8, :] + b_out[c]

    for n in range(half // chunk):
        shade(n)
    earlier = earlier_ref[...]
    occ_row = lines["occ"]
    for n in range(half // chunk):
        occ = lines_ref[occ_row : occ_row + 1, whole(n, 0, side)]
        raws = [
            raw_ref[0, n, :, k * chunk : (k + 1) * chunk] for k in range(slots)
        ]
        occupied = [(k < occ).astype(f32) for k in range(slots)]
        opticals = [
            step_length * (jnp.maximum(x, 0.0) + jnp.log1p(jnp.exp(-jnp.abs(x)))) * o
            for x, o in zip(raws, occupied)
        ]
        enters = sum_dot(earlier, jnp.concatenate(opticals, 1))
        before = jnp.zeros((1, chunk), f32)
        colors = [jnp.zeros((1, chunk), f32)] * (outs - 1)
        for k in range(slots):
            local = slice(k * half + n * chunk, k * half + (n + 1) * chunk)
            optical = opticals[k]
            entered = enters[:, k * chunk : (k + 1) * chunk] + before
            before = before + jnp.sum(optical, 0, keepdims=True)
            tanh = jnp.tanh(0.5 * optical)
            weight = jnp.exp(-entered) * (2.0 * tanh / (1.0 + tanh))
            for c in range(outs - 1):
                shading = jax.nn.sigmoid(raw_ref[c + 1, n, :, k * chunk : (k + 1) * chunk])
                light = weight * shading
                colors[c] = colors[c] + jnp.sum(light, 0, keepdims=True)
                kept_ref[c, :, local] = shading
                kept_ref[outs + c, :, local] = light
            kept_ref[outs - 1, :, local] = entered + optical
            kept_ref[2 * outs - 1, :, local] = raws[k]
        place = spot(n)
        for c in range(outs - 1):
            seg_ref[c : c + 1, place] = colors[c]
        seg_ref[outs - 1 : outs, place] = jnp.exp(-before)


def coefficient_kernel(
    seg_ref,
    first_ref,
    second_ref,
    first_ut_ref,
    second_ut_ref,
    later_ref,
    lines_ref,
    coef_ref,
    turned_ref,
    u_ref,
    *,
    owners,
    lines,
):
    outs, rays = seg_ref.shape
    samples, local = first_ref.shape[1:]
    half = rays // 2
    slots = local // half
    last = gather_bits(owners, rays // owners)[-1]
    side = (lax.axis_index("slab") >> last) & 1
    later = later_ref[...]
    chunk = 128

    def keep(index, lanes, value):
        coef_ref[index, :, lanes] = value
        value = value.astype(bf16)
        turned_ref[index, lanes, :] = jnp.concatenate([value] * (128 // samples), 0).T

    for kept_ref, ut_ref, where in (
        (first_ref, first_ut_ref, side),
        (second_ref, second_ut_ref, 1 - side),
    ):
        for n in range(half // chunk):
            base = (2 * n + where) * chunk
            through = seg_ref[outs - 1 : outs, pl.ds(pl.multiple_of(base, chunk), chunk)]
            occ = lines_ref[lines["occ"] : lines["occ"] + 1, pl.ds(pl.multiple_of(base, chunk), chunk)]
            after = [jnp.zeros((1, chunk), f32)] * (outs - 1)
            for k in reversed(range(slots)):
                lanes = pl.ds(pl.multiple_of(k * rays + base, chunk), chunk)
                at = slice(k * half + n * chunk, k * half + (n + 1) * chunk)
                u_ref[lanes, :] = ut_ref[:, at].T
                passed = jnp.exp(-kept_ref[outs - 1, :, at])
                occupied = (k < occ).astype(f32)
                density = step_length * occupied * jax.nn.sigmoid(kept_ref[2 * outs - 1, :, at])
                lights = [kept_ref[outs + c, :, at] for c in range(outs - 1)]
                behinds = sum_dot(later, jnp.concatenate(lights, 1))
                for c in range(outs - 1):
                    shading = kept_ref[c, :, at]
                    light = lights[c]
                    behind = behinds[:, c * chunk : (c + 1) * chunk] + after[c]
                    after[c] = after[c] + jnp.sum(light, 0, keepdims=True)
                    keep(c, lanes, density * (shading * passed - behind))
                    keep(outs + c, lanes, light * (1.0 - shading))
                keep(outs - 1, lanes, density * through)


def basis_kernel(turned_ref, u_ref, s_ref, low_ref, h1_ref, moved_ref, *, first, row_of):
    count, rays, width = h1_ref.shape
    samples = s_ref.shape[0]
    negative = (-s_ref[...]).astype(bf16)
    one = jnp.ones((samples, width), bf16)
    zero = jnp.zeros((samples, width), bf16)
    lane = lax.broadcasted_iota(jnp.int32, (8, 8 * samples), 1) // samples
    row = lax.broadcasted_iota(jnp.int32, (8, 8 * samples), 0)
    block_mask = lane == row
    repeat = 8 * samples // 128
    step = 128
    outs = moved_ref.shape[0]
    w = low_ref[row_of["w"], :]
    w_out = low_ref[row_of["w_out"], :].astype(f32)
    w_rows = [w_out[c : c + 1, :] for c in range(outs)]

    def slot_block(block, carry):
        for h in range(step // 16):
            base = pl.multiple_of(block * step + h * 16, 16)
            u16 = u_ref[pl.ds(first + base, 16), :]
            rows16 = [turned_ref[c, pl.ds(first + base, 16), :].astype(f32) for c in range(count)]
            for q in range(2):
                at = pl.multiple_of(block * step + h * 16 + q * 8, 8)
                left = [
                    jnp.where(
                        block_mask,
                        jnp.concatenate([rows16[c][q * 8 : q * 8 + 8]] * repeat, 1),
                        0.0,
                    )
                    for c in range(count)
                ]
                left = jnp.concatenate(left, 0).astype(bf16)
                tiles = [
                    jnp.where(
                        jnp.broadcast_to(u16[q * 8 + i : q * 8 + i + 1, :], (samples, width))
                        > negative,
                        one,
                        zero,
                    )
                    for i in range(8)
                ]
                h1 = nn_dot(left, jnp.concatenate(tiles, 0))
                for c in range(count):
                    h1_ref[c, pl.ds(at, 8), :] = h1[c * 8 : c * 8 + 8, :]
        return carry

    lax.fori_loop(0, rays // step, slot_block, 0)
    for c in range(outs):
        grad = w_rows[0] * h1_ref[c]
        if c + 1 < outs:
            grad = grad + w_rows[c + 1] * h1_ref[outs + c]
        moved_ref[c] = nt_dot(grad.astype(bf16), w)


def basis_cuts(total, bits):
    eighth = total // 8
    return [0, 2 * eighth, 5 * eighth, total] if bits > 2 else [0, total]


def basis_part(refs, row):
    for ref in refs:
        if row < ref.shape[1]:
            return ref, row
        row -= ref.shape[1]


def merge(first, second, forward):
    fc, ft = first
    sc, st = second
    return jnp.where(forward, fc + ft * sc, sc + st * fc), ft * st


def middle_kernel(*refs, owners, pieces, lines):
    bits = bits_of(owners)
    seg_ref, refs = refs[0], refs[1:]
    got_refs, refs = refs[:bits], refs[bits:]
    moved_refs, refs = refs[:pieces], refs[pieces:]
    lines_ref, keep_ref, send_ref, cot_ref, spread_ref, ray_ref = refs
    me = lax.axis_index("slab")
    outs = seg_ref.shape[0]
    channels = outs - 1
    rays = lines_ref.shape[1]
    width = moved_refs[0].shape[2]
    slots = sum(ref.shape[1] for ref in moved_refs) // rays
    forward = lines_ref[lines["direction"] : lines["direction"] + 1, :] == 0.0
    target = lines_ref[lines["target"] : lines["target"] + channels, :]

    def pair(values):
        return values[:channels, :], values[channels : channels + 1, :]

    low = high = None
    for b in reversed(range(bits)):
        piece = pair(got_refs[b][...])
        is_low = ((me >> b) & 1) == 1
        piece = (jnp.where(is_low, piece[0], 0.0), jnp.where(is_low, piece[1], 1.0))
        low = piece if low is None else merge(low, piece, forward)
    for b in range(bits):
        piece = pair(got_refs[b][...])
        is_high = ((me >> b) & 1) == 0
        piece = (jnp.where(is_high, piece[0], 0.0), jnp.where(is_high, piece[1], 1.0))
        high = piece if high is None else merge(high, piece, forward)
    seg_color, seg_trans = pair(seg_ref[...])
    before_color = jnp.where(forward, low[0], high[0])
    before_trans = jnp.where(forward, low[1], high[1])
    after_color = jnp.where(forward, high[0], low[0])
    color = before_color + before_trans * (seg_color + seg_trans * after_color)
    residual = color - target
    color_cot = before_trans * residual
    trans_cot = -before_trans * jnp.sum(after_color * residual, 0, keepdims=True)
    cot_ref[:channels, :] = color_cot
    cot_ref[channels:outs, :] = trans_cot
    cot_ref[outs : outs + channels, :] = color
    cot_ref[outs + channels :, :] = jnp.zeros((8 - outs - channels, rays), f32)
    chunk = 128
    values = jnp.concatenate([color_cot, trans_cot], 0)
    rounded = values.astype(bf16).astype(f32)
    values = jnp.concatenate([rounded, values - rounded], 0)
    row = lax.broadcasted_iota(jnp.int32, (2 * outs, outs * width), 0) % outs
    lane = lax.broadcasted_iota(jnp.int32, (2 * outs, outs * width), 1) // width
    spread = jnp.where(row == lane, 1.0, 0.0).astype(bf16)
    for n in range(rays // chunk):
        these = slice(n * chunk, (n + 1) * chunk)
        spread_ref[these, :] = nn_dot(values[:, these].T.astype(bf16), spread)
        grad = None
        for c in range(outs):
            whole = None
            for k in range(slots):
                ref, at = basis_part(moved_refs, k * rays + n * chunk)
                part = ref[c, at : at + chunk, :]
                whole = part if whole is None else whole + part
            term = spread_ref[these, c * width : (c + 1) * width] * whole
            grad = term if grad is None else grad + term
        ray_ref[these, :] = grad
    own = rays // owners
    for i, t in enumerate(halving_order(owners)):
        place = pl.multiple_of((me ^ t) * own, own)
        if i < owners // 2:
            keep_ref[i * own : (i + 1) * own, :] = ray_ref[pl.ds(place, own), :]
        else:
            at = i * own - rays // 2
            send_ref[at : at + own, :] = ray_ref[pl.ds(place, own), :].astype(bf16)


def brick_kernel(lines_ref, moved_ref, out_ref, *, first, shares):
    share = lax.axis_index("ray")
    rays = lines_ref.shape[1]
    total, width = moved_ref.shape
    owners = shares // 2
    part = out_ref.shape[0] // owners
    moved = moved_ref[...]
    row = lax.broadcasted_iota(jnp.int32, (part, rays), 0).astype(f32)
    for i in range(owners):
        begin = ((share ^ (first + i)) * part).astype(f32)
        acc = jnp.zeros((part, width), f32)
        for k in range(total // rays):
            one_hot = jnp.where(row + begin == lines_ref[k : k + 1, :], 1.0, 0.0).astype(bf16)
            acc = acc + nn_dot(one_hot, moved[k * rays : (k + 1) * rays])
        out_ref[i * part : (i + 1) * part, :] = acc.astype(out_ref.dtype)


def sample_kernel(
    cot_ref, coef_ref, u_ref, s_ref, low_ref, by_sample_ref, sums_ref, bias_ref, g_ref, *, first, rows
):
    outs = sums_ref.shape[0]
    channels = outs - 1
    rays = cot_ref.shape[1]
    total, width = u_ref.shape
    samples = by_sample_ref.shape[0]
    bias_sums = [jnp.zeros((1, 128), f32)] * outs
    for n in range(total // 128):
        lanes = slice(n * 128, n * 128 + 128)
        at = (n * 128) % rays
        cots = [cot_ref[c : c + 1, at : at + 128] for c in range(outs)]
        grads = [sum(cots[c] * coef_ref[c, first : first + samples, lanes] for c in range(outs))]
        for c in range(channels):
            grads.append(cots[c] * coef_ref[outs + c, first : first + samples, lanes])
        for c in range(outs):
            bias_sums[c] = bias_sums[c] + jnp.sum(grads[c], 0, keepdims=True)
        for j in range(0, samples, 8):
            g_ref[j // 8, :, lanes] = jnp.concatenate([g[j : j + 8] for g in grads], 0).astype(bf16)
    w_out = low_ref[rows["w_out"], :].astype(f32)
    w_rows = [w_out[c : c + 1, :] for c in range(outs)]
    row8 = lax.broadcasted_iota(jnp.int32, (8, width), 0)

    def sample_block(block, sums):
        left = g_ref[block]
        s8 = s_ref[pl.ds(pl.multiple_of(first + block * 8, 8), 8), :]
        acc = [jnp.zeros((8, width), f32)] * outs
        for i in range(0, 8, 2):
            edges = [(-s8[i + h : i + h + 1, :]).astype(bf16) for h in range(2)]
            h2 = None
            for n in range(total // 256):
                u = u_ref[n * 256 : n * 256 + 256, :]
                live = [
                    jnp.where(
                        u > jnp.broadcast_to(edge, u.shape),
                        jnp.ones(u.shape, bf16),
                        jnp.zeros(u.shape, bf16),
                    )
                    for edge in edges
                ]
                term = nn_dot(left[:, n * 256 : n * 256 + 256], jnp.concatenate(live, 1))
                h2 = term if h2 is None else h2 + term
            for c in range(outs):
                for h in range(2):
                    piece = h2[c * 8 : c * 8 + 8, h * width : (h + 1) * width]
                    acc[c] = acc[c] + jnp.where(row8 == i + h, piece, 0.0)
        by_sample_ref[pl.ds(pl.multiple_of(block * 8, 8), 8), :] = sum(
            w_rows[c] * acc[c] for c in range(outs)
        )
        return tuple(sums[c] + s8 * acc[c] for c in range(outs))

    sums = [jnp.zeros((8, width), f32)] * outs
    sums = lax.fori_loop(0, samples // 8, sample_block, tuple(sums), unroll=4)
    for c in range(outs):
        sums_ref[c] = sums[c]
        bias_ref[c : c + 1, :] = bias_sums[c]


def inputs_kernel(chosen_ref, sorted_ref, inputs_ref):
    total = chosen_ref.shape[1]
    ray_t = sorted_ref[...].astype(f32).T
    inputs = chosen_ref[...].astype(f32) + jnp.concatenate([ray_t] * (total // ray_t.shape[1]), 1)
    inputs_ref[...] = inputs.astype(bf16)


def slots_kernel(*refs, pieces, rows):
    h1_refs, refs = refs[:pieces], refs[pieces:]
    basis_refs, refs = refs[:pieces], refs[pieces:]
    spread_ref, u_ref, inputs_ref, low_ref, *refs = refs
    moved_ref, w_grad_ref, sums_ref, slot_ref = refs
    rays = spread_ref.shape[0]
    total, width = u_ref.shape
    outs = sums_ref.shape[0]
    w_out = low_ref[rows["w_out"], :].astype(f32)
    w_rows = [w_out[c : c + 1, :] for c in range(outs)]
    chunk = 32
    sums = [jnp.zeros((8, width), f32)] * outs
    for n in range(rays // chunk):
        these = slice(n * chunk, (n + 1) * chunk)
        cots = [spread_ref[these, c * width : (c + 1) * width] for c in range(outs)]
        for k in range(total // rays):
            whole = slice(k * rays + n * chunk, k * rays + (n + 1) * chunk)
            u = u_ref[whole, :].astype(f32)
            h1_ref, at = basis_part(h1_refs, whole.start)
            basis_ref, at = basis_part(basis_refs, whole.start)
            here = slice(at, at + chunk)
            products = [sum(cots[c] * h1_ref[c, here, :] for c in range(outs))]
            products += [cots[c] * h1_ref[outs + c, here, :] for c in range(outs - 1)]
            for c in range(outs):
                sums[c] = sums[c] + jnp.sum((u * products[c]).reshape(chunk // 8, 8, width), 0)
            slot_ref[whole, :] = sum(w_rows[c] * products[c] for c in range(outs)).astype(bf16)
            moved = sum(cots[c] * basis_ref[c, here, :] for c in range(outs))
            moved_ref[whole, :] = moved.astype(bf16)
    for c in range(outs):
        sums_ref[c] = sums[c]
    w_grad_ref[...] = nn_dot(inputs_ref[...], slot_ref[...])


def network_kernel(*refs, parts, rows):
    part_refs, refs = refs[: 3 * parts], refs[3 * parts :]
    w_grad_ref, sums_ref, low_ref, small_ref = refs
    by_sample = jnp.concatenate([part_refs[3 * i][...] for i in range(parts)], 0)
    samples, width = by_sample.shape
    outs = sums_ref.shape[0]
    w = low_ref[rows["w"], :]
    sample = low_ref[rows["sample"], :]
    sample_t = jnp.concatenate([sample] * (128 // samples), 0).T[:, :samples]
    rounded = by_sample.astype(bf16)
    small_ref[:samples, :] = nt_dot(rounded, w)
    small_ref[samples : samples + width, :] = w_grad_ref[...] + nn_dot(sample_t, rounded)
    at = samples + width
    small_ref[at : at + 1, :] = jnp.sum(by_sample, 0, keepdims=True)
    lane128 = lax.broadcasted_iota(jnp.int32, (1, 128), 1)
    bias = jnp.zeros((1, 128), f32)
    for c in range(outs):
        total = sums_ref[c] + sum(part_refs[3 * i + 1][c] for i in range(parts))
        small_ref[at + 1 + c : at + 2 + c, :] = jnp.sum(total, 0, keepdims=True)
        row = sum(part_refs[3 * i + 2][c : c + 1, :] for i in range(parts))
        bias = bias + jnp.where(lane128 == c, jnp.sum(row, 1, keepdims=True), 0.0)
    small_ref[at + 1 + outs : at + 2 + outs, :] = bias
    rest = small_ref.shape[0] - (at + 2 + outs)
    small_ref[at + 2 + outs :, :] = jnp.zeros((rest, width), f32)


def ray_sum_kernel(keep_ref, got_ref, cot_ref, out_ref, color_ref):
    out_ref[...] = keep_ref[...] + got_ref[...].astype(f32)
    channels, own = color_ref.shape
    rays = cot_ref.shape[1]
    me = lax.axis_index("slab")
    r_i = lax.broadcasted_iota(jnp.int32, (rays, own), 0)
    c_i = lax.broadcasted_iota(jnp.int32, (rays, own), 1)
    pick = jnp.where(r_i == c_i + me * own, 1.0, 0.0).astype(bf16)
    color = cot_ref[channels + 1 : 2 * channels + 1, :]
    high = color.astype(bf16)
    middle = (color - high.astype(f32)).astype(bf16)
    low = (color - high.astype(f32) - middle.astype(f32)).astype(bf16)
    picked = nn_dot(jnp.concatenate([high, middle, low], 0), pick)
    color_ref[...] = picked[:channels] + picked[channels : 2 * channels] + picked[2 * channels :]


def finish_kernel(
    ray_ref,
    color_ref,
    brick_ref,
    sent_ref,
    got_ref,
    color_out_ref,
    ray_out_ref,
    brick_out_ref,
    sample_ref,
    w_ref,
    b_ref,
    w_out_ref,
    b_out_ref,
):
    ray_out_ref[...] = ray_ref[...]
    color_out_ref[...] = color_ref[...]
    part = brick_ref.shape[0]
    brick_out_ref[...] = brick_ref[...] + got_ref[:part, :].astype(f32)
    small = sent_ref[part:, :].astype(f32) + got_ref[part:, :].astype(f32)
    samples, width = sample_ref.shape
    outs = w_out_ref.shape[0]
    at = samples + width
    sample_ref[...] = small[:samples]
    w_ref[...] = small[samples:at]
    b_ref[...] = small[at : at + 1]
    w_out_ref[...] = small[at + 1 : at + 1 + outs]
    b_out_ref[...] = small[at + 1 + outs : at + 2 + outs, :outs]


def body(
    ray_code,
    direction,
    target,
    brick_code,
    sample_code,
    w_hidden,
    b_hidden,
    w_out,
    b_out,
    brick_ids,
    occupancy,
):
    owners = lax.axis_size("slab")
    shares = lax.axis_size("ray")
    me = lax.axis_index("slab")
    ids = brick_ids[0]
    slots, rays = ids.shape
    total = slots * rays
    bricks, width = brick_code.shape[1:]
    samples = sample_code.shape[1]
    outs = w_out.shape[1]
    channels = outs - 1
    count = outs + channels

    def shaped(*shape):
        return jax.ShapeDtypeStruct(shape, f32)

    def shaped16(*shape):
        return jax.ShapeDtypeStruct(shape, bf16)

    rows = low_rows(width, samples)
    lines = line_rows(slots, channels)
    earlier, later = call(
        order_kernel,
        (shaped16(samples, samples), shaped16(samples, samples)),
        "order",
        flops=1 << 34,
    )()
    gathered, low, packed, w_t, s, wide, left = call(
        functools.partial(prepare_kernel, rows=rows, lines=lines),
        (
            shaped16(*ray_code.shape),
            shaped16(rows["w_out"].stop, width),
            shaped(lines["b_out"] + 1, rays),
            shaped16(width, width),
            shaped(samples, width),
            shaped16(samples, width, 128),
            shaped16(outs * 8, 8 * width),
        ),
        "prepare",
        flops=1 << 31,
    )(
        ray_code,
        w_hidden[0],
        sample_code[0],
        w_out[0],
        ids,
        occupancy,
        direction[None],
        target,
        b_hidden,
        b_out,
    )
    turns = gather_bits(owners, ray_code.shape[0])
    other = swap(ray_code, "slab", owners, 1 << turns[0])
    other, lines_later = lax.optimization_barrier((other, packed))
    for b in turns[1:]:
        gathered = jnp.concatenate([gathered, other], 0)
        other = swap(gathered, "slab", owners, 1 << b)
    chosen, project = call(
        chosen_kernel,
        (shaped16(width, total), shaped(width, total)),
        "chosen",
        flops=1 << 29,
    )(lines_later, brick_code[0], w_t)
    passes = ()
    kept = []
    uts = []
    for second, part in enumerate((gathered, other)):
        wide_rays = rays if second else rays // 2
        seg, kept_half, ut_half, ray_sorted = call(
            functools.partial(forward_kernel, owners=owners, second=second, lines=lines),
            (
                shaped(outs, wide_rays),
                shaped(2 * outs, samples, total // 2),
                shaped16(width, total // 2),
                shaped16(wide_rays, width),
            ),
            "forward",
            scratch=(
                pltpu.VMEM((rays // 2, width), bf16),
                pltpu.VMEM((outs, rays // 256, samples, slots * 128), f32),
            ),
            flops=1 << 30,
        )(part, project, w_t, wide, left, packed, earlier, *passes)
        passes = (seg, ray_sorted)
        kept.append(kept_half)
        uts.append(ut_half)

    coef, turned, u = call(
        functools.partial(coefficient_kernel, owners=owners, lines=lines),
        (
            shaped(count, samples, total),
            shaped16(count, total, 128),
            shaped16(total, width),
        ),
        "coefficients",
        flops=1 << 30,
    )(seg, *kept, *uts, later, packed)

    forward = packed[lines["direction"]][None] == 0.0
    group = (seg[:channels], seg[channels:])
    received = []
    basis = []
    bits = bits_of(owners)
    cuts = basis_cuts(total, bits)
    pieces = len(cuts) - 1
    turned_later, chosen_later = turned, chosen
    for b in range(bits):
        sent = jnp.concatenate(group, 0) if b > 0 else seg
        other = swap(sent, "slab", owners, 1 << b)
        if b < pieces:
            piece = cuts[b + 1] - cuts[b]
            basis.append(
                call(
                    functools.partial(basis_kernel, first=cuts[b], row_of=rows),
                    (shaped(count, piece, width), shaped(outs, piece, width)),
                    "basis",
                    flops=1 << 29,
                )(turned_later, u, s, low)
            )
        if b + 1 == bits:
            inputs = call(inputs_kernel, shaped16(width, total), "inputs", flops=1 << 20)(
                chosen_later, ray_sorted
            )
            other, inputs = lax.optimization_barrier((other, inputs))
        other, turned_later, chosen_later = lax.optimization_barrier(
            (other, turned_later, chosen_later)
        )
        received.append(other)
        theirs = (other[:channels], other[channels:])
        upper = ((me >> b) & 1) == 1
        first = jax.tree.map(lambda a, b: jnp.where(upper, b, a), group, theirs)
        second = jax.tree.map(lambda a, b: jnp.where(upper, a, b), group, theirs)
        group = merge(first, second, forward)

    h1, moved_basis = zip(*basis)
    ray_keep, ray_send, cots, spread = call(
        functools.partial(middle_kernel, owners=owners, pieces=pieces, lines=lines),
        (
            shaped(rays // 2, width),
            shaped16(rays // 2, width),
            shaped(8, rays),
            shaped(rays, outs * width),
        ),
        "middle",
        scratch=(pltpu.VMEM((rays, width), f32),),
        flops=1 << 29,
    )(seg, *received, *moved_basis, packed)
    moved, w_grad, sums = call(
        functools.partial(slots_kernel, pieces=pieces, rows=rows),
        (
            shaped16(total, width),
            shaped(width, width),
            shaped(outs, 8, width),
        ),
        "slots",
        scratch=(pltpu.VMEM((total, width), bf16),),
        flops=1 << 20,
    )(*h1, *moved_basis, spread, u, inputs, low)

    def merged(keep, got):
        half = keep.shape[0] // 2
        return keep[:half] + got[:half].astype(f32), (keep[half:] + got[half:].astype(f32)).astype(bf16)

    def part_by_sample(i, cots):
        return call(
            functools.partial(sample_kernel, first=i * samples // parts, rows=rows),
            (
                shaped(samples // parts, width),
                shaped(outs, 8, width),
                shaped(outs, 128),
            ),
            "by_sample",
            scratch=(pltpu.VMEM((samples // parts // 8, outs * 8, total), bf16),),
            flops=1 << 20,
        )(cots, coef, u, s, low)

    def by_brick(first, moved, shape):
        return call(
            functools.partial(brick_kernel, first=first, shares=shares),
            shape,
            "bricks",
            flops=1 << 20,
        )(packed, moved)

    parts = 2
    by_part = []
    later_cots = cots
    for b in range(bits):
        if b + 1 == bits:
            small_rows = -(-(samples + width + 2 + outs) // 16) * 16
            small = call(
                functools.partial(network_kernel, parts=parts, rows=rows),
                shaped(small_rows, width),
                "network",
                flops=1 << 20,
            )(*by_part, w_grad, sums, low)
            ray_send, small = lax.optimization_barrier((ray_send, small))
        ray_got = swap(ray_send, "slab", owners, 1 << halving_bits(owners)[b])
        if b < parts:
            by_part += part_by_sample(b, later_cots)
        if b == 1:
            brick_sent = by_brick(shares // 2, moved, shaped16(bricks // 2, width))
            w_grad, brick_sent = lax.optimization_barrier((w_grad, brick_sent))
        if b + 1 < bits:
            held = (ray_got, later_cots, moved, by_part)
            ray_got, later_cots, moved, by_part = lax.optimization_barrier(held)
            ray_keep, ray_send = merged(ray_keep, ray_got)

    small = small.astype(bf16)
    for b in reversed(range(bits_of(shares))):
        sent = jnp.concatenate([brick_sent, small], 0)
        if 1 << (b + 1) == shares:
            sent, moved = lax.optimization_barrier((sent, moved))
            brick = by_brick(0, moved, shaped(bricks // 2, width))
        other = swap(sent, "ray", shares, 1 << b)
        if b > 0:
            half = brick.shape[0]
            small = (sent[half:].astype(f32) + other[half:].astype(f32)).astype(bf16)
            brick_sent = (brick[half // 2 :] + other[half // 2 : half].astype(f32)).astype(bf16)
            brick = brick[: half // 2] + other[: half // 2].astype(f32)
    ray_sum, color_own = call(
        ray_sum_kernel,
        (shaped(rays // owners, width), shaped(channels, rays // owners)),
        "ray_sum",
        flops=1 << 31,
    )(ray_keep, ray_got, cots)
    color_out, ray_out, brick_out, sample_out, w_grad, b_grad, w_out_grad, b_out_grad = call(
        finish_kernel,
        (
            shaped(channels, rays // owners),
            shaped(rays // owners, width),
            shaped(bricks // shares, width),
            shaped(samples, width),
            shaped(width, width),
            shaped(1, width),
            shaped(outs, width),
            shaped(1, outs),
        ),
        "finish",
    )(ray_sum, color_own, brick, sent, other)
    return (
        color_out,
        ray_out,
        brick_out[None],
        sample_out[None],
        w_grad[None],
        b_grad,
        w_out_grad[None],
        b_out_grad,
    )


def solution(mesh):
    in_specs = (
        P(("ray", "slab"), None),
        P("ray"),
        P(None, "ray"),
        P("slab", None, None),
        P("slab", None, None),
        P("slab", None, None),
        P("slab", None),
        P("slab", None, None),
        P("slab", None),
        P("slab", None, "ray"),
        P("slab", "ray"),
    )
    out_specs = (
        P(None, ("ray", "slab")),
        P(("ray", "slab"), None),
        P("slab", "ray", None),
        P("slab", None, None),
        P("slab", None, None),
        P("slab", None),
        P("slab", None, None),
        P("slab", None),
    )
    return jax.shard_map(body, mesh=mesh, in_specs=in_specs, out_specs=out_specs, check_vma=False)
```

```python
import functools

import jax
import jax.numpy as jnp
from jax import lax
from jax.experimental import pallas as pl
from jax.experimental.pallas import tpu as pltpu
from jax.sharding import PartitionSpec as P

step_length = 0.002
f32 = jnp.float32
bf16 = jnp.bfloat16
vmem_bytes = 24 * 1024 * 1024


def bits_of(count):
    bits = count.bit_length() - 1
    assert count == 1 << bits
    return bits


def gather_bits(owners, own):
    last = max(bits_of(128 // own), 0) if own < 128 else 0
    return [b for b in reversed(range(bits_of(owners))) if b != last] + [last]


def gather_order(owners, own):
    order = [0]
    for b in gather_bits(owners, own)[:-1]:
        order = order + [t ^ (1 << b) for t in order]
    return order


def halving_bits(owners):
    bits = list(range(bits_of(owners)))
    return bits[1:-1] + bits[:1] + bits[1:][-1:]


def halving_order(owners):
    order = [0]
    for b in reversed(halving_bits(owners)):
        order = order + [t ^ (1 << b) for t in order]
    return order


def nt_dot(a, b, precision=None):
    return lax.dot_general(
        a, b, (((1,), (1,)), ((), ())), precision=precision, preferred_element_type=f32
    )


def nn_dot(a, b, precision=None):
    return jnp.dot(a, b, precision=precision, preferred_element_type=f32)


def swap(array, axis, size, distance):
    return lax.ppermute(array, axis, [(i, i ^ distance) for i in range(size)])


def sum_dot(ones, b):
    high = b.astype(bf16)
    low = (b - high.astype(f32)).astype(bf16)
    return nn_dot(ones, high) + nn_dot(ones, low)


def call(kernel, out_shape, name, scratch=(), flops=0):
    def run(*operands):
        return pl.pallas_call(
            kernel,
            out_shape=out_shape,
            in_specs=[pl.BlockSpec(memory_space=pltpu.VMEM)] * len(operands),
            out_specs=jax.tree.map(lambda _: pl.BlockSpec(memory_space=pltpu.VMEM), out_shape),
            scratch_shapes=list(scratch),
            compiler_params=pltpu.CompilerParams(vmem_limit_bytes=vmem_bytes),
            cost_estimate=pl.CostEstimate(flops=flops, bytes_accessed=1 << 10, transcendentals=0),
            name=name,
        )(*operands)

    return run


def low_rows(width, samples):
    starts = {"w": 0, "sample": width, "w_out": width + samples}
    sizes = {"w": width, "sample": samples, "w_out": 16}
    return {name: slice(at, at + sizes[name]) for name, at in starts.items()}


def line_rows(slots, channels):
    return {
        "ids": 0,
        "occ": slots,
        "direction": slots + 1,
        "target": slots + 2,
        "b_out": slots + 2 + channels,
    }


def order_kernel(earlier_ref, later_ref):
    shape = earlier_ref.shape
    r_i = lax.broadcasted_iota(jnp.int32, shape, 0)
    c_i = lax.broadcasted_iota(jnp.int32, shape, 1)
    earlier_ref[...] = jnp.where(c_i < r_i, 1.0, 0.0).astype(bf16)
    later_ref[...] = jnp.where(c_i > r_i, 1.0, 0.0).astype(bf16)


def chosen_kernel(lines_ref, brick_ref, w_t_ref, chosen_ref, project_ref):
    total = chosen_ref.shape[1]
    rays = lines_ref.shape[1]
    bricks = brick_ref.shape[0]
    brick_t = brick_ref[...].astype(f32).T.astype(bf16)
    w_t = w_t_ref[...]
    row = lax.broadcasted_iota(jnp.int32, (bricks, rays), 0).astype(f32)
    for k in range(total // rays):
        one_hot = jnp.where(row == lines_ref[k : k + 1, :], 1.0, 0.0).astype(bf16)
        chosen = nn_dot(brick_t, one_hot).astype(bf16)
        chosen_ref[:, k * rays : (k + 1) * rays] = chosen
        project_ref[:, k * rays : (k + 1) * rays] = nn_dot(w_t, chosen)


def prepare_kernel(
    ray_ref,
    w_ref,
    sample_ref,
    w_out_ref,
    ids_ref,
    occ_ref,
    direction_ref,
    target_ref,
    b_ref,
    b_out_ref,
    own_ref,
    low_ref,
    lines_ref,
    w_t_ref,
    s_ref,
    wide_ref,
    left_ref,
    *,
    rows,
    lines,
):
    slots, rays = ids_ref.shape
    width = w_t_ref.shape[0]
    samples = s_ref.shape[0]
    outs = w_out_ref.shape[0]
    own_ref[...] = ray_ref[...]
    w = w_ref[...]
    w_out = w_out_ref[...].astype(f32)
    low_ref[rows["w"], :] = w
    low_ref[rows["sample"], :] = sample_ref[...]
    low_ref[rows["w_out"], :] = jnp.concatenate(
        [w_out, jnp.zeros((16 - outs, width), f32)], 0
    ).astype(bf16)
    lines_ref[:slots, :] = ids_ref[...].astype(f32)
    lines_ref[lines["occ"] : lines["occ"] + 1, :] = occ_ref[...].astype(f32)
    lines_ref[lines["direction"] : lines["direction"] + 1, :] = direction_ref[...].astype(f32)
    lines_ref[lines["target"] : lines["target"] + outs - 1, :] = target_ref[...]
    lines_ref[lines["b_out"] : lines["b_out"] + 1, :outs] = b_out_ref[...]
    w_t = w.astype(f32).T.astype(bf16)
    w_t_ref[...] = w_t
    s = nn_dot(sample_ref[...], w) + b_ref[...]
    s_ref[...] = s.astype(bf16).astype(f32)
    s_t = jnp.concatenate([s] * (128 // samples), 0).T
    for j in range(samples):
        wide_ref[j] = jnp.broadcast_to(s_t[:, j : j + 1], (width, 128)).astype(bf16)
    w_rows = jnp.concatenate(
        [jnp.broadcast_to(w_out[c : c + 1, :], (8, width)) for c in range(outs)], 0
    )
    row8 = lax.broadcasted_iota(jnp.int32, (outs * 8, width), 0) % 8
    for i in range(8):
        left_ref[:, i * width : (i + 1) * width] = jnp.where(row8 == i, w_rows, 0.0).astype(bf16)


def forward_kernel(*refs, owners, second, lines):
    ray_ref, project_ref, w_t_ref, wide_ref, left_ref, lines_ref, earlier_ref, *refs = refs
    if second:
        before_refs, refs = refs[:2], refs[2:]
    seg_ref, kept_ref, ut_ref, sorted_ref, order_ref, raw_ref = refs
    width, total = project_ref.shape
    samples = wide_ref.shape[0]
    outs = seg_ref.shape[0]
    half, rays = ray_ref.shape[0], lines_ref.shape[1]
    slots = total // rays
    chunk = 128
    own = 2 * half // owners
    last = gather_bits(owners, own)[-1]
    me = lax.axis_index("slab")
    side = (me >> last) & 1

    def whole(n, k=0, side=side):
        return pl.ds(pl.multiple_of(k * rays + (2 * n + side) * chunk, chunk), chunk)

    if second:
        for n in range(half // chunk):
            part = slice(n * chunk, (n + 1) * chunk)
            seg_ref[:, whole(n)] = before_refs[0][:, part]
            sorted_ref[whole(n), :] = before_refs[1][part, :]
        side = 1 - side

    def spot(n, k=0):
        at = k * half + n * chunk
        return whole(n, k, side) if second else slice(at, at + chunk)

    flip = (1 << last) if second else 0
    for i, t in enumerate(gather_order(owners, own)):
        owner = me ^ (t ^ flip)
        place = ((owner >> (last + 1)) << last) | (owner & ((1 << last) - 1))
        order_ref[pl.ds(pl.multiple_of(place * own, own), own), :] = ray_ref[
            i * own : (i + 1) * own, :
        ]
    ray_t = nt_dot(w_t_ref[...], order_ref[...])
    for n in range(half // chunk):
        sorted_ref[spot(n), :] = order_ref[n * chunk : (n + 1) * chunk, :]
        for k in range(slots):
            part = project_ref[:, whole(n, k, side)] + ray_t[:, n * chunk : (n + 1) * chunk]
            ut_ref[:, k * half + n * chunk : k * half + (n + 1) * chunk] = part.astype(bf16)
    b_out = [lines_ref[lines["b_out"], c] for c in range(outs)]

    def shade(n):
        ut = [ut_ref[:, k * half + n * chunk : k * half + (n + 1) * chunk] for k in range(slots)]
        ut = jnp.concatenate(ut, 1)
        for block in range(samples // 8):
            acc = None
            for i in range(4):
                parts = []
                for h in range(2):
                    column = wide_ref[block * 8 + 2 * i + h]
                    column = jnp.concatenate([column] * slots, 1)
                    parts.append(jnp.maximum(ut + column, 0))
                left = left_ref[:, 2 * i * width : 2 * (i + 1) * width]
                term = nn_dot(left, jnp.concatenate(parts, 0))
                acc = term if acc is None else acc + term
            for c in range(outs):
                raw_ref[c, n, block * 8 : block * 8 + 8, :] = acc[c * 8 : c * 8 + 8, :] + b_out[c]

    for n in range(half // chunk):
        shade(n)
    earlier = earlier_ref[...]
    occ_row = lines["occ"]
    for n in range(half // chunk):
        occ = lines_ref[occ_row : occ_row + 1, whole(n, 0, side)]
        raws = [
            raw_ref[0, n, :, k * chunk : (k + 1) * chunk] for k in range(slots)
        ]
        occupied = [(k < occ).astype(f32) for k in range(slots)]
        opticals = [
            step_length * (jnp.maximum(x, 0.0) + jnp.log1p(jnp.exp(-jnp.abs(x)))) * o
            for x, o in zip(raws, occupied)
        ]
        enters = sum_dot(earlier, jnp.concatenate(opticals, 1))
        before = jnp.zeros((1, chunk), f32)
        colors = [jnp.zeros((1, chunk), f32)] * (outs - 1)
        for k in range(slots):
            local = slice(k * half + n * chunk, k * half + (n + 1) * chunk)
            optical = opticals[k]
            entered = enters[:, k * chunk : (k + 1) * chunk] + before
            before = before + jnp.sum(optical, 0, keepdims=True)
            tanh = jnp.tanh(0.5 * optical)
            weight = jnp.exp(-entered) * (2.0 * tanh / (1.0 + tanh))
            for c in range(outs - 1):
                shading = jax.nn.sigmoid(raw_ref[c + 1, n, :, k * chunk : (k + 1) * chunk])
                light = weight * shading
                colors[c] = colors[c] + jnp.sum(light, 0, keepdims=True)
                kept_ref[c, :, local] = shading
                kept_ref[outs + c, :, local] = light
            kept_ref[outs - 1, :, local] = entered + optical
            kept_ref[2 * outs - 1, :, local] = raws[k]
        place = spot(n)
        for c in range(outs - 1):
            seg_ref[c : c + 1, place] = colors[c]
        seg_ref[outs - 1 : outs, place] = jnp.exp(-before)


def coefficient_kernel(
    seg_ref,
    first_ref,
    second_ref,
    first_ut_ref,
    second_ut_ref,
    later_ref,
    lines_ref,
    coef_ref,
    turned_ref,
    u_ref,
    *,
    owners,
    lines,
):
    outs, rays = seg_ref.shape
    samples, local = first_ref.shape[1:]
    half = rays // 2
    slots = local // half
    last = gather_bits(owners, rays // owners)[-1]
    side = (lax.axis_index("slab") >> last) & 1
    later = later_ref[...]
    chunk = 128

    def keep(index, lanes, value):
        coef_ref[index, :, lanes] = value
        value = value.astype(bf16)
        turned_ref[index, lanes, :] = jnp.concatenate([value] * (128 // samples), 0).T

    for kept_ref, ut_ref, where in (
        (first_ref, first_ut_ref, side),
        (second_ref, second_ut_ref, 1 - side),
    ):
        for n in range(half // chunk):
            base = (2 * n + where) * chunk
            through = seg_ref[outs - 1 : outs, pl.ds(pl.multiple_of(base, chunk), chunk)]
            occ = lines_ref[lines["occ"] : lines["occ"] + 1, pl.ds(pl.multiple_of(base, chunk), chunk)]
            after = [jnp.zeros((1, chunk), f32)] * (outs - 1)
            for k in reversed(range(slots)):
                lanes = pl.ds(pl.multiple_of(k * rays + base, chunk), chunk)
                at = slice(k * half + n * chunk, k * half + (n + 1) * chunk)
                u_ref[lanes, :] = ut_ref[:, at].T
                passed = jnp.exp(-kept_ref[outs - 1, :, at])
                occupied = (k < occ).astype(f32)
                density = step_length * occupied * jax.nn.sigmoid(kept_ref[2 * outs - 1, :, at])
                lights = [kept_ref[outs + c, :, at] for c in range(outs - 1)]
                behinds = sum_dot(later, jnp.concatenate(lights, 1))
                for c in range(outs - 1):
                    shading = kept_ref[c, :, at]
                    light = lights[c]
                    behind = behinds[:, c * chunk : (c + 1) * chunk] + after[c]
                    after[c] = after[c] + jnp.sum(light, 0, keepdims=True)
                    keep(c, lanes, density * (shading * passed - behind))
                    keep(outs + c, lanes, light * (1.0 - shading))
                keep(outs - 1, lanes, density * through)


def basis_kernel(turned_ref, u_ref, s_ref, low_ref, h1_ref, moved_ref, *, first, row_of):
    count, rays, width = h1_ref.shape
    samples = s_ref.shape[0]
    negative = (-s_ref[...]).astype(bf16)
    one = jnp.ones((samples, width), bf16)
    zero = jnp.zeros((samples, width), bf16)
    lane = lax.broadcasted_iota(jnp.int32, (8, 8 * samples), 1) // samples
    row = lax.broadcasted_iota(jnp.int32, (8, 8 * samples), 0)
    block_mask = lane == row
    repeat = 8 * samples // 128
    step = 128
    outs = moved_ref.shape[0]
    w = low_ref[row_of["w"], :]
    w_out = low_ref[row_of["w_out"], :].astype(f32)
    w_rows = [w_out[c : c + 1, :] for c in range(outs)]

    def slot_block(block, carry):
        for h in range(step // 16):
            base = pl.multiple_of(block * step + h * 16, 16)
            u16 = u_ref[pl.ds(first + base, 16), :]
            rows16 = [turned_ref[c, pl.ds(first + base, 16), :].astype(f32) for c in range(count)]
            for q in range(2):
                at = pl.multiple_of(block * step + h * 16 + q * 8, 8)
                left = [
                    jnp.where(
                        block_mask,
                        jnp.concatenate([rows16[c][q * 8 : q * 8 + 8]] * repeat, 1),
                        0.0,
                    )
                    for c in range(count)
                ]
                left = jnp.concatenate(left, 0).astype(bf16)
                tiles = [
                    jnp.where(
                        jnp.broadcast_to(u16[q * 8 + i : q * 8 + i + 1, :], (samples, width))
                        > negative,
                        one,
                        zero,
                    )
                    for i in range(8)
                ]
                h1 = nn_dot(left, jnp.concatenate(tiles, 0))
                for c in range(count):
                    h1_ref[c, pl.ds(at, 8), :] = h1[c * 8 : c * 8 + 8, :]
        return carry

    lax.fori_loop(0, rays // step, slot_block, 0)
    for c in range(outs):
        grad = w_rows[0] * h1_ref[c]
        if c + 1 < outs:
            grad = grad + w_rows[c + 1] * h1_ref[outs + c]
        moved_ref[c] = nt_dot(grad.astype(bf16), w)


def basis_cuts(total, bits):
    eighth = total // 8
    return [0, 2 * eighth, 5 * eighth, total] if bits > 2 else [0, total]


def basis_part(refs, row):
    for ref in refs:
        if row < ref.shape[1]:
            return ref, row
        row -= ref.shape[1]


def merge(first, second, forward):
    fc, ft = first
    sc, st = second
    return jnp.where(forward, fc + ft * sc, sc + st * fc), ft * st


def pair_kernel(*refs):
    basis_refs, out_ref = refs[:-1], refs[-1]
    outs, rays, width = out_ref.shape
    total = sum(ref.shape[1] for ref in basis_refs)
    chunk = 128
    for n in range(rays // chunk):
        for c in range(outs):
            whole = None
            for k in range(total // rays):
                ref, at = basis_part(basis_refs, k * rays + n * chunk)
                part = ref[c, at : at + chunk, :]
                whole = part if whole is None else whole + part
            out_ref[c, n * chunk : (n + 1) * chunk, :] = whole


def middle_kernel(*refs, owners, lines):
    bits = bits_of(owners)
    seg_ref, refs = refs[0], refs[1:]
    got_refs, refs = refs[:bits], refs[bits:]
    paired_ref, refs = refs[0], refs[1:]
    lines_ref, keep_ref, send_ref, cot_ref, spread_ref, ray_ref = refs
    me = lax.axis_index("slab")
    outs = seg_ref.shape[0]
    channels = outs - 1
    rays = lines_ref.shape[1]
    width = paired_ref.shape[2]
    forward = lines_ref[lines["direction"] : lines["direction"] + 1, :] == 0.0
    target = lines_ref[lines["target"] : lines["target"] + channels, :]

    def pair(values):
        return values[:channels, :], values[channels : channels + 1, :]

    low = high = None
    for b in reversed(range(bits)):
        piece = pair(got_refs[b][...])
        is_low = ((me >> b) & 1) == 1
        piece = (jnp.where(is_low, piece[0], 0.0), jnp.where(is_low, piece[1], 1.0))
        low = piece if low is None else merge(low, piece, forward)
    for b in range(bits):
        piece = pair(got_refs[b][...])
        is_high = ((me >> b) & 1) == 0
        piece = (jnp.where(is_high, piece[0], 0.0), jnp.where(is_high, piece[1], 1.0))
        high = piece if high is None else merge(high, piece, forward)
    seg_color, seg_trans = pair(seg_ref[...])
    before_color = jnp.where(forward, low[0], high[0])
    before_trans = jnp.where(forward, low[1], high[1])
    after_color = jnp.where(forward, high[0], low[0])
    color = before_color + before_trans * (seg_color + seg_trans * after_color)
    residual = color - target
    color_cot = before_trans * residual
    trans_cot = -before_trans * jnp.sum(after_color * residual, 0, keepdims=True)
    cot_ref[:channels, :] = color_cot
    cot_ref[channels:outs, :] = trans_cot
    cot_ref[outs : outs + channels, :] = color
    cot_ref[outs + channels :, :] = jnp.zeros((8 - outs - channels, rays), f32)
    chunk = 128
    values = jnp.concatenate([color_cot, trans_cot], 0)
    rounded = values.astype(bf16).astype(f32)
    values = jnp.concatenate([rounded, values - rounded], 0)
    row = lax.broadcasted_iota(jnp.int32, (2 * outs, outs * width), 0) % outs
    lane = lax.broadcasted_iota(jnp.int32, (2 * outs, outs * width), 1) // width
    spread = jnp.where(row == lane, 1.0, 0.0).astype(bf16)
    for n in range(rays // chunk):
        these = slice(n * chunk, (n + 1) * chunk)
        spread_ref[these, :] = nn_dot(values[:, these].T.astype(bf16), spread)
        grad = None
        for c in range(outs):
            whole = paired_ref[c, these, :]
            term = spread_ref[these, c * width : (c + 1) * width] * whole
            grad = term if grad is None else grad + term
        ray_ref[these, :] = grad
    own = rays // owners
    for i, t in enumerate(halving_order(owners)):
        place = pl.multiple_of((me ^ t) * own, own)
        if i < owners // 2:
            keep_ref[i * own : (i + 1) * own, :] = ray_ref[pl.ds(place, own), :]
        else:
            at = i * own - rays // 2
            send_ref[at : at + own, :] = ray_ref[pl.ds(place, own), :].astype(bf16)


def brick_kernel(lines_ref, moved_ref, out_ref, *, first, shares):
    share = lax.axis_index("ray")
    rays = lines_ref.shape[1]
    total, width = moved_ref.shape
    owners = shares // 2
    part = out_ref.shape[0] // owners
    moved = moved_ref[...]
    row = lax.broadcasted_iota(jnp.int32, (part, rays), 0).astype(f32)
    for i in range(owners):
        begin = ((share ^ (first + i)) * part).astype(f32)
        acc = jnp.zeros((part, width), f32)
        for k in range(total // rays):
            one_hot = jnp.where(row + begin == lines_ref[k : k + 1, :], 1.0, 0.0).astype(bf16)
            acc = acc + nn_dot(one_hot, moved[k * rays : (k + 1) * rays])
        out_ref[i * part : (i + 1) * part, :] = acc.astype(out_ref.dtype)


def sample_kernel(
    cot_ref, coef_ref, u_ref, s_ref, low_ref, by_sample_ref, sums_ref, bias_ref, g_ref, *, first, rows
):
    outs = sums_ref.shape[0]
    channels = outs - 1
    rays = cot_ref.shape[1]
    total, width = u_ref.shape
    samples = by_sample_ref.shape[0]
    bias_sums = [jnp.zeros((1, 128), f32)] * outs
    for n in range(total // 128):
        lanes = slice(n * 128, n * 128 + 128)
        at = (n * 128) % rays
        cots = [cot_ref[c : c + 1, at : at + 128] for c in range(outs)]
        grads = [sum(cots[c] * coef_ref[c, first : first + samples, lanes] for c in range(outs))]
        for c in range(channels):
            grads.append(cots[c] * coef_ref[outs + c, first : first + samples, lanes])
        for c in range(outs):
            bias_sums[c] = bias_sums[c] + jnp.sum(grads[c], 0, keepdims=True)
        for j in range(0, samples, 8):
            g_ref[j // 8, :, lanes] = jnp.concatenate([g[j : j + 8] for g in grads], 0).astype(bf16)
    w_out = low_ref[rows["w_out"], :].astype(f32)
    w_rows = [w_out[c : c + 1, :] for c in range(outs)]
    row8 = lax.broadcasted_iota(jnp.int32, (8, width), 0)

    def sample_block(block, sums):
        left = g_ref[block]
        s8 = s_ref[pl.ds(pl.multiple_of(first + block * 8, 8), 8), :]
        acc = [jnp.zeros((8, width), f32)] * outs
        for i in range(0, 8, 2):
            edges = [(-s8[i + h : i + h + 1, :]).astype(bf16) for h in range(2)]
            h2 = None
            for n in range(total // 256):
                u = u_ref[n * 256 : n * 256 + 256, :]
                live = [
                    jnp.where(
                        u > jnp.broadcast_to(edge, u.shape),
                        jnp.ones(u.shape, bf16),
                        jnp.zeros(u.shape, bf16),
                    )
                    for edge in edges
                ]
                term = nn_dot(left[:, n * 256 : n * 256 + 256], jnp.concatenate(live, 1))
                h2 = term if h2 is None else h2 + term
            for c in range(outs):
                for h in range(2):
                    piece = h2[c * 8 : c * 8 + 8, h * width : (h + 1) * width]
                    acc[c] = acc[c] + jnp.where(row8 == i + h, piece, 0.0)
        by_sample_ref[pl.ds(pl.multiple_of(block * 8, 8), 8), :] = sum(
            w_rows[c] * acc[c] for c in range(outs)
        )
        return tuple(sums[c] + s8 * acc[c] for c in range(outs))

    sums = [jnp.zeros((8, width), f32)] * outs
    sums = lax.fori_loop(0, samples // 8, sample_block, tuple(sums), unroll=4)
    for c in range(outs):
        sums_ref[c] = sums[c]
        bias_ref[c : c + 1, :] = bias_sums[c]


def inputs_kernel(chosen_ref, sorted_ref, inputs_ref):
    total = chosen_ref.shape[1]
    ray_t = sorted_ref[...].astype(f32).T
    inputs = chosen_ref[...].astype(f32) + jnp.concatenate([ray_t] * (total // ray_t.shape[1]), 1)
    inputs_ref[...] = inputs.astype(bf16)


def slots_kernel(*refs, pieces, rows):
    h1_refs, refs = refs[:pieces], refs[pieces:]
    basis_refs, refs = refs[:pieces], refs[pieces:]
    spread_ref, u_ref, inputs_ref, low_ref, *refs = refs
    moved_ref, w_grad_ref, sums_ref, slot_ref = refs
    rays = spread_ref.shape[0]
    total, width = u_ref.shape
    outs = sums_ref.shape[0]
    w_out = low_ref[rows["w_out"], :].astype(f32)
    w_rows = [w_out[c : c + 1, :] for c in range(outs)]
    chunk = 32
    sums = [jnp.zeros((8, width), f32)] * outs
    for n in range(rays // chunk):
        these = slice(n * chunk, (n + 1) * chunk)
        cots = [spread_ref[these, c * width : (c + 1) * width] for c in range(outs)]
        for k in range(total // rays):
            whole = slice(k * rays + n * chunk, k * rays + (n + 1) * chunk)
            u = u_ref[whole, :].astype(f32)
            h1_ref, at = basis_part(h1_refs, whole.start)
            basis_ref, at = basis_part(basis_refs, whole.start)
            here = slice(at, at + chunk)
            products = [sum(cots[c] * h1_ref[c, here, :] for c in range(outs))]
            products += [cots[c] * h1_ref[outs + c, here, :] for c in range(outs - 1)]
            for c in range(outs):
                sums[c] = sums[c] + jnp.sum((u * products[c]).reshape(chunk // 8, 8, width), 0)
            slot_ref[whole, :] = sum(w_rows[c] * products[c] for c in range(outs)).astype(bf16)
            moved = sum(cots[c] * basis_ref[c, here, :] for c in range(outs))
            moved_ref[whole, :] = moved.astype(bf16)
    for c in range(outs):
        sums_ref[c] = sums[c]
    w_grad_ref[...] = nn_dot(inputs_ref[...], slot_ref[...])


def network_kernel(*refs, parts, rows):
    part_refs, refs = refs[: 3 * parts], refs[3 * parts :]
    w_grad_ref, sums_ref, low_ref, small_ref = refs
    by_sample = jnp.concatenate([part_refs[3 * i][...] for i in range(parts)], 0)
    samples, width = by_sample.shape
    outs = sums_ref.shape[0]
    w = low_ref[rows["w"], :]
    sample = low_ref[rows["sample"], :]
    sample_t = jnp.concatenate([sample] * (128 // samples), 0).T[:, :samples]
    rounded = by_sample.astype(bf16)
    small_ref[:samples, :] = nt_dot(rounded, w)
    small_ref[samples : samples + width, :] = w_grad_ref[...] + nn_dot(sample_t, rounded)
    at = samples + width
    small_ref[at : at + 1, :] = jnp.sum(by_sample, 0, keepdims=True)
    lane128 = lax.broadcasted_iota(jnp.int32, (1, 128), 1)
    bias = jnp.zeros((1, 128), f32)
    for c in range(outs):
        total = sums_ref[c] + sum(part_refs[3 * i + 1][c] for i in range(parts))
        small_ref[at + 1 + c : at + 2 + c, :] = jnp.sum(total, 0, keepdims=True)
        row = sum(part_refs[3 * i + 2][c : c + 1, :] for i in range(parts))
        bias = bias + jnp.where(lane128 == c, jnp.sum(row, 1, keepdims=True), 0.0)
    small_ref[at + 1 + outs : at + 2 + outs, :] = bias
    rest = small_ref.shape[0] - (at + 2 + outs)
    small_ref[at + 2 + outs :, :] = jnp.zeros((rest, width), f32)


def ray_sum_kernel(keep_ref, got_ref, cot_ref, out_ref, color_ref):
    out_ref[...] = keep_ref[...] + got_ref[...].astype(f32)
    channels, own = color_ref.shape
    rays = cot_ref.shape[1]
    me = lax.axis_index("slab")
    r_i = lax.broadcasted_iota(jnp.int32, (rays, own), 0)
    c_i = lax.broadcasted_iota(jnp.int32, (rays, own), 1)
    pick = jnp.where(r_i == c_i + me * own, 1.0, 0.0).astype(bf16)
    color = cot_ref[channels + 1 : 2 * channels + 1, :]
    high = color.astype(bf16)
    middle = (color - high.astype(f32)).astype(bf16)
    low = (color - high.astype(f32) - middle.astype(f32)).astype(bf16)
    picked = nn_dot(jnp.concatenate([high, middle, low], 0), pick)
    color_ref[...] = picked[:channels] + picked[channels : 2 * channels] + picked[2 * channels :]


def finish_kernel(
    ray_ref,
    color_ref,
    brick_ref,
    sent_ref,
    got_ref,
    color_out_ref,
    ray_out_ref,
    brick_out_ref,
    sample_ref,
    w_ref,
    b_ref,
    w_out_ref,
    b_out_ref,
):
    ray_out_ref[...] = ray_ref[...]
    color_out_ref[...] = color_ref[...]
    part = brick_ref.shape[0]
    brick_out_ref[...] = brick_ref[...] + got_ref[:part, :].astype(f32)
    small = sent_ref[part:, :].astype(f32) + got_ref[part:, :].astype(f32)
    samples, width = sample_ref.shape
    outs = w_out_ref.shape[0]
    at = samples + width
    sample_ref[...] = small[:samples]
    w_ref[...] = small[samples:at]
    b_ref[...] = small[at : at + 1]
    w_out_ref[...] = small[at + 1 : at + 1 + outs]
    b_out_ref[...] = small[at + 1 + outs : at + 2 + outs, :outs]


def body(
    ray_code,
    direction,
    target,
    brick_code,
    sample_code,
    w_hidden,
    b_hidden,
    w_out,
    b_out,
    brick_ids,
    occupancy,
):
    owners = lax.axis_size("slab")
    shares = lax.axis_size("ray")
    me = lax.axis_index("slab")
    ids = brick_ids[0]
    slots, rays = ids.shape
    total = slots * rays
    bricks, width = brick_code.shape[1:]
    samples = sample_code.shape[1]
    outs = w_out.shape[1]
    channels = outs - 1
    count = outs + channels

    def shaped(*shape):
        return jax.ShapeDtypeStruct(shape, f32)

    def shaped16(*shape):
        return jax.ShapeDtypeStruct(shape, bf16)

    rows = low_rows(width, samples)
    lines = line_rows(slots, channels)
    earlier, later = call(
        order_kernel,
        (shaped16(samples, samples), shaped16(samples, samples)),
        "order",
        flops=1 << 34,
    )()
    gathered, low, packed, w_t, s, wide, left = call(
        functools.partial(prepare_kernel, rows=rows, lines=lines),
        (
            shaped16(*ray_code.shape),
            shaped16(rows["w_out"].stop, width),
            shaped(lines["b_out"] + 1, rays),
            shaped16(width, width),
            shaped(samples, width),
            shaped16(samples, width, 128),
            shaped16(outs * 8, 8 * width),
        ),
        "prepare",
        flops=1 << 31,
    )(
        ray_code,
        w_hidden[0],
        sample_code[0],
        w_out[0],
        ids,
        occupancy,
        direction[None],
        target,
        b_hidden,
        b_out,
    )
    turns = gather_bits(owners, ray_code.shape[0])
    other = swap(ray_code, "slab", owners, 1 << turns[0])
    other, lines_later = lax.optimization_barrier((other, packed))
    for b in turns[1:]:
        gathered = jnp.concatenate([gathered, other], 0)
        other = swap(gathered, "slab", owners, 1 << b)
    chosen, project = call(
        chosen_kernel,
        (shaped16(width, total), shaped(width, total)),
        "chosen",
        flops=1 << 29,
    )(lines_later, brick_code[0], w_t)
    passes = ()
    kept = []
    uts = []
    for second, part in enumerate((gathered, other)):
        wide_rays = rays if second else rays // 2
        seg, kept_half, ut_half, ray_sorted = call(
            functools.partial(forward_kernel, owners=owners, second=second, lines=lines),
            (
                shaped(outs, wide_rays),
                shaped(2 * outs, samples, total // 2),
                shaped16(width, total // 2),
                shaped16(wide_rays, width),
            ),
            "forward",
            scratch=(
                pltpu.VMEM((rays // 2, width), bf16),
                pltpu.VMEM((outs, rays // 256, samples, slots * 128), f32),
            ),
            flops=1 << 30,
        )(part, project, w_t, wide, left, packed, earlier, *passes)
        passes = (seg, ray_sorted)
        kept.append(kept_half)
        uts.append(ut_half)

    coef, turned, u = call(
        functools.partial(coefficient_kernel, owners=owners, lines=lines),
        (
            shaped(count, samples, total),
            shaped16(count, total, 128),
            shaped16(total, width),
        ),
        "coefficients",
        flops=1 << 30,
    )(seg, *kept, *uts, later, packed)

    forward = packed[lines["direction"]][None] == 0.0
    group = (seg[:channels], seg[channels:])
    received = []
    basis = []
    bits = bits_of(owners)
    cuts = basis_cuts(total, bits)
    pieces = len(cuts) - 1
    turned_later, chosen_later = turned, chosen
    for b in range(bits):
        sent = jnp.concatenate(group, 0) if b > 0 else seg
        other = swap(sent, "slab", owners, 1 << b)
        if b < pieces:
            piece = cuts[b + 1] - cuts[b]
            basis.append(
                call(
                    functools.partial(basis_kernel, first=cuts[b], row_of=rows),
                    (shaped(count, piece, width), shaped(outs, piece, width)),
                    "basis",
                    flops=1 << 29,
                )(turned_later, u, s, low)
            )
        if b + 1 == bits:
            inputs = call(inputs_kernel, shaped16(width, total), "inputs", flops=1 << 20)(
                chosen_later, ray_sorted
            )
            paired = call(pair_kernel, shaped(outs, rays, width), "paired", flops=1 << 20)(
                *[moved for _, moved in basis]
            )
            other, inputs, paired = lax.optimization_barrier((other, inputs, paired))
        other, turned_later, chosen_later = lax.optimization_barrier(
            (other, turned_later, chosen_later)
        )
        received.append(other)
        theirs = (other[:channels], other[channels:])
        upper = ((me >> b) & 1) == 1
        first = jax.tree.map(lambda a, b: jnp.where(upper, b, a), group, theirs)
        second = jax.tree.map(lambda a, b: jnp.where(upper, a, b), group, theirs)
        group = merge(first, second, forward)

    h1, moved_basis = zip(*basis)
    ray_keep, ray_send, cots, spread = call(
        functools.partial(middle_kernel, owners=owners, lines=lines),
        (
            shaped(rays // 2, width),
            shaped16(rays // 2, width),
            shaped(8, rays),
            shaped(rays, outs * width),
        ),
        "middle",
        scratch=(pltpu.VMEM((rays, width), f32),),
        flops=1 << 29,
    )(seg, *received, paired, packed)
    moved, w_grad, sums = call(
        functools.partial(slots_kernel, pieces=pieces, rows=rows),
        (
            shaped16(total, width),
            shaped(width, width),
            shaped(outs, 8, width),
        ),
        "slots",
        scratch=(pltpu.VMEM((total, width), bf16),),
        flops=1 << 20,
    )(*h1, *moved_basis, spread, u, inputs, low)

    def merged(keep, got):
        half = keep.shape[0] // 2
        return keep[:half] + got[:half].astype(f32), (keep[half:] + got[half:].astype(f32)).astype(bf16)

    def part_by_sample(i, cots):
        return call(
            functools.partial(sample_kernel, first=i * samples // parts, rows=rows),
            (
                shaped(samples // parts, width),
                shaped(outs, 8, width),
                shaped(outs, 128),
            ),
            "by_sample",
            scratch=(pltpu.VMEM((samples // parts // 8, outs * 8, total), bf16),),
            flops=1 << 20,
        )(cots, coef, u, s, low)

    def by_brick(first, moved, shape):
        return call(
            functools.partial(brick_kernel, first=first, shares=shares),
            shape,
            "bricks",
            flops=1 << 20,
        )(packed, moved)

    parts = 2
    by_part = []
    later_cots = cots
    for b in range(bits):
        if b + 1 == bits:
            small_rows = -(-(samples + width + 2 + outs) // 16) * 16
            small = call(
                functools.partial(network_kernel, parts=parts, rows=rows),
                shaped(small_rows, width),
                "network",
                flops=1 << 20,
            )(*by_part, w_grad, sums, low)
            ray_send, small = lax.optimization_barrier((ray_send, small))
        ray_got = swap(ray_send, "slab", owners, 1 << halving_bits(owners)[b])
        if b < parts:
            by_part += part_by_sample(b, later_cots)
        if b == 1:
            brick_sent = by_brick(shares // 2, moved, shaped16(bricks // 2, width))
            w_grad, brick_sent = lax.optimization_barrier((w_grad, brick_sent))
        if b + 1 < bits:
            held = (ray_got, later_cots, moved, by_part)
            ray_got, later_cots, moved, by_part = lax.optimization_barrier(held)
            ray_keep, ray_send = merged(ray_keep, ray_got)

    small = small.astype(bf16)
    for b in reversed(range(bits_of(shares))):
        sent = jnp.concatenate([brick_sent, small], 0)
        if 1 << (b + 1) == shares:
            sent, moved = lax.optimization_barrier((sent, moved))
            brick = by_brick(0, moved, shaped(bricks // 2, width))
        other = swap(sent, "ray", shares, 1 << b)
        if b > 0:
            half = brick.shape[0]
            small = (sent[half:].astype(f32) + other[half:].astype(f32)).astype(bf16)
            brick_sent = (brick[half // 2 :] + other[half // 2 : half].astype(f32)).astype(bf16)
            brick = brick[: half // 2] + other[: half // 2].astype(f32)
    ray_sum, color_own = call(
        ray_sum_kernel,
        (shaped(rays // owners, width), shaped(channels, rays // owners)),
        "ray_sum",
        flops=1 << 31,
    )(ray_keep, ray_got, cots)
    color_out, ray_out, brick_out, sample_out, w_grad, b_grad, w_out_grad, b_out_grad = call(
        finish_kernel,
        (
            shaped(channels, rays // owners),
            shaped(rays // owners, width),
            shaped(bricks // shares, width),
            shaped(samples, width),
            shaped(width, width),
            shaped(1, width),
            shaped(outs, width),
            shaped(1, outs),
        ),
        "finish",
    )(ray_sum, color_own, brick, sent, other)
    return (
        color_out,
        ray_out,
        brick_out[None],
        sample_out[None],
        w_grad[None],
        b_grad,
        w_out_grad[None],
        b_out_grad,
    )


def solution(mesh):
    in_specs = (
        P(("ray", "slab"), None),
        P("ray"),
        P(None, "ray"),
        P("slab", None, None),
        P("slab", None, None),
        P("slab", None, None),
        P("slab", None),
        P("slab", None, None),
        P("slab", None),
        P("slab", None, "ray"),
        P("slab", "ray"),
    )
    out_specs = (
        P(None, ("ray", "slab")),
        P(("ray", "slab"), None),
        P("slab", "ray", None),
        P("slab", None, None),
        P("slab", None, None),
        P("slab", None),
        P("slab", None, None),
        P("slab", None),
    )
    return jax.shard_map(body, mesh=mesh, in_specs=in_specs, out_specs=out_specs, check_vma=False)
```

```python
import functools

import jax
import jax.numpy as jnp
from jax import lax
from jax.experimental import pallas as pl
from jax.experimental.pallas import tpu as pltpu
from jax.sharding import PartitionSpec as P

step_length = 0.002
f32 = jnp.float32
bf16 = jnp.bfloat16
vmem_bytes = 24 * 1024 * 1024


def bits_of(count):
    bits = count.bit_length() - 1
    assert count == 1 << bits
    return bits


def gather_bits(owners, own):
    last = max(bits_of(128 // own), 0) if own < 128 else 0
    return [b for b in reversed(range(bits_of(owners))) if b != last] + [last]


def gather_order(owners, own):
    order = [0]
    for b in gather_bits(owners, own)[:-1]:
        order = order + [t ^ (1 << b) for t in order]
    return order


def halving_bits(owners):
    bits = list(range(bits_of(owners)))
    return bits


def halving_order(owners):
    order = [0]
    for b in reversed(halving_bits(owners)):
        order = order + [t ^ (1 << b) for t in order]
    return order


def nt_dot(a, b, precision=None):
    return lax.dot_general(
        a, b, (((1,), (1,)), ((), ())), precision=precision, preferred_element_type=f32
    )


def nn_dot(a, b, precision=None):
    return jnp.dot(a, b, precision=precision, preferred_element_type=f32)


def swap(array, axis, size, distance):
    return lax.ppermute(array, axis, [(i, i ^ distance) for i in range(size)])


def sum_dot(ones, b):
    high = b.astype(bf16)
    low = (b - high.astype(f32)).astype(bf16)
    return nn_dot(ones, high) + nn_dot(ones, low)


def call(kernel, out_shape, name, scratch=(), flops=0):
    def run(*operands):
        return pl.pallas_call(
            kernel,
            out_shape=out_shape,
            in_specs=[pl.BlockSpec(memory_space=pltpu.VMEM)] * len(operands),
            out_specs=jax.tree.map(lambda _: pl.BlockSpec(memory_space=pltpu.VMEM), out_shape),
            scratch_shapes=list(scratch),
            compiler_params=pltpu.CompilerParams(vmem_limit_bytes=vmem_bytes),
            cost_estimate=pl.CostEstimate(flops=flops, bytes_accessed=1 << 10, transcendentals=0),
            name=name,
        )(*operands)

    return run


def low_rows(width, samples):
    starts = {"w": 0, "sample": width, "w_out": width + samples}
    sizes = {"w": width, "sample": samples, "w_out": 16}
    return {name: slice(at, at + sizes[name]) for name, at in starts.items()}


def line_rows(slots, channels):
    return {
        "ids": 0,
        "occ": slots,
        "direction": slots + 1,
        "target": slots + 2,
        "b_out": slots + 2 + channels,
    }


def order_kernel(earlier_ref, later_ref):
    shape = earlier_ref.shape
    r_i = lax.broadcasted_iota(jnp.int32, shape, 0)
    c_i = lax.broadcasted_iota(jnp.int32, shape, 1)
    earlier_ref[...] = jnp.where(c_i < r_i, 1.0, 0.0).astype(bf16)
    later_ref[...] = jnp.where(c_i > r_i, 1.0, 0.0).astype(bf16)


def chosen_kernel(lines_ref, brick_ref, w_t_ref, chosen_ref, project_ref):
    total = chosen_ref.shape[1]
    rays = lines_ref.shape[1]
    bricks = brick_ref.shape[0]
    brick_t = brick_ref[...].astype(f32).T.astype(bf16)
    w_t = w_t_ref[...]
    row = lax.broadcasted_iota(jnp.int32, (bricks, rays), 0).astype(f32)
    for k in range(total // rays):
        one_hot = jnp.where(row == lines_ref[k : k + 1, :], 1.0, 0.0).astype(bf16)
        chosen = nn_dot(brick_t, one_hot).astype(bf16)
        chosen_ref[:, k * rays : (k + 1) * rays] = chosen
        project_ref[:, k * rays : (k + 1) * rays] = nn_dot(w_t, chosen)


def prepare_kernel(
    ray_ref,
    w_ref,
    sample_ref,
    w_out_ref,
    ids_ref,
    occ_ref,
    direction_ref,
    target_ref,
    b_ref,
    b_out_ref,
    own_ref,
    low_ref,
    lines_ref,
    w_t_ref,
    s_ref,
    wide_ref,
    left_ref,
    *,
    rows,
    lines,
):
    slots, rays = ids_ref.shape
    width = w_t_ref.shape[0]
    samples = s_ref.shape[0]
    outs = w_out_ref.shape[0]
    own_ref[...] = ray_ref[...]
    w = w_ref[...]
    w_out = w_out_ref[...].astype(f32)
    low_ref[rows["w"], :] = w
    low_ref[rows["sample"], :] = sample_ref[...]
    low_ref[rows["w_out"], :] = jnp.concatenate(
        [w_out, jnp.zeros((16 - outs, width), f32)], 0
    ).astype(bf16)
    lines_ref[:slots, :] = ids_ref[...].astype(f32)
    lines_ref[lines["occ"] : lines["occ"] + 1, :] = occ_ref[...].astype(f32)
    lines_ref[lines["direction"] : lines["direction"] + 1, :] = direction_ref[...].astype(f32)
    lines_ref[lines["target"] : lines["target"] + outs - 1, :] = target_ref[...]
    lines_ref[lines["b_out"] : lines["b_out"] + 1, :outs] = b_out_ref[...]
    w_t = w.astype(f32).T.astype(bf16)
    w_t_ref[...] = w_t
    s = nn_dot(sample_ref[...], w) + b_ref[...]
    s_ref[...] = s.astype(bf16).astype(f32)
    s_t = jnp.concatenate([s] * (128 // samples), 0).T
    for j in range(samples):
        wide_ref[j] = jnp.broadcast_to(s_t[:, j : j + 1], (width, 128)).astype(bf16)
    w_rows = jnp.concatenate(
        [jnp.broadcast_to(w_out[c : c + 1, :], (8, width)) for c in range(outs)], 0
    )
    row8 = lax.broadcasted_iota(jnp.int32, (outs * 8, width), 0) % 8
    for i in range(8):
        left_ref[:, i * width : (i + 1) * width] = jnp.where(row8 == i, w_rows, 0.0).astype(bf16)


def forward_kernel(*refs, owners, second, lines):
    ray_ref, project_ref, w_t_ref, wide_ref, left_ref, lines_ref, earlier_ref, *refs = refs
    if second:
        before_refs, refs = refs[:2], refs[2:]
    seg_ref, kept_ref, ut_ref, sorted_ref, order_ref, raw_ref = refs
    width, total = project_ref.shape
    samples = wide_ref.shape[0]
    outs = seg_ref.shape[0]
    half, rays = ray_ref.shape[0], lines_ref.shape[1]
    slots = total // rays
    chunk = 128
    own = 2 * half // owners
    last = gather_bits(owners, own)[-1]
    me = lax.axis_index("slab")
    side = (me >> last) & 1

    def whole(n, k=0, side=side):
        return pl.ds(pl.multiple_of(k * rays + (2 * n + side) * chunk, chunk), chunk)

    if second:
        for n in range(half // chunk):
            part = slice(n * chunk, (n + 1) * chunk)
            seg_ref[:, whole(n)] = before_refs[0][:, part]
            sorted_ref[whole(n), :] = before_refs[1][part, :]
        side = 1 - side

    def spot(n, k=0):
        at = k * half + n * chunk
        return whole(n, k, side) if second else slice(at, at + chunk)

    flip = (1 << last) if second else 0
    for i, t in enumerate(gather_order(owners, own)):
        owner = me ^ (t ^ flip)
        place = ((owner >> (last + 1)) << last) | (owner & ((1 << last) - 1))
        order_ref[pl.ds(pl.multiple_of(place * own, own), own), :] = ray_ref[
            i * own : (i + 1) * own, :
        ]
    ray_t = nt_dot(w_t_ref[...], order_ref[...])
    for n in range(half // chunk):
        sorted_ref[spot(n), :] = order_ref[n * chunk : (n + 1) * chunk, :]
        for k in range(slots):
            part = project_ref[:, whole(n, k, side)] + ray_t[:, n * chunk : (n + 1) * chunk]
            ut_ref[:, k * half + n * chunk : k * half + (n + 1) * chunk] = part.astype(bf16)
    b_out = [lines_ref[lines["b_out"], c] for c in range(outs)]

    def shade(n):
        ut = [ut_ref[:, k * half + n * chunk : k * half + (n + 1) * chunk] for k in range(slots)]
        ut = jnp.concatenate(ut, 1)
        for block in range(samples // 8):
            acc = None
            for i in range(4):
                parts = []
                for h in range(2):
                    column = wide_ref[block * 8 + 2 * i + h]
                    column = jnp.concatenate([column] * slots, 1)
                    parts.append(jnp.maximum(ut + column, 0))
                left = left_ref[:, 2 * i * width : 2 * (i + 1) * width]
                term = nn_dot(left, jnp.concatenate(parts, 0))
                acc = term if acc is None else acc + term
            for c in range(outs):
                raw_ref[c, n, block * 8 : block * 8 + 8, :] = acc[c * 8 : c * 8 + 8, :] + b_out[c]

    for n in range(half // chunk):
        shade(n)
    earlier = earlier_ref[...]
    occ_row = lines["occ"]
    for n in range(half // chunk):
        occ = lines_ref[occ_row : occ_row + 1, whole(n, 0, side)]
        raws = [
            raw_ref[0, n, :, k * chunk : (k + 1) * chunk] for k in range(slots)
        ]
        occupied = [(k < occ).astype(f32) for k in range(slots)]
        opticals = [
            step_length * (jnp.maximum(x, 0.0) + jnp.log1p(jnp.exp(-jnp.abs(x)))) * o
            for x, o in zip(raws, occupied)
        ]
        enters = sum_dot(earlier, jnp.concatenate(opticals, 1))
        before = jnp.zeros((1, chunk), f32)
        colors = [jnp.zeros((1, chunk), f32)] * (outs - 1)
        for k in range(slots):
            local = slice(k * half + n * chunk, k * half + (n + 1) * chunk)
            optical = opticals[k]
            entered = enters[:, k * chunk : (k + 1) * chunk] + before
            before = before + jnp.sum(optical, 0, keepdims=True)
            tanh = jnp.tanh(0.5 * optical)
            weight = jnp.exp(-entered) * (2.0 * tanh / (1.0 + tanh))
            for c in range(outs - 1):
                shading = jax.nn.sigmoid(raw_ref[c + 1, n, :, k * chunk : (k + 1) * chunk])
                light = weight * shading
                colors[c] = colors[c] + jnp.sum(light, 0, keepdims=True)
                kept_ref[c, :, local] = shading
                kept_ref[outs + c, :, local] = light
            kept_ref[outs - 1, :, local] = entered + optical
            kept_ref[2 * outs - 1, :, local] = raws[k]
        place = spot(n)
        for c in range(outs - 1):
            seg_ref[c : c + 1, place] = colors[c]
        seg_ref[outs - 1 : outs, place] = jnp.exp(-before)


def coefficient_kernel(
    seg_ref,
    first_ref,
    second_ref,
    first_ut_ref,
    second_ut_ref,
    later_ref,
    lines_ref,
    coef_ref,
    turned_ref,
    u_ref,
    *,
    owners,
    lines,
):
    outs, rays = seg_ref.shape
    samples, local = first_ref.shape[1:]
    half = rays // 2
    slots = local // half
    last = gather_bits(owners, rays // owners)[-1]
    side = (lax.axis_index("slab") >> last) & 1
    later = later_ref[...]
    chunk = 128

    def keep(index, lanes, value):
        coef_ref[index, :, lanes] = value
        value = value.astype(bf16)
        turned_ref[index, lanes, :] = jnp.concatenate([value] * (128 // samples), 0).T

    for kept_ref, ut_ref, where in (
        (first_ref, first_ut_ref, side),
        (second_ref, second_ut_ref, 1 - side),
    ):
        for n in range(half // chunk):
            base = (2 * n + where) * chunk
            through = seg_ref[outs - 1 : outs, pl.ds(pl.multiple_of(base, chunk), chunk)]
            occ = lines_ref[lines["occ"] : lines["occ"] + 1, pl.ds(pl.multiple_of(base, chunk), chunk)]
            after = [jnp.zeros((1, chunk), f32)] * (outs - 1)
            for k in reversed(range(slots)):
                lanes = pl.ds(pl.multiple_of(k * rays + base, chunk), chunk)
                at = slice(k * half + n * chunk, k * half + (n + 1) * chunk)
                u_ref[lanes, :] = ut_ref[:, at].T
                passed = jnp.exp(-kept_ref[outs - 1, :, at])
                occupied = (k < occ).astype(f32)
                density = step_length * occupied * jax.nn.sigmoid(kept_ref[2 * outs - 1, :, at])
                lights = [kept_ref[outs + c, :, at] for c in range(outs - 1)]
                behinds = sum_dot(later, jnp.concatenate(lights, 1))
                for c in range(outs - 1):
                    shading = kept_ref[c, :, at]
                    light = lights[c]
                    behind = behinds[:, c * chunk : (c + 1) * chunk] + after[c]
                    after[c] = after[c] + jnp.sum(light, 0, keepdims=True)
                    keep(c, lanes, density * (shading * passed - behind))
                    keep(outs + c, lanes, light * (1.0 - shading))
                keep(outs - 1, lanes, density * through)


def basis_kernel(turned_ref, u_ref, s_ref, low_ref, h1_ref, moved_ref, *, first, row_of):
    count, rays, width = h1_ref.shape
    samples = s_ref.shape[0]
    negative = (-s_ref[...]).astype(bf16)
    one = jnp.ones((samples, width), bf16)
    zero = jnp.zeros((samples, width), bf16)
    lane = lax.broadcasted_iota(jnp.int32, (8, 8 * samples), 1) // samples
    row = lax.broadcasted_iota(jnp.int32, (8, 8 * samples), 0)
    block_mask = lane == row
    repeat = 8 * samples // 128
    step = 128
    outs = moved_ref.shape[0]
    w = low_ref[row_of["w"], :]
    w_out = low_ref[row_of["w_out"], :].astype(f32)
    w_rows = [w_out[c : c + 1, :] for c in range(outs)]

    def slot_block(block, carry):
        for h in range(step // 16):
            base = pl.multiple_of(block * step + h * 16, 16)
            u16 = u_ref[pl.ds(first + base, 16), :]
            rows16 = [turned_ref[c, pl.ds(first + base, 16), :].astype(f32) for c in range(count)]
            for q in range(2):
                at = pl.multiple_of(block * step + h * 16 + q * 8, 8)
                left = [
                    jnp.where(
                        block_mask,
                        jnp.concatenate([rows16[c][q * 8 : q * 8 + 8]] * repeat, 1),
                        0.0,
                    )
                    for c in range(count)
                ]
                left = jnp.concatenate(left, 0).astype(bf16)
                tiles = [
                    jnp.where(
                        jnp.broadcast_to(u16[q * 8 + i : q * 8 + i + 1, :], (samples, width))
                        > negative,
                        one,
                        zero,
                    )
                    for i in range(8)
                ]
                h1 = nn_dot(left, jnp.concatenate(tiles, 0))
                for c in range(count):
                    h1_ref[c, pl.ds(at, 8), :] = h1[c * 8 : c * 8 + 8, :]
        return carry

    lax.fori_loop(0, rays // step, slot_block, 0)
    for c in range(outs):
        grad = w_rows[0] * h1_ref[c]
        if c + 1 < outs:
            grad = grad + w_rows[c + 1] * h1_ref[outs + c]
        moved_ref[c] = nt_dot(grad.astype(bf16), w)


def basis_cuts(total, bits):
    eighth = total // 8
    return [0, 2 * eighth, 5 * eighth, total] if bits > 2 else [0, total]


def basis_part(refs, row):
    for ref in refs:
        if row < ref.shape[1]:
            return ref, row
        row -= ref.shape[1]


def merge(first, second, forward):
    fc, ft = first
    sc, st = second
    return jnp.where(forward, fc + ft * sc, sc + st * fc), ft * st


def middle_kernel(*refs, owners, pieces, lines):
    bits = bits_of(owners)
    seg_ref, refs = refs[0], refs[1:]
    got_refs, refs = refs[:bits], refs[bits:]
    moved_refs, refs = refs[:pieces], refs[pieces:]
    lines_ref, keep_ref, send_ref, cot_ref, spread_ref, ray_ref = refs
    me = lax.axis_index("slab")
    outs = seg_ref.shape[0]
    channels = outs - 1
    rays = lines_ref.shape[1]
    width = moved_refs[0].shape[2]
    slots = sum(ref.shape[1] for ref in moved_refs) // rays
    forward = lines_ref[lines["direction"] : lines["direction"] + 1, :] == 0.0
    target = lines_ref[lines["target"] : lines["target"] + channels, :]

    def pair(values):
        return values[:channels, :], values[channels : channels + 1, :]

    low = high = None
    for b in reversed(range(bits)):
        piece = pair(got_refs[b][...])
        is_low = ((me >> b) & 1) == 1
        piece = (jnp.where(is_low, piece[0], 0.0), jnp.where(is_low, piece[1], 1.0))
        low = piece if low is None else merge(low, piece, forward)
    for b in range(bits):
        piece = pair(got_refs[b][...])
        is_high = ((me >> b) & 1) == 0
        piece = (jnp.where(is_high, piece[0], 0.0), jnp.where(is_high, piece[1], 1.0))
        high = piece if high is None else merge(high, piece, forward)
    seg_color, seg_trans = pair(seg_ref[...])
    before_color = jnp.where(forward, low[0], high[0])
    before_trans = jnp.where(forward, low[1], high[1])
    after_color = jnp.where(forward, high[0], low[0])
    color = before_color + before_trans * (seg_color + seg_trans * after_color)
    residual = color - target
    color_cot = before_trans * residual
    trans_cot = -before_trans * jnp.sum(after_color * residual, 0, keepdims=True)
    cot_ref[:channels, :] = color_cot
    cot_ref[channels:outs, :] = trans_cot
    cot_ref[outs : outs + channels, :] = color
    cot_ref[outs + channels :, :] = jnp.zeros((8 - outs - channels, rays), f32)
    chunk = 128
    values = jnp.concatenate([color_cot, trans_cot], 0)
    rounded = values.astype(bf16).astype(f32)
    values = jnp.concatenate([rounded, values - rounded], 0)
    row = lax.broadcasted_iota(jnp.int32, (2 * outs, outs * width), 0) % outs
    lane = lax.broadcasted_iota(jnp.int32, (2 * outs, outs * width), 1) // width
    spread = jnp.where(row == lane, 1.0, 0.0).astype(bf16)
    for n in range(rays // chunk):
        these = slice(n * chunk, (n + 1) * chunk)
        spread_ref[these, :] = nn_dot(values[:, these].T.astype(bf16), spread)
        grad = None
        for c in range(outs):
            whole = None
            for k in range(slots):
                ref, at = basis_part(moved_refs, k * rays + n * chunk)
                part = ref[c, at : at + chunk, :]
                whole = part if whole is None else whole + part
            term = spread_ref[these, c * width : (c + 1) * width] * whole
            grad = term if grad is None else grad + term
        ray_ref[these, :] = grad
    own = rays // owners
    for i, t in enumerate(halving_order(owners)):
        place = pl.multiple_of((me ^ t) * own, own)
        if i < owners // 2:
            keep_ref[i * own : (i + 1) * own, :] = ray_ref[pl.ds(place, own), :]
        else:
            at = i * own - rays // 2
            send_ref[at : at + own, :] = ray_ref[pl.ds(place, own), :].astype(bf16)


def brick_kernel(lines_ref, moved_ref, out_ref, *, first, shares):
    share = lax.axis_index("ray")
    rays = lines_ref.shape[1]
    total, width = moved_ref.shape
    owners = shares // 2
    part = out_ref.shape[0] // owners
    moved = moved_ref[...]
    row = lax.broadcasted_iota(jnp.int32, (part, rays), 0).astype(f32)
    for i in range(owners):
        begin = ((share ^ (first + i)) * part).astype(f32)
        acc = jnp.zeros((part, width), f32)
        for k in range(total // rays):
            one_hot = jnp.where(row + begin == lines_ref[k : k + 1, :], 1.0, 0.0).astype(bf16)
            acc = acc + nn_dot(one_hot, moved[k * rays : (k + 1) * rays])
        out_ref[i * part : (i + 1) * part, :] = acc.astype(out_ref.dtype)


def sample_kernel(
    cot_ref, coef_ref, u_ref, s_ref, low_ref, by_sample_ref, sums_ref, bias_ref, g_ref, *, first, rows
):
    outs = sums_ref.shape[0]
    channels = outs - 1
    rays = cot_ref.shape[1]
    total, width = u_ref.shape
    samples = by_sample_ref.shape[0]
    bias_sums = [jnp.zeros((1, 128), f32)] * outs
    for n in range(total // 128):
        lanes = slice(n * 128, n * 128 + 128)
        at = (n * 128) % rays
        cots = [cot_ref[c : c + 1, at : at + 128] for c in range(outs)]
        grads = [sum(cots[c] * coef_ref[c, first : first + samples, lanes] for c in range(outs))]
        for c in range(channels):
            grads.append(cots[c] * coef_ref[outs + c, first : first + samples, lanes])
        for c in range(outs):
            bias_sums[c] = bias_sums[c] + jnp.sum(grads[c], 0, keepdims=True)
        for j in range(0, samples, 8):
            g_ref[j // 8, :, lanes] = jnp.concatenate([g[j : j + 8] for g in grads], 0).astype(bf16)
    w_out = low_ref[rows["w_out"], :].astype(f32)
    w_rows = [w_out[c : c + 1, :] for c in range(outs)]
    row8 = lax.broadcasted_iota(jnp.int32, (8, width), 0)

    def sample_block(block, sums):
        left = g_ref[block]
        s8 = s_ref[pl.ds(pl.multiple_of(first + block * 8, 8), 8), :]
        acc = [jnp.zeros((8, width), f32)] * outs
        for i in range(0, 8, 2):
            edges = [(-s8[i + h : i + h + 1, :]).astype(bf16) for h in range(2)]
            h2 = None
            for n in range(total // 256):
                u = u_ref[n * 256 : n * 256 + 256, :]
                live = [
                    jnp.where(
                        u > jnp.broadcast_to(edge, u.shape),
                        jnp.ones(u.shape, bf16),
                        jnp.zeros(u.shape, bf16),
                    )
                    for edge in edges
                ]
                term = nn_dot(left[:, n * 256 : n * 256 + 256], jnp.concatenate(live, 1))
                h2 = term if h2 is None else h2 + term
            for c in range(outs):
                for h in range(2):
                    piece = h2[c * 8 : c * 8 + 8, h * width : (h + 1) * width]
                    acc[c] = acc[c] + jnp.where(row8 == i + h, piece, 0.0)
        by_sample_ref[pl.ds(pl.multiple_of(block * 8, 8), 8), :] = sum(
            w_rows[c] * acc[c] for c in range(outs)
        )
        return tuple(sums[c] + s8 * acc[c] for c in range(outs))

    sums = [jnp.zeros((8, width), f32)] * outs
    sums = lax.fori_loop(0, samples // 8, sample_block, tuple(sums), unroll=4)
    for c in range(outs):
        sums_ref[c] = sums[c]
        bias_ref[c : c + 1, :] = bias_sums[c]


def inputs_kernel(chosen_ref, sorted_ref, inputs_ref):
    total = chosen_ref.shape[1]
    ray_t = sorted_ref[...].astype(f32).T
    inputs = chosen_ref[...].astype(f32) + jnp.concatenate([ray_t] * (total // ray_t.shape[1]), 1)
    inputs_ref[...] = inputs.astype(bf16)


def slots_kernel(*refs, pieces, rows):
    h1_refs, refs = refs[:pieces], refs[pieces:]
    basis_refs, refs = refs[:pieces], refs[pieces:]
    spread_ref, u_ref, inputs_ref, low_ref, *refs = refs
    moved_ref, w_grad_ref, sums_ref, slot_ref = refs
    rays = spread_ref.shape[0]
    total, width = u_ref.shape
    outs = sums_ref.shape[0]
    w_out = low_ref[rows["w_out"], :].astype(f32)
    w_rows = [w_out[c : c + 1, :] for c in range(outs)]
    chunk = 32
    sums = [jnp.zeros((8, width), f32)] * outs
    for n in range(rays // chunk):
        these = slice(n * chunk, (n + 1) * chunk)
        cots = [spread_ref[these, c * width : (c + 1) * width] for c in range(outs)]
        for k in range(total // rays):
            whole = slice(k * rays + n * chunk, k * rays + (n + 1) * chunk)
            u = u_ref[whole, :].astype(f32)
            h1_ref, at = basis_part(h1_refs, whole.start)
            basis_ref, at = basis_part(basis_refs, whole.start)
            here = slice(at, at + chunk)
            products = [sum(cots[c] * h1_ref[c, here, :] for c in range(outs))]
            products += [cots[c] * h1_ref[outs + c, here, :] for c in range(outs - 1)]
            for c in range(outs):
                sums[c] = sums[c] + jnp.sum((u * products[c]).reshape(chunk // 8, 8, width), 0)
            slot_ref[whole, :] = sum(w_rows[c] * products[c] for c in range(outs)).astype(bf16)
            moved = sum(cots[c] * basis_ref[c, here, :] for c in range(outs))
            moved_ref[whole, :] = moved.astype(bf16)
    for c in range(outs):
        sums_ref[c] = sums[c]
    w_grad_ref[...] = nn_dot(inputs_ref[...], slot_ref[...])


def network_kernel(*refs, parts, rows):
    part_refs, refs = refs[: 3 * parts], refs[3 * parts :]
    w_grad_ref, sums_ref, low_ref, small_ref = refs
    by_sample = jnp.concatenate([part_refs[3 * i][...] for i in range(parts)], 0)
    samples, width = by_sample.shape
    outs = sums_ref.shape[0]
    w = low_ref[rows["w"], :]
    sample = low_ref[rows["sample"], :]
    sample_t = jnp.concatenate([sample] * (128 // samples), 0).T[:, :samples]
    rounded = by_sample.astype(bf16)
    small_ref[:samples, :] = nt_dot(rounded, w)
    small_ref[samples : samples + width, :] = w_grad_ref[...] + nn_dot(sample_t, rounded)
    at = samples + width
    small_ref[at : at + 1, :] = jnp.sum(by_sample, 0, keepdims=True)
    lane128 = lax.broadcasted_iota(jnp.int32, (1, 128), 1)
    bias = jnp.zeros((1, 128), f32)
    for c in range(outs):
        total = sums_ref[c] + sum(part_refs[3 * i + 1][c] for i in range(parts))
        small_ref[at + 1 + c : at + 2 + c, :] = jnp.sum(total, 0, keepdims=True)
        row = sum(part_refs[3 * i + 2][c : c + 1, :] for i in range(parts))
        bias = bias + jnp.where(lane128 == c, jnp.sum(row, 1, keepdims=True), 0.0)
    small_ref[at + 1 + outs : at + 2 + outs, :] = bias
    rest = small_ref.shape[0] - (at + 2 + outs)
    small_ref[at + 2 + outs :, :] = jnp.zeros((rest, width), f32)


def ray_sum_kernel(keep_ref, got_ref, cot_ref, out_ref, color_ref):
    out_ref[...] = keep_ref[...] + got_ref[...].astype(f32)
    channels, own = color_ref.shape
    rays = cot_ref.shape[1]
    me = lax.axis_index("slab")
    r_i = lax.broadcasted_iota(jnp.int32, (rays, own), 0)
    c_i = lax.broadcasted_iota(jnp.int32, (rays, own), 1)
    pick = jnp.where(r_i == c_i + me * own, 1.0, 0.0).astype(bf16)
    color = cot_ref[channels + 1 : 2 * channels + 1, :]
    high = color.astype(bf16)
    middle = (color - high.astype(f32)).astype(bf16)
    low = (color - high.astype(f32) - middle.astype(f32)).astype(bf16)
    picked = nn_dot(jnp.concatenate([high, middle, low], 0), pick)
    color_ref[...] = picked[:channels] + picked[channels : 2 * channels] + picked[2 * channels :]


def finish_kernel(
    ray_ref,
    color_ref,
    brick_ref,
    sent_ref,
    got_ref,
    color_out_ref,
    ray_out_ref,
    brick_out_ref,
    sample_ref,
    w_ref,
    b_ref,
    w_out_ref,
    b_out_ref,
):
    ray_out_ref[...] = ray_ref[...]
    color_out_ref[...] = color_ref[...]
    part = brick_ref.shape[0]
    brick_out_ref[...] = brick_ref[...] + got_ref[:part, :].astype(f32)
    small = sent_ref[part:, :].astype(f32) + got_ref[part:, :].astype(f32)
    samples, width = sample_ref.shape
    outs = w_out_ref.shape[0]
    at = samples + width
    sample_ref[...] = small[:samples]
    w_ref[...] = small[samples:at]
    b_ref[...] = small[at : at + 1]
    w_out_ref[...] = small[at + 1 : at + 1 + outs]
    b_out_ref[...] = small[at + 1 + outs : at + 2 + outs, :outs]


def body(
    ray_code,
    direction,
    target,
    brick_code,
    sample_code,
    w_hidden,
    b_hidden,
    w_out,
    b_out,
    brick_ids,
    occupancy,
):
    owners = lax.axis_size("slab")
    shares = lax.axis_size("ray")
    me = lax.axis_index("slab")
    ids = brick_ids[0]
    slots, rays = ids.shape
    total = slots * rays
    bricks, width = brick_code.shape[1:]
    samples = sample_code.shape[1]
    outs = w_out.shape[1]
    channels = outs - 1
    count = outs + channels

    def shaped(*shape):
        return jax.ShapeDtypeStruct(shape, f32)

    def shaped16(*shape):
        return jax.ShapeDtypeStruct(shape, bf16)

    rows = low_rows(width, samples)
    lines = line_rows(slots, channels)
    earlier, later = call(
        order_kernel,
        (shaped16(samples, samples), shaped16(samples, samples)),
        "order",
        flops=1 << 34,
    )()
    gathered, low, packed, w_t, s, wide, left = call(
        functools.partial(prepare_kernel, rows=rows, lines=lines),
        (
            shaped16(*ray_code.shape),
            shaped16(rows["w_out"].stop, width),
            shaped(lines["b_out"] + 1, rays),
            shaped16(width, width),
            shaped(samples, width),
            shaped16(samples, width, 128),
            shaped16(outs * 8, 8 * width),
        ),
        "prepare",
        flops=1 << 31,
    )(
        ray_code,
        w_hidden[0],
        sample_code[0],
        w_out[0],
        ids,
        occupancy,
        direction[None],
        target,
        b_hidden,
        b_out,
    )
    turns = gather_bits(owners, ray_code.shape[0])
    other = swap(ray_code, "slab", owners, 1 << turns[0])
    other, lines_later = lax.optimization_barrier((other, packed))
    for b in turns[1:]:
        gathered = jnp.concatenate([gathered, other], 0)
        other = swap(gathered, "slab", owners, 1 << b)
    chosen, project = call(
        chosen_kernel,
        (shaped16(width, total), shaped(width, total)),
        "chosen",
        flops=1 << 29,
    )(lines_later, brick_code[0], w_t)
    passes = ()
    kept = []
    uts = []
    for second, part in enumerate((gathered, other)):
        wide_rays = rays if second else rays // 2
        seg, kept_half, ut_half, ray_sorted = call(
            functools.partial(forward_kernel, owners=owners, second=second, lines=lines),
            (
                shaped(outs, wide_rays),
                shaped(2 * outs, samples, total // 2),
                shaped16(width, total // 2),
                shaped16(wide_rays, width),
            ),
            "forward",
            scratch=(
                pltpu.VMEM((rays // 2, width), bf16),
                pltpu.VMEM((outs, rays // 256, samples, slots * 128), f32),
            ),
            flops=1 << 30,
        )(part, project, w_t, wide, left, packed, earlier, *passes)
        passes = (seg, ray_sorted)
        kept.append(kept_half)
        uts.append(ut_half)

    coef, turned, u = call(
        functools.partial(coefficient_kernel, owners=owners, lines=lines),
        (
            shaped(count, samples, total),
            shaped16(count, total, 128),
            shaped16(total, width),
        ),
        "coefficients",
        flops=1 << 30,
    )(seg, *kept, *uts, later, packed)

    forward = packed[lines["direction"]][None] == 0.0
    group = (seg[:channels], seg[channels:])
    received = []
    basis = []
    bits = bits_of(owners)
    cuts = basis_cuts(total, bits)
    pieces = len(cuts) - 1
    turned_later, chosen_later = turned, chosen
    for b in range(bits):
        sent = jnp.concatenate(group, 0) if b > 0 else seg
        other = swap(sent, "slab", owners, 1 << b)
        if b < pieces:
            piece = cuts[b + 1] - cuts[b]
            basis.append(
                call(
                    functools.partial(basis_kernel, first=cuts[b], row_of=rows),
                    (shaped(count, piece, width), shaped(outs, piece, width)),
                    "basis",
                    flops=1 << 29,
                )(turned_later, u, s, low)
            )
        if b + 1 == bits:
            inputs = call(inputs_kernel, shaped16(width, total), "inputs", flops=1 << 20)(
                chosen_later, ray_sorted
            )
            other, inputs = lax.optimization_barrier((other, inputs))
        other, turned_later, chosen_later = lax.optimization_barrier(
            (other, turned_later, chosen_later)
        )
        received.append(other)
        theirs = (other[:channels], other[channels:])
        upper = ((me >> b) & 1) == 1
        first = jax.tree.map(lambda a, b: jnp.where(upper, b, a), group, theirs)
        second = jax.tree.map(lambda a, b: jnp.where(upper, a, b), group, theirs)
        group = merge(first, second, forward)

    h1, moved_basis = zip(*basis)
    ray_keep, ray_send, cots, spread = call(
        functools.partial(middle_kernel, owners=owners, pieces=pieces, lines=lines),
        (
            shaped(rays // 2, width),
            shaped16(rays // 2, width),
            shaped(8, rays),
            shaped(rays, outs * width),
        ),
        "middle",
        scratch=(pltpu.VMEM((rays, width), f32),),
        flops=1 << 29,
    )(seg, *received, *moved_basis, packed)
    moved, w_grad, sums = call(
        functools.partial(slots_kernel, pieces=pieces, rows=rows),
        (
            shaped16(total, width),
            shaped(width, width),
            shaped(outs, 8, width),
        ),
        "slots",
        scratch=(pltpu.VMEM((total, width), bf16),),
        flops=1 << 20,
    )(*h1, *moved_basis, spread, u, inputs, low)

    def merged(keep, got):
        half = keep.shape[0] // 2
        return keep[:half] + got[:half].astype(f32), (keep[half:] + got[half:].astype(f32)).astype(bf16)

    def part_by_sample(i, cots):
        return call(
            functools.partial(sample_kernel, first=i * samples // parts, rows=rows),
            (
                shaped(samples // parts, width),
                shaped(outs, 8, width),
                shaped(outs, 128),
            ),
            "by_sample",
            scratch=(pltpu.VMEM((samples // parts // 8, outs * 8, total), bf16),),
            flops=1 << 20,
        )(cots, coef, u, s, low)

    def by_brick(first, moved, shape):
        return call(
            functools.partial(brick_kernel, first=first, shares=shares),
            shape,
            "bricks",
            flops=1 << 20,
        )(packed, moved)

    parts = 2
    by_part = []
    later_cots = cots
    for b in range(bits):
        if b + 1 == bits:
            small_rows = -(-(samples + width + 2 + outs) // 16) * 16
            small = call(
                functools.partial(network_kernel, parts=parts, rows=rows),
                shaped(small_rows, width),
                "network",
                flops=1 << 20,
            )(*by_part, w_grad, sums, low)
            ray_send, small = lax.optimization_barrier((ray_send, small))
        ray_got = swap(ray_send, "slab", owners, 1 << halving_bits(owners)[b])
        if b < parts:
            by_part += part_by_sample(b, later_cots)
        if b == 1:
            brick_sent = by_brick(shares // 2, moved, shaped16(bricks // 2, width))
            w_grad, brick_sent = lax.optimization_barrier((w_grad, brick_sent))
        if b + 1 < bits:
            held = (ray_got, later_cots, moved, by_part)
            ray_got, later_cots, moved, by_part = lax.optimization_barrier(held)
            ray_keep, ray_send = merged(ray_keep, ray_got)

    small = small.astype(bf16)
    for b in reversed(range(bits_of(shares))):
        sent = jnp.concatenate([brick_sent, small], 0)
        if 1 << (b + 1) == shares:
            sent, moved = lax.optimization_barrier((sent, moved))
            brick = by_brick(0, moved, shaped(bricks // 2, width))
        other = swap(sent, "ray", shares, 1 << b)
        if b > 0:
            half = brick.shape[0]
            small = (sent[half:].astype(f32) + other[half:].astype(f32)).astype(bf16)
            brick_sent = (brick[half // 2 :] + other[half // 2 : half].astype(f32)).astype(bf16)
            brick = brick[: half // 2] + other[: half // 2].astype(f32)
    ray_sum, color_own = call(
        ray_sum_kernel,
        (shaped(rays // owners, width), shaped(channels, rays // owners)),
        "ray_sum",
        flops=1 << 31,
    )(ray_keep, ray_got, cots)
    color_out, ray_out, brick_out, sample_out, w_grad, b_grad, w_out_grad, b_out_grad = call(
        finish_kernel,
        (
            shaped(channels, rays // owners),
            shaped(rays // owners, width),
            shaped(bricks // shares, width),
            shaped(samples, width),
            shaped(width, width),
            shaped(1, width),
            shaped(outs, width),
            shaped(1, outs),
        ),
        "finish",
    )(ray_sum, color_own, brick, sent, other)
    return (
        color_out,
        ray_out,
        brick_out[None],
        sample_out[None],
        w_grad[None],
        b_grad,
        w_out_grad[None],
        b_out_grad,
    )


def solution(mesh):
    in_specs = (
        P(("ray", "slab"), None),
        P("ray"),
        P(None, "ray"),
        P("slab", None, None),
        P("slab", None, None),
        P("slab", None, None),
        P("slab", None),
        P("slab", None, None),
        P("slab", None),
        P("slab", None, "ray"),
        P("slab", "ray"),
    )
    out_specs = (
        P(None, ("ray", "slab")),
        P(("ray", "slab"), None),
        P("slab", "ray", None),
        P("slab", None, None),
        P("slab", None, None),
        P("slab", None),
        P("slab", None, None),
        P("slab", None),
    )
    return jax.shard_map(body, mesh=mesh, in_specs=in_specs, out_specs=out_specs, check_vma=False)
```
